32 devices in a mesh: slab: 8 (over y, x, core), brick: 4 (over z).
Axes of the slice: x: 2, y: 2, z: 4, core: 2. Of those that a mesh axis runs over, the one named last changes fastest.
Arguments:
- velocity: float32 [3, 16, 32, 257], P(None, 'slab', 'brick'), may hold values from -6 to 6
- energy: float32 [8, 8, 16, 128], P(None, 'slab', 'brick'), may hold values from 0.5 to 2
- density: float32 [8, 8, 16, 128], P(None, 'slab', 'brick'), may hold values from 0.5 to 18, as said below
- material: int32 [8, 16, 128], P('slab', 'brick'), may hold values from 0 to 1
- geometry: bfloat16 [81, 8, 8, 16, 128], P(None, None, 'slab', 'brick'), may hold values from -2 to 2
- mass_weight: float32 [27, 8, 16, 128], P(None, 'slab', 'brick'), may hold values from 2 to 8
- energy_mass: float32 [8, 8, 16, 128], P(None, 'slab', 'brick'), may hold values from 0.5 to 2
Outputs:
- velocity_half: float32 [3, 16, 32, 257], P(None, 'slab', 'brick')
- energy_half: float32 [8, 8, 16, 128], P(None, 'slab', 'brick')
The draws below stay inside these ranges and needn't reach their ends.
Inputs may be any that keep to these rules, and one draw needn't show every extreme that they name: `density`: densities at the thermodynamic degrees of freedom, positive.
All inputs are finite; a program needn't handle non-finite values.
Results may differ from the reference program's by a relative error of at most 0.005.
Values may be sent and summed in bfloat16 or wider, within the bound.
No kernel may reach another device: no remote copies, remote signals or barrier semaphores. Data moves between devices by JAX's collectives and lax.ppermute only.
A program may use at most 64 MiB of HBM per device.

```python
import math
import jax
import jax.numpy as jnp
import numpy as np
from jax import lax

VDOF = 81
TDOF = 8
QUAD = 27
BZ = 128
ITERS = 3
NZX = 8
NZY = 16
NX = 16
NY = 32
NZN = 257


def draw_density(key, part):
    shape = (TDOF, NZX, NZY, BZ)
    position = jnp.arange(NZX, dtype=jnp.float32)[None, :, None, None] / NZX
    spread = jnp.exp(jax.random.uniform(key, shape, jnp.float32, math.log(0.5), math.log(2.0)))
    return spread * jnp.power(3.0, position)


def place_ends(values, stream_key, smallest, high):
    place = [jax.random.randint(jax.random.fold_in(stream_key, axis), (), 0, length) for axis, length in enumerate(values.shape)]
    longest = values.shape.index(max(values.shape))
    neighbour = place[:longest] + [(place[longest] + 1) % values.shape[longest]] + place[longest + 1:]
    return values.at[tuple(place)].set(smallest).at[tuple(neighbour)].set(high)


def block_levels(rng, shape, cuts, smallest, top_value):
    level = 1.0
    for dim, shards_of in cuts:
        draws = jax.random.uniform(jax.random.fold_in(jax.random.fold_in(rng, 6), dim), (shards_of,), jnp.float32, smallest / len(cuts), top_value / len(cuts))
        level = level * jnp.repeat(jnp.exp(draws), shape[dim] // shards_of).reshape((-1,) + (1,) * (len(shape) - 1 - dim))
    return level


def normal_values(rng, dims, width, limit, split=(), held_as=jnp.bfloat16):
    values = jax.random.normal(rng, dims, jnp.float32) * width
    if len(split) > 0:
        values = block_levels(rng, dims, split, -0.22, 0.18) * values
    return jnp.clip(values, min=-limit, max=limit).astype(held_as)


def setup_inputs(seed: int = 0) -> dict:
    key_list = jax.random.split(jax.random.key(seed), 8)
    return {
        "velocity": normal_values(key_list[0], (3, NX, NY, NZN), 1.0, 6.0, ((1, 8), (2, 4)), jnp.float32),
        "energy": jnp.clip(jnp.exp(math.log(2.0) - 1.3862944 * jax.random.uniform(key_list[1], (TDOF, NZX, NZY, BZ), jnp.float32) ** block_levels(key_list[1], (TDOF, NZX, NZY, BZ), ((1, 8), (2, 4)), -0.2, 0.2)), 0.5, 2.0),
        "density": draw_density(jax.random.fold_in(key_list[7], 71), 0),
        "material": place_ends(jax.random.randint(key_list[3], (NZX, NZY, BZ), 0, 2), jax.random.fold_in(key_list[3], 1), 0, 1).astype(jnp.int32),
        "geometry": normal_values(key_list[4], (VDOF, TDOF, NZX, NZY, BZ), TDOF ** -0.5, 2.0, ((2, 8), (3, 4))),
        "mass_weight": jnp.clip(jnp.exp(math.log(8.0) - 1.3862944 * jax.random.uniform(key_list[5], (QUAD, NZX, NZY, BZ), jnp.float32) ** block_levels(key_list[5], (QUAD, NZX, NZY, BZ), ((1, 8), (2, 4)), -0.2, 0.2)), 2.0, 8.0),
        "energy_mass": jnp.clip(jnp.exp(math.log(2.0) - 1.3862944 * jax.random.uniform(key_list[6], (TDOF, NZX, NZY, BZ), jnp.float32) ** block_levels(key_list[6], (TDOF, NZX, NZY, BZ), ((1, 8), (2, 4)), -0.2, 0.2)), 0.5, 2.0),
    }


HALF_STEP = 0.25
GRAVITY = 1.0
PRECISE = lax.Precision.HIGHEST

def basis_tables():
    offset = np.sqrt(0.6) / 2.0
    points = np.array([0.5 - offset, 0.5, 0.5 + offset])
    weights_line = np.array([5.0, 8.0, 5.0]) / 18.0
    node_spots = np.array([0.0, 0.5, 1.0])
    lagrange = np.ones((3, 3))
    for a in range(3):
        for second in range(3):
            if second != a:
                lagrange[a] = lagrange[a] * (points - node_spots[second]) / (node_spots[a] - node_spots[second])
    basis_full = (lagrange[:, None, None, :, None, None] * lagrange[None, :, None, None, :, None] * lagrange[None, None, :, None, None, :]).reshape(27, 27)
    weights = (weights_line[:, None, None] * weights_line[None, :, None] * weights_line[None, None, :]).reshape(27)
    return (jnp.asarray(basis_full, jnp.float32), jnp.asarray(weights, jnp.float32))

def to_zones(field, count_x, count_y, count_z):
    pieces = []
    for a in range(3):
        for b in range(3):
            for c in range(3):
                pieces.append(lax.slice(field, (0, a, b, c), (3, a + 2 * count_x - 1, b + 2 * count_y - 1, c + 2 * count_z - 1), (1, 2, 2, 2)))
    return jnp.stack(pieces, axis=1)

def from_zones(values, count_x, count_y, count_z):
    summed = None
    n = 0
    for a in range(3):
        for b in range(3):
            for c in range(3):
                padded = lax.pad(values[:, n], jnp.array(0, values.dtype), ((0, 0, 0), (a, 2 - a, 1), (b, 2 - b, 1), (c, 2 - c, 1)))
                summed = padded if summed is None else summed + padded
                n = n + 1
    return summed

def apply_mass(zone_values, weight_eff, basis_table):
    at_points = jnp.einsum('nq,knxyz->kqxyz', basis_table, zone_values, precision=PRECISE)
    return jnp.einsum('nq,kqxyz->knxyz', basis_table, at_points * weight_eff[None], precision=PRECISE)

def wall_mask(field):
    component = lax.broadcasted_iota(jnp.int32, field.shape, 0)
    height = lax.broadcasted_iota(jnp.int32, field.shape, 3)
    at_wall = (component == 2) & ((height == 0) | (height == field.shape[3] - 1))
    return jnp.where(at_wall, jnp.zeros((), field.dtype), field)

def extend(field):
    field = jnp.concatenate([field, field[:, :1]], axis=1)
    return jnp.concatenate([field, field[:, :, :1]], axis=2)

def fold_wrap(field):
    field = field.at[:, 0].add(field[:, -1])[:, :-1]
    return field.at[:, :, 0].add(field[:, :, -1])[:, :, :-1]

def reference(velocity, energy, density, material, geometry, mass_weight, energy_mass):
    basis_table, quad_weights = basis_tables()
    weight_eff = mass_weight * quad_weights[:, None, None, None]
    zone_vel = to_zones(extend(velocity), NZX, NZY, BZ).astype(jnp.bfloat16)
    zone_rows = zone_vel.reshape(3 * 27, NZX, NZY, BZ)
    gamma_less = jnp.where(material == 0, 2.0 / 3.0, 0.4).astype(jnp.float32)
    pressure = (gamma_less[None] * density * energy).astype(jnp.bfloat16)

    def one_block(position):
        geometry_block = lax.dynamic_slice_in_dim(geometry, position, 1, 2).astype(jnp.float32)
        press_block = lax.dynamic_slice_in_dim(pressure, position, 1, 1).astype(jnp.float32)
        row_block = lax.dynamic_slice_in_dim(zone_rows, position, 1, 1).astype(jnp.float32)
        force = jnp.einsum('rcxyz,cxyz->rxyz', geometry_block, press_block)
        work_done = jnp.einsum('rcxyz,rxyz->cxyz', geometry_block, row_block)
        return (force[:, 0], work_done[:, 0])
    force, work_done = lax.map(one_block, jnp.arange(NZX, dtype=jnp.int32))
    force = jnp.moveaxis(force, 0, 1)
    work_done = jnp.moveaxis(work_done, 0, 1)
    energy_half = energy + HALF_STEP * pressure.astype(jnp.float32) * work_done / energy_mass
    zone_force = -force.reshape(3, 27, NZX, NZY, BZ)
    gravity_term = -GRAVITY * jnp.einsum('nq,qxyz->nxyz', basis_table, weight_eff, precision=PRECISE)
    zone_force = zone_force.at[2].add(gravity_term)
    right_side = wall_mask(fold_wrap(from_zones(zone_force, NZX, NZY, BZ)))

    def operate(field):
        zones = to_zones(extend(field), NZX, NZY, BZ)
        return wall_mask(fold_wrap(from_zones(apply_mass(zones, weight_eff, basis_table), NZX, NZY, BZ)))
    acceleration = jnp.zeros_like(right_side)
    residual = right_side
    direction = right_side
    norm_now = jnp.sum(residual * residual)
    for iteration in range(ITERS):
        image_new = operate(direction)
        step_size = norm_now / jnp.sum(direction * image_new)
        acceleration = acceleration + step_size * direction
        residual = residual - step_size * image_new
        norm_next = jnp.sum(residual * residual)
        direction = residual + norm_next / norm_now * direction
        norm_now = norm_next
    velocity_half = velocity + HALF_STEP * acceleration
    return (velocity_half, energy_half)
```

```python
import jax
import jax.numpy as jnp
import numpy as np
from jax import lax
from jax.experimental import pallas as pl
from jax.experimental.pallas import tpu as pltpu
from jax.sharding import PartitionSpec as P

HALF_STEP = 0.25
GRAVITY = 1.0
F32 = jnp.float32
BF16 = jnp.bfloat16

OFFSET = float(np.sqrt(0.6) / 2.0)
SIDE = 0.3
MIDDLE = 0.4
LINE_WEIGHTS = (5.0 / 18.0, 8.0 / 18.0, 5.0 / 18.0)
POINT_WEIGHT = [a * b * c for a in LINE_WEIGHTS for b in LINE_WEIGHTS for c in LINE_WEIGHTS]
OWN = 4
HALO = 2


def lines(direction):
    stride = (9, 3, 1)[direction]
    return [(n, n + stride, n + 2 * stride) for n in range(27) if (n // stride) % 3 == 0]


def to_points(values):
    values = list(values)
    for direction in range(3):
        for i, j, k in lines(direction):
            even = SIDE * (values[i] + values[k]) + MIDDLE * values[j]
            odd = OFFSET * (values[i] - values[k])
            values[i], values[k] = even + odd, even - odd
    return values


def from_points(values):
    values = list(values)
    for direction in range(3):
        for i, j, k in lines(direction):
            total = values[i] + values[k]
            odd = OFFSET * (values[i] - values[k])
            even = SIDE * total
            values[i], values[k] = even + odd, even - odd
            values[j] = values[j] + MIDDLE * total
    return values


def lane_of(shape):
    return lax.broadcasted_iota(jnp.int32, shape, len(shape) - 1)


def assemble_z(values, wall):
    values = list(values)
    lane = lane_of(values[0].shape)
    first, last = lane == 0, lane == 127
    for i, _, k in lines(2):
        total = values[i] + jnp.where(first, 0.0, pltpu.roll(values[k], 1, 1))
        top = values[k]
        if wall:
            total = jnp.where(first, 0.0, total)
            top = jnp.zeros_like(top)
        values[i] = total
        values[k] = jnp.where(last, top, pltpu.roll(total, 127, 1))
    return values


def assemble_y(values):
    values = list(values)
    for i, _, k in lines(1):
        values[i] = values[i] + pltpu.roll(values[k], 1, 0)
        values[k] = pltpu.roll(values[i], 7, 0)
    return values


def force_kernel(geometry, density, energy, material, mass_weight, field, to_left, to_right):
    gamma = jnp.where(material[...] == 0, 2.0 / 3.0, 0.4).astype(F32)
    pressure = (gamma[None] * density[...] * energy[...]).astype(BF16).astype(F32)
    gravity = from_points([mass_weight[q] * POINT_WEIGHT[q] for q in range(27)])
    for comp in range(3):
        for n in range(27):
            r = 27 * comp + n
            block = geometry[pl.ds(8 * r, 8)].astype(F32)
            value = -jnp.sum(block * pressure, axis=0)
            if comp == 2:
                value = value - GRAVITY * gravity[n]
            field[r] = value
            if n // 9 == 0:
                to_left[9 * comp + n] = value
            if n // 9 == 2:
                to_right[9 * comp + n - 18] = value


def spread_kernel(velocity, out):
    rows = velocity[...].astype(BF16).reshape(48, velocity.shape[3])
    low = rows[:, :256]
    high = rows[:, 256:257].astype(F32)
    node = lax.broadcasted_iota(jnp.int32, (256, 384), 0)
    lane = lax.broadcasted_iota(jnp.int32, (256, 384), 1)
    pick = (node == 2 * (lane % 128) + lane // 128).astype(F32).astype(BF16)
    spread = jnp.dot(low, pick, preferred_element_type=F32)
    top = jnp.where(lane_of((48, 128)) == 127, high, 0.0)
    spread = jnp.concatenate([spread[:, :256], spread[:, 256:] + top], axis=1)
    row = lax.broadcasted_iota(jnp.int32, (96, 48), 0)
    source = lax.broadcasted_iota(jnp.int32, (96, 48), 1)
    wanted = (row // 16) * 8 + 2 * (row % 8) + (row // 8) % 2
    move = ((source == wanted) & (row % 8 < OWN)).astype(F32).astype(BF16)
    moved = jnp.dot(move, spread.astype(BF16), preferred_element_type=F32)
    for group in range(12):
        for c in range(3):
            out[3 * group + c] = moved[8 * group : 8 * group + 8, 128 * c : 128 * c + 128]


def rim_kernel(field, from_left, from_right, mass_weight, spread, out, to_low, to_high):
    for comp in range(3):
        for n in range(27):
            r = 27 * comp + n
            value = field[r]
            if n // 9 == 0:
                value = value + from_left[9 * comp + n]
            if n // 9 == 2:
                value = value + from_right[9 * comp + n - 18]
            out[r] = value
            to_low[r] = value[:HALO]
            to_high[r] = value[OWN - HALO :]
    for q in range(27):
        to_low[81 + q] = mass_weight[q, :HALO]
        to_high[81 + q] = mass_weight[q, OWN - HALO :]
    for comp in range(3):
        for a in range(2):
            for c in range(3):
                to_low[108 + 6 * comp + 3 * a + c] = spread[12 * comp + 6 * a + c, :HALO]


def send_planes(values, comp, to_left, to_right):
    slot = 0
    for b in range(2):
        for c in range(3):
            to_left[6 * comp + slot] = values[3 * b + c]
            to_right[6 * comp + slot] = values[18 + 3 * b + c]
            slot += 1


def apply_mass(values, weight, wall):
    points = to_points(values)
    points = [points[q] * weight[q] for q in range(27)]
    return assemble_y(assemble_z(from_points(points), wall))


def first_kernel(
    own, from_low, from_high, mass_weight, spread, field, weight, image, to_left, to_right, speeds, rows
):
    for q in range(27):
        rows[q, :HALO] = from_low[81 + q]
        rows[q, HALO : HALO + OWN] = mass_weight[q]
        rows[q, HALO + OWN :] = from_high[81 + q]
    for q in range(27):
        weight[q] = rows[q] * POINT_WEIGHT[q]
    for r in range(81):
        rows[r, :HALO] = from_low[r]
        rows[r, HALO : HALO + OWN] = own[r]
        rows[r, HALO + OWN :] = from_high[r]
    for comp in range(3):
        values = [rows[27 * comp + n] for n in range(27)]
        values = assemble_y(assemble_z(values, comp == 2))
        for n in range(27):
            field[27 * comp + n] = values[n]
        values = apply_mass(values, weight, comp == 2)
        for n in range(27):
            image[27 * comp + n] = values[n]
        send_planes(values, comp, to_left, to_right)
    row = lax.broadcasted_iota(jnp.int32, (8, 128), 0)
    for comp in range(3):
        for a in range(2):
            for c in range(3):
                for b in range(2):
                    value = spread[12 * comp + 6 * a + 3 * b + c]
                    speeds[18 * comp + 9 * a + 3 * b + c] = value
                    if a == 0:
                        to_left[18 + 9 * comp + 3 * b + c] = value
                beyond = from_high[108 + 6 * comp + 3 * a + c, 0:1]
                value = spread[12 * comp + 6 * a + c]
                value = jnp.where(row == OWN - 1, beyond, pltpu.roll(value, 7, 0))
                speeds[18 * comp + 9 * a + 6 + c] = value
                if a == 0:
                    to_left[18 + 9 * comp + 6 + c] = value


def take_planes(image, from_left, from_right, comp):
    values = [image[27 * comp + n] for n in range(27)]
    slot = 0
    for b in range(2):
        for c in range(3):
            values[3 * b + c] = values[3 * b + c] + from_left[6 * comp + slot]
            values[18 + 3 * b + c] = values[18 + 3 * b + c] + from_right[6 * comp + slot]
            slot += 1
    for a in (0, 18):
        for c in range(3):
            values[a + 6 + c] = pltpu.roll(values[a + c], 7, 0)
    return values


def second_kernel(image, from_left, from_right, weight, field, image_out, to_left, to_right):
    for comp in range(3):
        values = take_planes(image, from_left, from_right, comp)
        for n in range(27):
            field[27 * comp + n] = values[n]
        values = apply_mass(values, weight, comp == 2)
        for n in range(27):
            image_out[27 * comp + n] = values[n]
        send_planes(values, comp, to_left, to_right)


def work_kernel(geometry, density, energy, material, energy_mass, speeds, from_right, out):
    gamma = jnp.where(material[...] == 0, 2.0 / 3.0, 0.4).astype(F32)
    pressure = (gamma[None] * density[...] * energy[...]).astype(BF16).astype(F32)
    work = jnp.zeros_like(pressure)
    for comp in range(3):
        for n in range(27):
            if n < 18:
                speed = speeds[18 * comp + n, :OWN]
            else:
                speed = from_right[18 + 9 * comp + n - 18, :OWN]
            work = work + geometry[pl.ds(8 * (27 * comp + n), 8)].astype(F32) * speed[None]
    out[...] = energy[...] + HALF_STEP * pressure * work / energy_mass[...]


def dot_owned(first, second, comp, total):
    last = lane_of((8, 128)) == 127
    for a in range(2):
        for b in range(2):
            n = 27 * comp + 9 * a + 3 * b
            total = total + first[n] * second[n] + first[n + 1] * second[n + 1]
            total = total + jnp.where(last, first[n + 2] * second[n + 2], 0.0)
    return total


def moment_kernel(image, from_left, from_right, weight, zeroth, first, second, moments):
    zero = jnp.zeros((8, 128), F32)
    energy_norm = zero
    for comp in range(3):
        values = take_planes(image, from_left, from_right, comp)
        for n in range(27):
            second[27 * comp + n] = values[n]
        points = to_points(values)
        for q in range(27):
            energy_norm = energy_norm + points[q] * points[q] * weight[q]
    pairs = [(zeroth, zeroth), (zeroth, first), (first, first), (first, second), (second, second)]
    totals = []
    for one, other in pairs:
        total = zero
        for comp in range(3):
            total = dot_owned(one, other, comp, total)
        totals.append(total)
    totals.append(energy_norm)
    row = lax.broadcasted_iota(jnp.int32, (8, 128), 0)
    lane = lane_of((1, 128))
    mine = (row >= HALO) & (row < HALO + OWN)
    line = jnp.zeros((1, 128), F32)
    for k, total in enumerate(totals):
        total = jnp.sum(jnp.where(mine, total, 0.0), axis=0, keepdims=True)
        line = jnp.where(lane == k, jnp.sum(total, axis=1, keepdims=True), line)
    moments[...] = jnp.broadcast_to(line, moments.shape)


def solve(moments):
    def ratio(top, pivot, scale):
        good = pivot > 1e-7 * scale
        return jnp.where(good, top / jnp.where(good, pivot, 1.0), 0.0)

    m = moments
    l10 = ratio(m[2], m[1], 0.0)
    l20 = ratio(m[3], m[1], 0.0)
    d1 = m[3] - l10 * m[2]
    e1 = m[4] - l20 * m[2]
    l21 = ratio(e1, d1, m[3])
    d2 = m[5] - l20 * m[3] - l21 * e1
    y1 = m[1] - l10 * m[0]
    y2 = m[2] - l20 * m[0] - l21 * y1
    c2 = ratio(y2, d2, m[5])
    c1 = ratio(y1, d1, m[3]) - l21 * c2
    c0 = ratio(m[0], m[1], 0.0) - l10 * c1 - l20 * c2
    return c0, c1, c2


def halves(x):
    high = x.astype(BF16)
    return high, (x - high.astype(F32)).astype(BF16)


def last_kernel(moments, zeroth, first, second, velocity, out):
    line = jnp.sum(moments[...], axis=0, keepdims=True)
    lane = lane_of((1, 128))
    mu = [jnp.sum(jnp.where(lane == k, line, 0.0), axis=1, keepdims=True) for k in range(6)]
    c0, c1, c2 = [HALF_STEP * c for c in solve(mu)]
    blocks = []
    for c in range(3):
        column = []
        for comp in range(3):
            for a in range(2):
                for b in range(2):
                    n = 27 * comp + 9 * a + 3 * b + c
                    column.append(c0 * zeroth[n] + c1 * first[n] + c2 * second[n])
        blocks.append(jnp.concatenate(column, axis=0))
    joined = jnp.concatenate(blocks, axis=1)
    row = lax.broadcasted_iota(jnp.int32, (48, 96), 0)
    source = lax.broadcasted_iota(jnp.int32, (48, 96), 1)
    wanted = (row // 8) * 16 + (row % 2) * 8 + HALO + (row % 8) // 2
    move = (source == wanted).astype(F32).astype(BF16)
    high, low = halves(joined)
    moved = jnp.dot(move, high, preferred_element_type=F32) + jnp.dot(move, low, preferred_element_type=F32)
    source = lax.broadcasted_iota(jnp.int32, (384, 384), 0)
    node = lax.broadcasted_iota(jnp.int32, (384, 384), 1)
    wanted = jnp.where(node < 256, (node % 2) * 128 + node // 2, 383)
    place = ((source == wanted) & (node <= 256)).astype(F32).astype(BF16)
    high, low = halves(moved)
    placed = jnp.dot(high, place, preferred_element_type=F32) + jnp.dot(low, place, preferred_element_type=F32)
    for comp in range(3):
        for x in range(2):
            start = 16 * comp + 8 * x
            out[comp, x] = velocity[comp, x] + placed[start : start + 8, : velocity.shape[3]]


VMEM = pl.BlockSpec(memory_space=pltpu.VMEM)


def call(kernel, outs, *args, scratch=(), flops=100000):
    shapes = [jax.ShapeDtypeStruct(shape, F32) for shape in outs]
    moved = sum(a.size * a.dtype.itemsize for a in args) + sum(4 * int(np.prod(s)) for s in outs)
    return pl.pallas_call(
        kernel,
        out_shape=shapes,
        in_specs=[VMEM] * len(args),
        out_specs=[VMEM] * len(outs),
        scratch_shapes=list(scratch),
        compiler_params=pltpu.CompilerParams(vmem_limit_bytes=32 * 1024 * 1024),
        cost_estimate=pl.CostEstimate(flops=flops, bytes_accessed=moved, transcendentals=0),
        name=kernel.__name__,
    )(*args)


def shift(x, axis, by):
    count = lax.axis_size(axis)
    return lax.ppermute(x, axis, [(i, (i + by) % count) for i in range(count)])


def local(velocity, energy, density, material, geometry, mass_weight, energy_mass):
    tile = (4, 128)
    geometry = geometry.reshape((648,) + tile)
    density = density.reshape((8,) + tile)
    energy = energy.reshape((8,) + tile)
    energy_mass = energy_mass.reshape((8,) + tile)
    mass_weight = mass_weight.reshape((27,) + tile)
    material = material.reshape(tile)
    full = (8, 128)
    pair = (2, 128)
    devices = lax.axis_size("slab") * lax.axis_size("brick")

    force, to_left, to_right = call(
        force_kernel, [(81,) + tile, (27,) + tile, (27,) + tile], geometry, density, energy, material, mass_weight
    )
    (spread,) = call(spread_kernel, [(36,) + full], velocity)
    from_right = shift(to_left, "slab", -1)
    from_left = shift(to_right, "slab", 1)
    own, to_low, to_high = call(
        rim_kernel,
        [(81,) + tile, (126,) + pair, (108,) + pair],
        force, from_left, from_right, mass_weight, spread,
    )
    from_high = shift(to_low, "brick", -1)
    from_low = shift(to_high, "brick", 1)
    zeroth, weight, image, to_left, to_right, speeds = call(
        first_kernel,
        [(81,) + full, (27,) + full, (81,) + full, (45,) + full, (18,) + full, (54,) + full],
        own, from_low, from_high, mass_weight, spread,
        scratch=[pltpu.VMEM((81,) + full, F32)],
    )
    from_right = shift(to_left, "slab", -1)
    from_left = shift(to_right, "slab", 1)
    first, image, to_left, to_right = call(
        second_kernel,
        [(81,) + full, (81,) + full, (18,) + full, (18,) + full],
        image, from_left, from_right, weight,
    )
    (energy_half,) = call(
        work_kernel, [(8,) + tile], geometry, density, energy, material, energy_mass, speeds, from_right
    )
    from_right = shift(to_left, "slab", -1)
    from_left = shift(to_right, "slab", 1)
    second, moments = call(
        moment_kernel, [(81,) + full, (devices, 128)], image, from_left, from_right, weight, zeroth, first
    )
    moments = lax.all_to_all(moments, ("slab", "brick"), 0, 0, tiled=True)
    (velocity_half,) = call(last_kernel, [velocity.shape], moments, zeroth, first, second, velocity)
    return (velocity_half, energy_half.reshape(8, 1, 4, 128))


def solution(mesh):
    nodes = P(None, "slab", "brick", None)
    return jax.shard_map(
        local,
        mesh=mesh,
        in_specs=(
            nodes,
            nodes,
            nodes,
            P("slab", "brick", None),
            P(None, None, "slab", "brick", None),
            nodes,
            nodes,
        ),
        out_specs=(nodes, nodes),
        check_vma=False,
    )
```

```python
import jax
import jax.numpy as jnp
import numpy as np
from jax import lax
from jax.experimental import pallas as pl
from jax.experimental.pallas import tpu as pltpu
from jax.sharding import PartitionSpec as P

HALF_STEP = 0.25
GRAVITY = 1.0
F32 = jnp.float32
BF16 = jnp.bfloat16

OFFSET = float(np.sqrt(0.6) / 2.0)
SIDE = 0.3
MIDDLE = 0.4
LINE_WEIGHTS = (5.0 / 18.0, 8.0 / 18.0, 5.0 / 18.0)
POINT_WEIGHT = [a * b * c for a in LINE_WEIGHTS for b in LINE_WEIGHTS for c in LINE_WEIGHTS]
OWN = 4
HALO = 2


def lines(direction):
    stride = (9, 3, 1)[direction]
    return [(n, n + stride, n + 2 * stride) for n in range(27) if (n // stride) % 3 == 0]


def to_points(values):
    values = list(values)
    for direction in range(3):
        for i, j, k in lines(direction):
            even = SIDE * (values[i] + values[k]) + MIDDLE * values[j]
            odd = OFFSET * (values[i] - values[k])
            values[i], values[k] = even + odd, even - odd
    return values


def from_points(values):
    values = list(values)
    for direction in range(3):
        for i, j, k in lines(direction):
            total = values[i] + values[k]
            odd = OFFSET * (values[i] - values[k])
            even = SIDE * total
            values[i], values[k] = even + odd, even - odd
            values[j] = values[j] + MIDDLE * total
    return values


def lane_of(shape):
    return lax.broadcasted_iota(jnp.int32, shape, len(shape) - 1)


def assemble_z(values, wall):
    values = list(values)
    lane = lane_of(values[0].shape)
    first, last = lane == 0, lane == 127
    for i, _, k in lines(2):
        total = values[i] + jnp.where(first, 0.0, pltpu.roll(values[k], 1, 1))
        top = values[k]
        if wall:
            total = jnp.where(first, 0.0, total)
            top = jnp.zeros_like(top)
        values[i] = total
        values[k] = jnp.where(last, top, pltpu.roll(total, 127, 1))
    return values


def assemble_y(values):
    values = list(values)
    for i, _, k in lines(1):
        values[i] = values[i] + pltpu.roll(values[k], 1, 0)
        values[k] = pltpu.roll(values[i], 7, 0)
    return values


def force_kernel(
    geometry_in, density_in, energy_in, material_in, mass_weight_in,
    field, to_left, to_right,
    geometry, density, energy, material, mass_weight, sems,
):
    small = [
        pltpu.make_async_copy(source, target, sems.at[3 + i])
        for i, (source, target) in enumerate(
            [(density_in, density), (energy_in, energy), (material_in, material), (mass_weight_in, mass_weight)]
        )
    ]
    parts = [
        pltpu.make_async_copy(
            geometry_in.at[pl.ds(216 * comp, 216)], geometry.at[pl.ds(216 * comp, 216)], sems.at[comp]
        )
        for comp in range(3)
    ]
    for copy in small + parts:
        copy.start()
    for copy in small:
        copy.wait()
    gamma = jnp.where(material[...] == 0, 2.0 / 3.0, 0.4).astype(F32)
    pressure = (gamma[None] * density[...] * energy[...]).astype(BF16).astype(F32)
    gravity = from_points([mass_weight[q] * POINT_WEIGHT[q] for q in range(27)])
    for comp in range(3):
        parts[comp].wait()
        for n in range(27):
            r = 27 * comp + n
            block = geometry[pl.ds(8 * r, 8)].astype(F32)
            value = -jnp.sum(block * pressure, axis=0)
            if comp == 2:
                value = value - GRAVITY * gravity[n]
            field[r] = value
            if n // 9 == 0:
                to_left[9 * comp + n] = value
            if n // 9 == 2:
                to_right[9 * comp + n - 18] = value


def spread_kernel(velocity, out):
    rows = velocity[...].astype(BF16).reshape(48, velocity.shape[3])
    low = rows[:, :256]
    high = rows[:, 256:257].astype(F32)
    node = lax.broadcasted_iota(jnp.int32, (256, 384), 0)
    lane = lax.broadcasted_iota(jnp.int32, (256, 384), 1)
    pick = (node == 2 * (lane % 128) + lane // 128).astype(F32).astype(BF16)
    spread = jnp.dot(low, pick, preferred_element_type=F32)
    top = jnp.where(lane_of((48, 128)) == 127, high, 0.0)
    spread = jnp.concatenate([spread[:, :256], spread[:, 256:] + top], axis=1)
    row = lax.broadcasted_iota(jnp.int32, (96, 48), 0)
    source = lax.broadcasted_iota(jnp.int32, (96, 48), 1)
    wanted = (row // 16) * 8 + 2 * (row % 8) + (row // 8) % 2
    move = ((source == wanted) & (row % 8 < OWN)).astype(F32).astype(BF16)
    moved = jnp.dot(move, spread.astype(BF16), preferred_element_type=F32)
    for group in range(12):
        for c in range(3):
            out[3 * group + c] = moved[8 * group : 8 * group + 8, 128 * c : 128 * c + 128]


def rim_kernel(field, from_left, from_right, mass_weight, spread, out, to_low, to_high):
    for comp in range(3):
        for n in range(27):
            r = 27 * comp + n
            value = field[r]
            if n // 9 == 0:
                value = value + from_left[9 * comp + n]
            if n // 9 == 2:
                value = value + from_right[9 * comp + n - 18]
            out[r] = value
            to_low[r] = value[:HALO].astype(BF16)
            to_high[r] = value[OWN - HALO :].astype(BF16)
    for q in range(27):
        to_low[81 + q] = mass_weight[q, :HALO].astype(BF16)
        to_high[81 + q] = mass_weight[q, OWN - HALO :].astype(BF16)
    for comp in range(3):
        for a in range(2):
            for c in range(3):
                to_low[108 + 6 * comp + 3 * a + c] = spread[12 * comp + 6 * a + c, :HALO].astype(BF16)


def send_planes(values, comp, to_left, to_right):
    slot = 0
    for b in range(2):
        for c in range(3):
            to_left[6 * comp + slot] = values[3 * b + c]
            to_right[6 * comp + slot] = values[18 + 3 * b + c]
            slot += 1


def apply_mass(values, weight, wall):
    points = to_points(values)
    points = [points[q] * weight[q] for q in range(27)]
    return assemble_y(assemble_z(from_points(points), wall))


def first_kernel(
    own, from_low, from_high, mass_weight, spread, field, weight, image, to_left, to_right, speeds, rows
):
    for q in range(27):
        rows[q, :HALO] = from_low[81 + q].astype(F32)
        rows[q, HALO : HALO + OWN] = mass_weight[q]
        rows[q, HALO + OWN :] = from_high[81 + q].astype(F32)
    for q in range(27):
        weight[q] = rows[q] * POINT_WEIGHT[q]
    for r in range(81):
        rows[r, :HALO] = from_low[r].astype(F32)
        rows[r, HALO : HALO + OWN] = own[r]
        rows[r, HALO + OWN :] = from_high[r].astype(F32)
    for comp in range(3):
        values = [rows[27 * comp + n] for n in range(27)]
        values = assemble_y(assemble_z(values, comp == 2))
        for n in range(27):
            field[27 * comp + n] = values[n]
        values = apply_mass(values, weight, comp == 2)
        for n in range(27):
            image[27 * comp + n] = values[n]
        send_planes(values, comp, to_left, to_right)
    row = lax.broadcasted_iota(jnp.int32, (8, 128), 0)
    plane = []
    for comp in range(3):
        for a in range(2):
            speed = [spread[12 * comp + 6 * a + n] for n in range(6)]
            for c in range(3):
                beyond = from_high[108 + 6 * comp + 3 * a + c].astype(F32)[0:1]
                speed.append(jnp.where(row == OWN - 1, beyond, pltpu.roll(speed[c], 7, 0)))
            for n in range(9):
                speeds[18 * comp + 9 * a + n] = speed[n]
            if a == 0:
                plane += speed
    for n in range(0, 27, 2):
        upper = plane[n] if n == 26 else pltpu.roll(plane[n + 1], 4, 0)
        to_left[18 + n // 2] = jnp.where(row < OWN, plane[n], upper)


def take_planes(image, from_left, from_right, comp):
    values = [image[27 * comp + n] for n in range(27)]
    slot = 0
    for b in range(2):
        for c in range(3):
            values[3 * b + c] = values[3 * b + c] + from_left[6 * comp + slot]
            values[18 + 3 * b + c] = values[18 + 3 * b + c] + from_right[6 * comp + slot]
            slot += 1
    for a in (0, 18):
        for c in range(3):
            values[a + 6 + c] = pltpu.roll(values[a + c], 7, 0)
    return values


def second_kernel(image, from_left, from_right, weight, field, image_out, to_left, to_right):
    for comp in range(3):
        values = take_planes(image, from_left, from_right, comp)
        for n in range(27):
            field[27 * comp + n] = values[n]
        values = apply_mass(values, weight, comp == 2)
        for n in range(27):
            image_out[27 * comp + n] = values[n]
        send_planes(values, comp, to_left, to_right)


def work_kernel(geometry, density, energy, material, energy_mass, speeds, from_right, out):
    gamma = jnp.where(material[...] == 0, 2.0 / 3.0, 0.4).astype(F32)
    pressure = (gamma[None] * density[...] * energy[...]).astype(BF16).astype(F32)
    work = jnp.zeros_like(pressure)
    for comp in range(3):
        for n in range(27):
            if n < 18:
                speed = speeds[18 * comp + n, :OWN]
            else:
                k = 9 * comp + n - 18
                speed = from_right[18 + k // 2, OWN * (k % 2) : OWN * (k % 2) + OWN]
            work = work + geometry[pl.ds(8 * (27 * comp + n), 8)].astype(F32) * speed[None]
    out[...] = energy[...] + HALF_STEP * pressure * work / energy_mass[...]


def dot_owned(first, second, comp, total):
    last = lane_of((8, 128)) == 127
    for a in range(2):
        for b in range(2):
            n = 27 * comp + 9 * a + 3 * b
            total = total + first[n] * second[n] + first[n + 1] * second[n + 1]
            total = total + jnp.where(last, first[n + 2] * second[n + 2], 0.0)
    return total


def product_kernel(zeroth, first, products):
    for k, (one, other) in enumerate([(zeroth, zeroth), (zeroth, first), (first, first)]):
        total = jnp.zeros((8, 128), F32)
        for comp in range(3):
            total = dot_owned(one, other, comp, total)
        products[k] = total


def moment_kernel(image, from_left, from_right, weight, first, products, second, moments):
    zero = jnp.zeros((8, 128), F32)
    cross, norm, quadratic = zero, zero, zero
    for comp in range(3):
        values = take_planes(image, from_left, from_right, comp)
        for n in range(27):
            second[27 * comp + n] = values[n]
        values_at = {27 * comp + n: values[n] for n in range(27)}
        cross = dot_owned(first, values_at, comp, cross)
        norm = dot_owned(values_at, values_at, comp, norm)
        points = to_points(values)
        for q in range(27):
            quadratic = quadratic + points[q] * points[q] * weight[q]
    row = lax.broadcasted_iota(jnp.int32, (8, 128), 0)
    lane = lane_of((1, 128))
    mine = (row >= HALO) & (row < HALO + OWN)
    line = jnp.zeros((1, 128), F32)
    for k, total in enumerate([products[0], products[1], products[2], cross, norm, quadratic]):
        total = jnp.sum(jnp.where(mine, total, 0.0), axis=0, keepdims=True)
        line = jnp.where(lane == k, jnp.sum(total, axis=1, keepdims=True), line)
    moments[...] = jnp.broadcast_to(line, moments.shape)


def solve(moments):
    def ratio(top, pivot, scale):
        good = pivot > 1e-7 * scale
        return jnp.where(good, top / jnp.where(good, pivot, 1.0), 0.0)

    m = moments
    l10 = ratio(m[2], m[1], 0.0)
    l20 = ratio(m[3], m[1], 0.0)
    d1 = m[3] - l10 * m[2]
    e1 = m[4] - l20 * m[2]
    l21 = ratio(e1, d1, m[3])
    d2 = m[5] - l20 * m[3] - l21 * e1
    y1 = m[1] - l10 * m[0]
    y2 = m[2] - l20 * m[0] - l21 * y1
    c2 = ratio(y2, d2, m[5])
    c1 = ratio(y1, d1, m[3]) - l21 * c2
    c0 = ratio(m[0], m[1], 0.0) - l10 * c1 - l20 * c2
    return c0, c1, c2


def halves(x):
    high = x.astype(BF16)
    return high, (x - high.astype(F32)).astype(BF16)


def nodal_kernel(zeroth, first, second, out):
    row = lax.broadcasted_iota(jnp.int32, (48, 96), 0)
    source = lax.broadcasted_iota(jnp.int32, (48, 96), 1)
    wanted = (row // 8) * 16 + (row % 2) * 8 + HALO + (row % 8) // 2
    move = (source == wanted).astype(F32).astype(BF16)
    source = lax.broadcasted_iota(jnp.int32, (384, 384), 0)
    node = lax.broadcasted_iota(jnp.int32, (384, 384), 1)
    wanted = jnp.where(node < 256, (node % 2) * 128 + node // 2, 383)
    place = ((source == wanted) & (node <= 256)).astype(F32).astype(BF16)
    for k, field in enumerate((zeroth, first, second)):
        blocks = []
        for c in range(3):
            column = []
            for comp in range(3):
                for a in range(2):
                    for b in range(2):
                        column.append(field[27 * comp + 9 * a + 3 * b + c])
            blocks.append(jnp.concatenate(column, axis=0))
        high, low = halves(jnp.concatenate(blocks, axis=1))
        moved = jnp.dot(move, high, preferred_element_type=F32) + jnp.dot(move, low, preferred_element_type=F32)
        high, low = halves(moved)
        out[k] = jnp.dot(high, place, preferred_element_type=F32) + jnp.dot(low, place, preferred_element_type=F32)


def last_kernel(moments, nodal, velocity, out):
    line = jnp.sum(moments[...], axis=0, keepdims=True)
    lane = lane_of((1, 128))
    mu = [jnp.sum(jnp.where(lane == k, line, 0.0), axis=1, keepdims=True) for k in range(6)]
    c0, c1, c2 = [HALF_STEP * c for c in solve(mu)]
    for comp in range(3):
        for x in range(2):
            start = 16 * comp + 8 * x
            part = [nodal[k, pl.ds(start, 8), : velocity.shape[3]] for k in range(3)]
            out[comp, x] = velocity[comp, x] + (c0 * part[0] + c1 * part[1] + c2 * part[2])


VMEM = pl.BlockSpec(memory_space=pltpu.VMEM)


def call(kernel, outs, *args, scratch=(), flops=100000, place=VMEM, dtypes=None):
    shapes = [jax.ShapeDtypeStruct(shape, dtype) for shape, dtype in zip(outs, dtypes or [F32] * len(outs))]
    moved = sum(a.size * a.dtype.itemsize for a in args) + sum(4 * int(np.prod(s)) for s in outs)
    return pl.pallas_call(
        kernel,
        out_shape=shapes,
        in_specs=[place] * len(args),
        out_specs=[VMEM] * len(outs),
        scratch_shapes=list(scratch),
        compiler_params=pltpu.CompilerParams(vmem_limit_bytes=32 * 1024 * 1024),
        cost_estimate=pl.CostEstimate(flops=flops, bytes_accessed=moved, transcendentals=0),
        name=kernel.__name__,
    )(*args)


def shift(x, axis, by):
    count = lax.axis_size(axis)
    return lax.ppermute(x, axis, [(i, (i + by) % count) for i in range(count)])


def local(velocity, energy, density, material, geometry, mass_weight, energy_mass):
    tile = (4, 128)
    geometry = geometry.reshape((648,) + tile)
    density = density.reshape((8,) + tile)
    energy = energy.reshape((8,) + tile)
    energy_mass = energy_mass.reshape((8,) + tile)
    mass_weight = mass_weight.reshape((27,) + tile)
    material = material.reshape(tile)
    full = (8, 128)
    pair = (2, 128)
    devices = lax.axis_size("slab") * lax.axis_size("brick")

    force, to_left, to_right = call(
        force_kernel,
        [(81,) + tile, (27,) + tile, (27,) + tile],
        *[pltpu.with_memory_space_constraint(x, pltpu.HBM) for x in (geometry, density, energy, material, mass_weight)],
        scratch=[
            pltpu.VMEM((648,) + tile, BF16),
            pltpu.VMEM((8,) + tile, F32),
            pltpu.VMEM((8,) + tile, F32),
            pltpu.VMEM(tile, jnp.int32),
            pltpu.VMEM((27,) + tile, F32),
            pltpu.SemaphoreType.DMA((7,)),
        ],
        place=pl.BlockSpec(memory_space=pltpu.HBM),
    )
    (spread,) = call(spread_kernel, [(36,) + full], velocity)
    from_right = shift(to_left, "slab", -1)
    from_left = shift(to_right, "slab", 1)
    own, to_low, to_high = call(
        rim_kernel,
        [(81,) + tile, (126,) + pair, (108,) + pair],
        force, from_left, from_right, mass_weight, spread,
        dtypes=[F32, BF16, BF16],
    )
    from_high = shift(to_low, "brick", -1)
    from_low = shift(to_high, "brick", 1)
    zeroth, weight, image, to_left, to_right, speeds = call(
        first_kernel,
        [(81,) + full, (27,) + full, (81,) + full, (32,) + full, (18,) + full, (54,) + full],
        own, from_low, from_high, mass_weight, spread,
        scratch=[pltpu.VMEM((81,) + full, F32)],
    )
    from_right = shift(to_left, "slab", -1)
    from_left = shift(to_right, "slab", 1)
    first, image, to_left, to_right = call(
        second_kernel,
        [(81,) + full, (81,) + full, (18,) + full, (18,) + full],
        image, from_left, from_right, weight,
    )
    (energy_half,) = call(
        work_kernel, [(8,) + tile], geometry, density, energy, material, energy_mass, speeds, from_right
    )
    from_right = shift(to_left, "slab", -1)
    from_left = shift(to_right, "slab", 1)
    (products,) = call(product_kernel, [(3,) + full], zeroth, first)
    second, moments = call(
        moment_kernel, [(81,) + full, (devices, 128)], image, from_left, from_right, weight, first, products
    )
    moments = lax.all_to_all(moments, ("slab", "brick"), 0, 0, tiled=True)
    (nodal,) = call(nodal_kernel, [(3, 48, 384)], zeroth, first, second)
    (velocity_half,) = call(last_kernel, [velocity.shape], moments, nodal, velocity)
    return (velocity_half, energy_half.reshape(8, 1, 4, 128))


def solution(mesh):
    nodes = P(None, "slab", "brick", None)
    return jax.shard_map(
        local,
        mesh=mesh,
        in_specs=(
            nodes,
            nodes,
            nodes,
            P("slab", "brick", None),
            P(None, None, "slab", "brick", None),
            nodes,
            nodes,
        ),
        out_specs=(nodes, nodes),
        check_vma=False,
    )
```

```python
import jax
import jax.numpy as jnp
import numpy as np
from jax import lax
from jax.experimental import pallas as pl
from jax.experimental.pallas import tpu as pltpu
from jax.sharding import PartitionSpec as P

HALF_STEP = 0.25
GRAVITY = 1.0
F32 = jnp.float32
BF16 = jnp.bfloat16

OFFSET = float(np.sqrt(0.6) / 2.0)
SIDE = 0.3
MIDDLE = 0.4
LINE_WEIGHTS = (5.0 / 18.0, 8.0 / 18.0, 5.0 / 18.0)
POINT_WEIGHT = [a * b * c for a in LINE_WEIGHTS for b in LINE_WEIGHTS for c in LINE_WEIGHTS]
OWN = 4
HALO = 2


def lines(direction):
    stride = (9, 3, 1)[direction]
    return [(n, n + stride, n + 2 * stride) for n in range(27) if (n // stride) % 3 == 0]


def to_points(values):
    values = list(values)
    for direction in range(3):
        for i, j, k in lines(direction):
            even = SIDE * (values[i] + values[k]) + MIDDLE * values[j]
            odd = OFFSET * (values[i] - values[k])
            values[i], values[k] = even + odd, even - odd
    return values


def from_points(values):
    values = list(values)
    for direction in range(3):
        for i, j, k in lines(direction):
            total = values[i] + values[k]
            odd = OFFSET * (values[i] - values[k])
            even = SIDE * total
            values[i], values[k] = even + odd, even - odd
            values[j] = values[j] + MIDDLE * total
    return values


def lane_of(shape):
    return lax.broadcasted_iota(jnp.int32, shape, len(shape) - 1)


def assemble_z(values, wall):
    values = list(values)
    lane = lane_of(values[0].shape)
    first, last = lane == 0, lane == 127
    for i, _, k in lines(2):
        total = values[i] + jnp.where(first, 0.0, pltpu.roll(values[k], 1, 1))
        top = values[k]
        if wall:
            total = jnp.where(first, 0.0, total)
            top = jnp.zeros_like(top)
        values[i] = total
        values[k] = jnp.where(last, top, pltpu.roll(total, 127, 1))
    return values


def assemble_y(values):
    values = list(values)
    for i, _, k in lines(1):
        values[i] = values[i] + pltpu.roll(values[k], 1, 0)
        values[k] = pltpu.roll(values[i], 7, 0)
    return values


def force_kernel(
    geometry_in, density_in, energy_in, material_in, mass_weight_in,
    field, to_left, to_right,
    geometry, density, energy, material, mass_weight, sems,
):
    small = [
        pltpu.make_async_copy(source, target, sems.at[3 + i])
        for i, (source, target) in enumerate(
            [(density_in, density), (energy_in, energy), (material_in, material), (mass_weight_in, mass_weight)]
        )
    ]
    parts = [
        pltpu.make_async_copy(
            geometry_in.at[pl.ds(216 * comp, 216)], geometry.at[pl.ds(216 * comp, 216)], sems.at[comp]
        )
        for comp in range(3)
    ]
    for copy in small + parts:
        copy.start()
    for copy in small:
        copy.wait()
    gamma = jnp.where(material[...] == 0, 2.0 / 3.0, 0.4).astype(F32)
    pressure = (gamma[None] * density[...] * energy[...]).astype(BF16).astype(F32)
    gravity = from_points([mass_weight[q] * POINT_WEIGHT[q] for q in range(27)])
    for comp in range(3):
        parts[comp].wait()
        for n in range(27):
            r = 27 * comp + n
            block = geometry[pl.ds(8 * r, 8)].astype(F32)
            value = -jnp.sum(block * pressure, axis=0)
            if comp == 2:
                value = value - GRAVITY * gravity[n]
            field[r] = value
            if n // 9 == 0:
                to_left[9 * comp + n] = value.astype(BF16)
            if n // 9 == 2:
                to_right[9 * comp + n - 18] = value.astype(BF16)


def spread_kernel(velocity, out):
    rows = velocity[...].astype(BF16).reshape(48, velocity.shape[3])
    low = rows[:, :256]
    high = rows[:, 256:257].astype(F32)
    node = lax.broadcasted_iota(jnp.int32, (256, 384), 0)
    lane = lax.broadcasted_iota(jnp.int32, (256, 384), 1)
    pick = (node == 2 * (lane % 128) + lane // 128).astype(F32).astype(BF16)
    spread = jnp.dot(low, pick, preferred_element_type=F32)
    top = jnp.where(lane_of((48, 128)) == 127, high, 0.0)
    spread = jnp.concatenate([spread[:, :256], spread[:, 256:] + top], axis=1)
    row = lax.broadcasted_iota(jnp.int32, (96, 48), 0)
    source = lax.broadcasted_iota(jnp.int32, (96, 48), 1)
    wanted = (row // 16) * 8 + 2 * (row % 8) + (row // 8) % 2
    move = ((source == wanted) & (row % 8 < OWN)).astype(F32).astype(BF16)
    moved = jnp.dot(move, spread.astype(BF16), preferred_element_type=F32)
    for group in range(12):
        for c in range(3):
            out[3 * group + c] = moved[8 * group : 8 * group + 8, 128 * c : 128 * c + 128]


def rim_kernel(field, from_left, from_right, mass_weight, spread, out, to_low, to_high):
    for comp in range(3):
        for n in range(27):
            r = 27 * comp + n
            value = field[r]
            if n // 9 == 0:
                value = value + from_left[9 * comp + n].astype(F32)
            if n // 9 == 2:
                value = value + from_right[9 * comp + n - 18].astype(F32)
            out[r] = value
            to_low[r] = value[:HALO].astype(BF16)
            to_high[r] = value[OWN - HALO :].astype(BF16)
    for q in range(27):
        to_low[81 + q] = mass_weight[q, :HALO].astype(BF16)
        to_high[81 + q] = mass_weight[q, OWN - HALO :].astype(BF16)
    for comp in range(3):
        for a in range(2):
            for c in range(3):
                to_low[108 + 6 * comp + 3 * a + c] = spread[12 * comp + 6 * a + c, :HALO].astype(BF16)


def send_planes(values, comp, to_left, to_right):
    slot = 0
    for b in range(2):
        for c in range(3):
            to_left[6 * comp + slot] = values[3 * b + c].astype(BF16)
            to_right[6 * comp + slot] = values[18 + 3 * b + c].astype(BF16)
            slot += 1


def apply_mass(values, weight, wall):
    points = to_points(values)
    points = [points[q] * weight[q] for q in range(27)]
    return assemble_y(assemble_z(from_points(points), wall))


def first_kernel(
    own, from_low, from_high, mass_weight, spread, field, weight, image, to_left, to_right, speeds, rows
):
    for q in range(27):
        rows[q, :HALO] = from_low[81 + q].astype(F32)
        rows[q, HALO : HALO + OWN] = mass_weight[q]
        rows[q, HALO + OWN :] = from_high[81 + q].astype(F32)
    for q in range(27):
        weight[q] = rows[q] * POINT_WEIGHT[q]
    for r in range(81):
        rows[r, :HALO] = from_low[r].astype(F32)
        rows[r, HALO : HALO + OWN] = own[r]
        rows[r, HALO + OWN :] = from_high[r].astype(F32)
    for comp in range(3):
        values = [rows[27 * comp + n] for n in range(27)]
        values = assemble_y(assemble_z(values, comp == 2))
        for n in range(27):
            field[27 * comp + n] = values[n]
        values = apply_mass(values, weight, comp == 2)
        for n in range(27):
            image[27 * comp + n] = values[n]
        send_planes(values, comp, to_left, to_right)
    row = lax.broadcasted_iota(jnp.int32, (8, 128), 0)
    plane = []
    for comp in range(3):
        for a in range(2):
            speed = [spread[12 * comp + 6 * a + n] for n in range(6)]
            for c in range(3):
                beyond = from_high[108 + 6 * comp + 3 * a + c].astype(F32)[0:1]
                speed.append(jnp.where(row == OWN - 1, beyond, pltpu.roll(speed[c], 7, 0)))
            for n in range(9):
                speeds[18 * comp + 9 * a + n] = speed[n]
            if a == 0:
                plane += speed
    for n in range(0, 27, 2):
        upper = plane[n] if n == 26 else pltpu.roll(plane[n + 1], 4, 0)
        to_left[18 + n // 2] = jnp.where(row < OWN, plane[n], upper).astype(BF16)


def take_planes(image, from_left, from_right, comp):
    values = [image[27 * comp + n] for n in range(27)]
    slot = 0
    for b in range(2):
        for c in range(3):
            values[3 * b + c] = values[3 * b + c] + from_left[6 * comp + slot].astype(F32)
            values[18 + 3 * b + c] = values[18 + 3 * b + c] + from_right[6 * comp + slot].astype(F32)
            slot += 1
    for a in (0, 18):
        for c in range(3):
            values[a + 6 + c] = pltpu.roll(values[a + c], 7, 0)
    return values


def second_kernel(image, from_left, from_right, weight, field, image_out, to_left, to_right):
    for comp in range(3):
        values = take_planes(image, from_left, from_right, comp)
        for n in range(27):
            field[27 * comp + n] = values[n]
        values = apply_mass(values, weight, comp == 2)
        for n in range(27):
            image_out[27 * comp + n] = values[n]
        send_planes(values, comp, to_left, to_right)


def work_kernel(geometry, density, energy, material, energy_mass, speeds, from_right, out):
    gamma = jnp.where(material[...] == 0, 2.0 / 3.0, 0.4).astype(F32)
    pressure = (gamma[None] * density[...] * energy[...]).astype(BF16).astype(F32)
    work = jnp.zeros_like(pressure)
    for comp in range(3):
        for n in range(27):
            if n < 18:
                speed = speeds[18 * comp + n, :OWN]
            else:
                k = 9 * comp + n - 18
                speed = from_right[18 + k // 2].astype(F32)[OWN * (k % 2) : OWN * (k % 2) + OWN]
            work = work + geometry[pl.ds(8 * (27 * comp + n), 8)].astype(F32) * speed[None]
    out[...] = energy[...] + HALF_STEP * pressure * work / energy_mass[...]


def dot_owned(first, second, comp, total):
    last = lane_of((8, 128)) == 127
    for a in range(2):
        for b in range(2):
            n = 27 * comp + 9 * a + 3 * b
            total = total + first[n] * second[n] + first[n + 1] * second[n + 1]
            total = total + jnp.where(last, first[n + 2] * second[n + 2], 0.0)
    return total


def product_kernel(zeroth, first, products):
    for k, (one, other) in enumerate([(zeroth, zeroth), (zeroth, first), (first, first)]):
        total = jnp.zeros((8, 128), F32)
        for comp in range(3):
            total = dot_owned(one, other, comp, total)
        products[k] = total


def moment_kernel(image, from_left, from_right, weight, first, products, second, moments):
    zero = jnp.zeros((8, 128), F32)
    cross, norm, quadratic = zero, zero, zero
    for comp in range(3):
        values = take_planes(image, from_left, from_right, comp)
        for n in range(27):
            second[27 * comp + n] = values[n]
        values_at = {27 * comp + n: values[n] for n in range(27)}
        cross = dot_owned(first, values_at, comp, cross)
        norm = dot_owned(values_at, values_at, comp, norm)
        points = to_points(values)
        for q in range(27):
            quadratic = quadratic + points[q] * points[q] * weight[q]
    row = lax.broadcasted_iota(jnp.int32, (8, 128), 0)
    mine = (row >= HALO) & (row < HALO + OWN)
    sums = jnp.zeros((8, 128), F32)
    for k, total in enumerate([products[0], products[1], products[2], cross, norm, quadratic]):
        total = jnp.sum(jnp.where(mine, total, 0.0), axis=0, keepdims=True)
        sums = jnp.where(row == k, total, sums)
    sums = jnp.sum(sums, axis=1, keepdims=True)
    line = jnp.sum(jnp.where(lane_of((8, 128)) == row, sums, 0.0), axis=0, keepdims=True)
    moments[...] = jnp.broadcast_to(line, moments.shape)


def solve(moments):
    def ratio(top, pivot, scale):
        good = pivot > 1e-7 * scale
        return jnp.where(good, top / jnp.where(good, pivot, 1.0), 0.0)

    m = moments
    l10 = ratio(m[2], m[1], 0.0)
    l20 = ratio(m[3], m[1], 0.0)
    d1 = m[3] - l10 * m[2]
    e1 = m[4] - l20 * m[2]
    l21 = ratio(e1, d1, m[3])
    d2 = m[5] - l20 * m[3] - l21 * e1
    y1 = m[1] - l10 * m[0]
    y2 = m[2] - l20 * m[0] - l21 * y1
    c2 = ratio(y2, d2, m[5])
    c1 = ratio(y1, d1, m[3]) - l21 * c2
    c0 = ratio(m[0], m[1], 0.0) - l10 * c1 - l20 * c2
    return c0, c1, c2


def halves(x):
    high = x.astype(BF16)
    return high, (x - high.astype(F32)).astype(BF16)


def nodal_kernel(zeroth, first, second, out):
    row = lax.broadcasted_iota(jnp.int32, (48, 96), 0)
    source = lax.broadcasted_iota(jnp.int32, (48, 96), 1)
    wanted = (row // 8) * 16 + (row % 2) * 8 + HALO + (row % 8) // 2
    move = (source == wanted).astype(F32).astype(BF16)
    source = lax.broadcasted_iota(jnp.int32, (384, 384), 0)
    node = lax.broadcasted_iota(jnp.int32, (384, 384), 1)
    wanted = jnp.where(node < 256, (node % 2) * 128 + node // 2, 383)
    place = ((source == wanted) & (node <= 256)).astype(F32).astype(BF16)
    for k, field in enumerate((zeroth, first, second)):
        blocks = []
        for c in range(3):
            column = []
            for comp in range(3):
                for a in range(2):
                    for b in range(2):
                        column.append(field[27 * comp + 9 * a + 3 * b + c])
            blocks.append(jnp.concatenate(column, axis=0))
        high, low = halves(jnp.concatenate(blocks, axis=1))
        moved = jnp.dot(move, high, preferred_element_type=F32) + jnp.dot(move, low, preferred_element_type=F32)
        high, low = halves(moved)
        out[k] = jnp.dot(high, place, preferred_element_type=F32) + jnp.dot(low, place, preferred_element_type=F32)


def last_kernel(moments, nodal, velocity, out):
    line = jnp.sum(moments[...], axis=0, keepdims=True)
    lane = lane_of((1, 128))
    mu = [jnp.sum(jnp.where(lane == k, line, 0.0), axis=1, keepdims=True) for k in range(6)]
    c0, c1, c2 = [HALF_STEP * c for c in solve(mu)]
    for comp in range(3):
        for x in range(2):
            start = 16 * comp + 8 * x
            part = [nodal[k, pl.ds(start, 8), : velocity.shape[3]] for k in range(3)]
            out[comp, x] = velocity[comp, x] + (c0 * part[0] + c1 * part[1] + c2 * part[2])


VMEM = pl.BlockSpec(memory_space=pltpu.VMEM)


def call(kernel, outs, *args, scratch=(), flops=100000, place=VMEM, dtypes=None):
    shapes = [jax.ShapeDtypeStruct(shape, dtype) for shape, dtype in zip(outs, dtypes or [F32] * len(outs))]
    moved = sum(a.size * a.dtype.itemsize for a in args) + sum(4 * int(np.prod(s)) for s in outs)
    return pl.pallas_call(
        kernel,
        out_shape=shapes,
        in_specs=[place] * len(args),
        out_specs=[VMEM] * len(outs),
        scratch_shapes=list(scratch),
        compiler_params=pltpu.CompilerParams(vmem_limit_bytes=32 * 1024 * 1024),
        cost_estimate=pl.CostEstimate(flops=flops, bytes_accessed=moved, transcendentals=0),
        name=kernel.__name__,
    )(*args)


def shift(x, axis, by):
    count = lax.axis_size(axis)
    return lax.ppermute(x, axis, [(i, (i + by) % count) for i in range(count)])


def local(velocity, energy, density, material, geometry, mass_weight, energy_mass):
    tile = (4, 128)
    geometry = geometry.reshape((648,) + tile)
    density = density.reshape((8,) + tile)
    energy = energy.reshape((8,) + tile)
    energy_mass = energy_mass.reshape((8,) + tile)
    mass_weight = mass_weight.reshape((27,) + tile)
    material = material.reshape(tile)
    full = (8, 128)
    pair = (2, 128)
    devices = lax.axis_size("slab") * lax.axis_size("brick")

    force, to_left, to_right = call(
        force_kernel,
        [(81,) + tile, (27,) + tile, (27,) + tile],
        *[pltpu.with_memory_space_constraint(x, pltpu.HBM) for x in (geometry, density, energy, material, mass_weight)],
        scratch=[
            pltpu.VMEM((648,) + tile, BF16),
            pltpu.VMEM((8,) + tile, F32),
            pltpu.VMEM((8,) + tile, F32),
            pltpu.VMEM(tile, jnp.int32),
            pltpu.VMEM((27,) + tile, F32),
            pltpu.SemaphoreType.DMA((7,)),
        ],
        place=pl.BlockSpec(memory_space=pltpu.HBM),
        dtypes=[F32, BF16, BF16],
    )
    (spread,) = call(spread_kernel, [(36,) + full], velocity)
    from_right = shift(to_left, "slab", -1)
    from_left = shift(to_right, "slab", 1)
    own, to_low, to_high = call(
        rim_kernel,
        [(81,) + tile, (126,) + pair, (108,) + pair],
        force, from_left, from_right, mass_weight, spread,
        dtypes=[F32, BF16, BF16],
    )
    from_high = shift(to_low, "brick", -1)
    from_low = shift(to_high, "brick", 1)
    zeroth, weight, image, to_left, to_right, speeds = call(
        first_kernel,
        [(81,) + full, (27,) + full, (81,) + full, (32,) + full, (18,) + full, (54,) + full],
        own, from_low, from_high, mass_weight, spread,
        scratch=[pltpu.VMEM((81,) + full, F32)],
        dtypes=[F32, F32, F32, BF16, BF16, F32],
    )
    from_right = shift(to_left, "slab", -1)
    from_left = shift(to_right, "slab", 1)
    first, image, to_left, to_right = call(
        second_kernel,
        [(81,) + full, (81,) + full, (18,) + full, (18,) + full],
        image, from_left, from_right, weight,
        dtypes=[F32, F32, BF16, BF16],
    )
    (energy_half,) = call(
        work_kernel, [(8,) + tile], geometry, density, energy, material, energy_mass, speeds, from_right
    )
    from_right = shift(to_left, "slab", -1)
    from_left = shift(to_right, "slab", 1)
    (products,) = call(product_kernel, [(3,) + full], zeroth, first)
    second, moments = call(
        moment_kernel, [(81,) + full, (devices, 128)], image, from_left, from_right, weight, first, products
    )
    moments = pltpu.with_memory_space_constraint(moments, pltpu.VMEM)
    moments = lax.all_to_all(moments, ("slab", "brick"), 0, 0, tiled=True)
    (nodal,) = call(nodal_kernel, [(3, 48, 384)], zeroth, first, second)
    (velocity_half,) = call(last_kernel, [velocity.shape], moments, nodal, velocity)
    return (velocity_half, energy_half.reshape(8, 1, 4, 128))


def solution(mesh):
    nodes = P(None, "slab", "brick", None)
    return jax.shard_map(
        local,
        mesh=mesh,
        in_specs=(
            nodes,
            nodes,
            nodes,
            P("slab", "brick", None),
            P(None, None, "slab", "brick", None),
            nodes,
            nodes,
        ),
        out_specs=(nodes, nodes),
        check_vma=False,
    )
```

```python
import jax
import jax.numpy as jnp
import numpy as np
from jax import lax
from jax.experimental import pallas as pl
from jax.experimental.pallas import tpu as pltpu
from jax.sharding import PartitionSpec as P

HALF_STEP = 0.25
GRAVITY = 1.0
F32 = jnp.float32
BF16 = jnp.bfloat16

OFFSET = float(np.sqrt(0.6) / 2.0)
SIDE = 0.3
MIDDLE = 0.4
LINE_WEIGHTS = (5.0 / 18.0, 8.0 / 18.0, 5.0 / 18.0)
POINT_WEIGHT = [a * b * c for a in LINE_WEIGHTS for b in LINE_WEIGHTS for c in LINE_WEIGHTS]
OWN = 4
HALO = 2


def lines(direction):
    stride = (9, 3, 1)[direction]
    return [(n, n + stride, n + 2 * stride) for n in range(27) if (n // stride) % 3 == 0]


def to_points(values):
    values = list(values)
    for direction in range(3):
        for i, j, k in lines(direction):
            even = SIDE * (values[i] + values[k]) + MIDDLE * values[j]
            odd = OFFSET * (values[i] - values[k])
            values[i], values[k] = even + odd, even - odd
    return values


def from_points(values):
    values = list(values)
    for direction in range(3):
        for i, j, k in lines(direction):
            total = values[i] + values[k]
            odd = OFFSET * (values[i] - values[k])
            even = SIDE * total
            values[i], values[k] = even + odd, even - odd
            values[j] = values[j] + MIDDLE * total
    return values


def lane_of(shape):
    return lax.broadcasted_iota(jnp.int32, shape, len(shape) - 1)


def assemble_z(values, wall):
    values = list(values)
    lane = lane_of(values[0].shape)
    first, last = lane == 0, lane == 127
    for i, _, k in lines(2):
        total = values[i] + jnp.where(first, 0.0, pltpu.roll(values[k], 1, 1))
        top = values[k]
        if wall:
            total = jnp.where(first, 0.0, total)
            top = jnp.zeros_like(top)
        values[i] = total
        values[k] = jnp.where(last, top, pltpu.roll(total, 127, 1))
    return values


def assemble_y(values):
    values = list(values)
    for i, _, k in lines(1):
        values[i] = values[i] + pltpu.roll(values[k], 1, 0)
        values[k] = pltpu.roll(values[i], 7, 0)
    return values


def is_even():
    return lax.axis_index("slab") % 2 == 0


def put(near, far, slot, left, right, even):
    near[slot] = jnp.where(even, right, left).astype(BF16)
    far[slot] = jnp.where(even, left, right).astype(BF16)


def get(near, far, slot, even):
    one, other = near[slot].astype(F32), far[slot].astype(F32)
    return jnp.where(even, other, one), jnp.where(even, one, other)


def force_kernel(
    geometry_in, density_in, energy_in, material_in, mass_weight_in,
    field, near, far,
    geometry, density, energy, material, mass_weight, sems,
):
    small = [
        pltpu.make_async_copy(source, target, sems.at[3 + i])
        for i, (source, target) in enumerate(
            [(density_in, density), (energy_in, energy), (material_in, material), (mass_weight_in, mass_weight)]
        )
    ]
    parts = [
        pltpu.make_async_copy(
            geometry_in.at[pl.ds(216 * comp, 216)], geometry.at[pl.ds(216 * comp, 216)], sems.at[comp]
        )
        for comp in range(3)
    ]
    for copy in small + parts:
        copy.start()
    for copy in small:
        copy.wait()
    gamma = jnp.where(material[...] == 0, 2.0 / 3.0, 0.4).astype(F32)
    pressure = (gamma[None] * density[...] * energy[...]).astype(BF16).astype(F32)
    gravity = from_points([mass_weight[q] * POINT_WEIGHT[q] for q in range(27)])
    even = is_even()
    for comp in range(3):
        parts[comp].wait()
        values = []
        for n in range(27):
            r = 27 * comp + n
            block = geometry[pl.ds(8 * r, 8)].astype(F32)
            value = -jnp.sum(block * pressure, axis=0)
            if comp == 2:
                value = value - GRAVITY * gravity[n]
            field[r] = value
            values.append(value)
        for n in range(9):
            put(near, far, 9 * comp + n, values[n], values[18 + n], even)


def spread_kernel(velocity, out):
    rows = velocity[...].astype(BF16).reshape(48, velocity.shape[3])
    low = rows[:, :256]
    high = rows[:, 256:257].astype(F32)
    node = lax.broadcasted_iota(jnp.int32, (256, 384), 0)
    lane = lax.broadcasted_iota(jnp.int32, (256, 384), 1)
    pick = (node == 2 * (lane % 128) + lane // 128).astype(F32).astype(BF16)
    spread = jnp.dot(low, pick, preferred_element_type=F32)
    top = jnp.where(lane_of((48, 128)) == 127, high, 0.0)
    spread = jnp.concatenate([spread[:, :256], spread[:, 256:] + top], axis=1)
    row = lax.broadcasted_iota(jnp.int32, (96, 48), 0)
    source = lax.broadcasted_iota(jnp.int32, (96, 48), 1)
    wanted = (row // 16) * 8 + 2 * (row % 8) + (row // 8) % 2
    move = ((source == wanted) & (row % 8 < OWN)).astype(F32).astype(BF16)
    moved = jnp.dot(move, spread.astype(BF16), preferred_element_type=F32)
    for group in range(12):
        for c in range(3):
            out[3 * group + c] = moved[8 * group : 8 * group + 8, 128 * c : 128 * c + 128]


def rim_kernel(field, near, far, mass_weight, spread, out, to_low, to_high):
    even = is_even()
    for comp in range(3):
        values = [field[27 * comp + n] for n in range(27)]
        for n in range(9):
            left, right = get(near, far, 9 * comp + n, even)
            values[n] = values[n] + left
            values[18 + n] = values[18 + n] + right
        for n in range(27):
            r = 27 * comp + n
            out[r] = values[n]
            to_low[r] = values[n][:HALO].astype(BF16)
            to_high[r] = values[n][OWN - HALO :].astype(BF16)
    for q in range(27):
        to_low[81 + q] = mass_weight[q, :HALO].astype(BF16)
        to_high[81 + q] = mass_weight[q, OWN - HALO :].astype(BF16)
    for comp in range(3):
        for a in range(2):
            for c in range(3):
                to_low[108 + 6 * comp + 3 * a + c] = spread[12 * comp + 6 * a + c, :HALO].astype(BF16)


def send_planes(values, comp, near, far, even):
    for b in range(2):
        for c in range(3):
            n = 3 * b + c
            put(near, far, 6 * comp + n, values[n], values[18 + n], even)


def apply_mass(values, weight, wall):
    points = to_points(values)
    points = [points[q] * weight[q] for q in range(27)]
    return assemble_y(assemble_z(from_points(points), wall))


def first_kernel(
    own, from_low, from_high, mass_weight, spread, field, weight, image, near, far, speeds, rows
):
    even = is_even()
    for q in range(27):
        rows[q, :HALO] = from_low[81 + q].astype(F32)
        rows[q, HALO : HALO + OWN] = mass_weight[q]
        rows[q, HALO + OWN :] = from_high[81 + q].astype(F32)
    for q in range(27):
        weight[q] = rows[q] * POINT_WEIGHT[q]
    for r in range(81):
        rows[r, :HALO] = from_low[r].astype(F32)
        rows[r, HALO : HALO + OWN] = own[r]
        rows[r, HALO + OWN :] = from_high[r].astype(F32)
    for comp in range(3):
        values = [rows[27 * comp + n] for n in range(27)]
        values = assemble_y(assemble_z(values, comp == 2))
        for n in range(27):
            field[27 * comp + n] = values[n]
        values = apply_mass(values, weight, comp == 2)
        for n in range(27):
            image[27 * comp + n] = values[n]
        send_planes(values, comp, near, far, even)
    row = lax.broadcasted_iota(jnp.int32, (8, 128), 0)
    plane = []
    for comp in range(3):
        for a in range(2):
            speed = [spread[12 * comp + 6 * a + n] for n in range(6)]
            for c in range(3):
                beyond = from_high[108 + 6 * comp + 3 * a + c].astype(F32)[0:1]
                speed.append(jnp.where(row == OWN - 1, beyond, pltpu.roll(speed[c], 7, 0)))
            for n in range(9):
                speeds[18 * comp + 9 * a + n] = speed[n]
            if a == 0:
                plane += speed
    for n in range(0, 27, 2):
        upper = plane[n] if n == 26 else pltpu.roll(plane[n + 1], 4, 0)
        both = jnp.where(row < OWN, plane[n], upper).astype(BF16)
        near[18 + n // 2] = both
        far[18 + n // 2] = both


def take_planes(image, near, far, comp, even):
    values = [image[27 * comp + n] for n in range(27)]
    for b in range(2):
        for c in range(3):
            n = 3 * b + c
            left, right = get(near, far, 6 * comp + n, even)
            values[n] = values[n] + left
            values[18 + n] = values[18 + n] + right
    for a in (0, 18):
        for c in range(3):
            values[a + 6 + c] = pltpu.roll(values[a + c], 7, 0)
    return values


def second_kernel(image, near_in, far_in, weight, field, image_out, near, far):
    even = is_even()
    for comp in range(3):
        values = take_planes(image, near_in, far_in, comp, even)
        for n in range(27):
            field[27 * comp + n] = values[n]
        values = apply_mass(values, weight, comp == 2)
        for n in range(27):
            image_out[27 * comp + n] = values[n]
        send_planes(values, comp, near, far, even)


def work_kernel(geometry, density, energy, material, energy_mass, speeds, near, far, out):
    even = is_even()
    gamma = jnp.where(material[...] == 0, 2.0 / 3.0, 0.4).astype(F32)
    pressure = (gamma[None] * density[...] * energy[...]).astype(BF16).astype(F32)
    work = jnp.zeros_like(pressure)
    for comp in range(3):
        for n in range(27):
            if n < 18:
                speed = speeds[18 * comp + n, :OWN]
            else:
                k = 9 * comp + n - 18
                _, speed = get(near, far, 18 + k // 2, even)
                speed = speed[OWN * (k % 2) : OWN * (k % 2) + OWN]
            work = work + geometry[pl.ds(8 * (27 * comp + n), 8)].astype(F32) * speed[None]
    out[...] = energy[...] + HALF_STEP * pressure * work / energy_mass[...]


def dot_owned(first, second, comp, total):
    last = lane_of((8, 128)) == 127
    for a in range(2):
        for b in range(2):
            n = 27 * comp + 9 * a + 3 * b
            total = total + first[n] * second[n] + first[n + 1] * second[n + 1]
            total = total + jnp.where(last, first[n + 2] * second[n + 2], 0.0)
    return total


def product_kernel(zeroth, first, products):
    for k, (one, other) in enumerate([(zeroth, zeroth), (zeroth, first), (first, first)]):
        total = jnp.zeros((8, 128), F32)
        for comp in range(3):
            total = dot_owned(one, other, comp, total)
        products[k] = total


def moment_kernel(image, near, far, weight, first, products, second, moments):
    zero = jnp.zeros((8, 128), F32)
    cross, norm = zero, zero
    quadratic = [zero] * 3
    even = is_even()
    for comp in range(3):
        values = take_planes(image, near, far, comp, even)
        for n in range(27):
            second[27 * comp + n] = values[n]
        values_at = {27 * comp + n: values[n] for n in range(27)}
        cross = dot_owned(first, values_at, comp, cross)
        norm = dot_owned(values_at, values_at, comp, norm)
        points = to_points(values)
        for q in range(27):
            quadratic[q % 3] = quadratic[q % 3] + points[q] * points[q] * weight[q]
    quadratic = quadratic[0] + quadratic[1] + quadratic[2]
    row = lax.broadcasted_iota(jnp.int32, (8, 128), 0)
    mine = (row >= HALO) & (row < HALO + OWN)
    sums = jnp.zeros((8, 128), F32)
    for k, total in enumerate([products[0], products[1], products[2], cross, norm, quadratic]):
        total = jnp.sum(jnp.where(mine, total, 0.0), axis=0, keepdims=True)
        sums = jnp.where(row == k, total, sums)
    sums = jnp.sum(sums, axis=1, keepdims=True)
    line = jnp.sum(jnp.where(lane_of((8, 128)) == row, sums, 0.0), axis=0, keepdims=True)
    moments[...] = jnp.broadcast_to(line, moments.shape)


def solve(moments):
    def ratio(top, pivot, scale):
        good = pivot > 1e-7 * scale
        return jnp.where(good, top / jnp.where(good, pivot, 1.0), 0.0)

    m = moments
    l10 = ratio(m[2], m[1], 0.0)
    l20 = ratio(m[3], m[1], 0.0)
    d1 = m[3] - l10 * m[2]
    e1 = m[4] - l20 * m[2]
    l21 = ratio(e1, d1, m[3])
    d2 = m[5] - l20 * m[3] - l21 * e1
    y1 = m[1] - l10 * m[0]
    y2 = m[2] - l20 * m[0] - l21 * y1
    c2 = ratio(y2, d2, m[5])
    c1 = ratio(y1, d1, m[3]) - l21 * c2
    c0 = ratio(m[0], m[1], 0.0) - l10 * c1 - l20 * c2
    return c0, c1, c2


def halves(x):
    high = x.astype(BF16)
    return high, (x - high.astype(F32)).astype(BF16)


def nodal_kernel(zeroth, first, second, out):
    row = lax.broadcasted_iota(jnp.int32, (48, 96), 0)
    source = lax.broadcasted_iota(jnp.int32, (48, 96), 1)
    wanted = (row // 8) * 16 + (row % 2) * 8 + HALO + (row % 8) // 2
    move = (source == wanted).astype(F32).astype(BF16)
    source = lax.broadcasted_iota(jnp.int32, (384, 384), 0)
    node = lax.broadcasted_iota(jnp.int32, (384, 384), 1)
    wanted = jnp.where(node < 256, (node % 2) * 128 + node // 2, 383)
    place = ((source == wanted) & (node <= 256)).astype(F32).astype(BF16)
    for k, field in enumerate((zeroth, first, second)):
        blocks = []
        for c in range(3):
            column = []
            for comp in range(3):
                for a in range(2):
                    for b in range(2):
                        column.append(field[27 * comp + 9 * a + 3 * b + c])
            blocks.append(jnp.concatenate(column, axis=0))
        high, low = halves(jnp.concatenate(blocks, axis=1))
        moved = jnp.dot(move, high, preferred_element_type=F32) + jnp.dot(move, low, preferred_element_type=F32)
        high, low = halves(moved)
        out[k] = jnp.dot(high, place, preferred_element_type=F32) + jnp.dot(low, place, preferred_element_type=F32)


def last_kernel(moments, nodal, velocity, out):
    line = jnp.sum(moments[...], axis=0, keepdims=True)
    lane = lane_of((1, 128))
    mu = [jnp.sum(jnp.where(lane == k, line, 0.0), axis=1, keepdims=True) for k in range(6)]
    c0, c1, c2 = [HALF_STEP * c for c in solve(mu)]
    for comp in range(3):
        for x in range(2):
            start = 16 * comp + 8 * x
            part = [nodal[k, pl.ds(start, 8), : velocity.shape[3]] for k in range(3)]
            out[comp, x] = velocity[comp, x] + (c0 * part[0] + c1 * part[1] + c2 * part[2])


VMEM = pl.BlockSpec(memory_space=pltpu.VMEM)


def call(kernel, outs, *args, scratch=(), flops=100000, place=VMEM, dtypes=None):
    shapes = [jax.ShapeDtypeStruct(shape, dtype) for shape, dtype in zip(outs, dtypes or [F32] * len(outs))]
    moved = sum(a.size * a.dtype.itemsize for a in args) + sum(4 * int(np.prod(s)) for s in outs)
    return pl.pallas_call(
        kernel,
        out_shape=shapes,
        in_specs=[place] * len(args),
        out_specs=[VMEM] * len(outs),
        scratch_shapes=list(scratch),
        compiler_params=pltpu.CompilerParams(vmem_limit_bytes=32 * 1024 * 1024),
        cost_estimate=pl.CostEstimate(flops=flops, bytes_accessed=moved, transcendentals=0),
        name=kernel.__name__,
    )(*args)


def shift(x, axis, by):
    count = lax.axis_size(axis)
    return lax.ppermute(x, axis, [(i, (i + by) % count) for i in range(count)])


def swap(near, far):
    count = lax.axis_size("slab")
    far = lax.ppermute(far, "slab", [(i, (i + (1 if i % 2 else -1)) % count) for i in range(count)])
    near = lax.ppermute(near, "slab", [(i, i + (-1 if i % 2 else 1)) for i in range(count)])
    return near, far


def local(velocity, energy, density, material, geometry, mass_weight, energy_mass):
    tile = (4, 128)
    geometry = geometry.reshape((648,) + tile)
    density = density.reshape((8,) + tile)
    energy = energy.reshape((8,) + tile)
    energy_mass = energy_mass.reshape((8,) + tile)
    mass_weight = mass_weight.reshape((27,) + tile)
    material = material.reshape(tile)
    full = (8, 128)
    pair = (2, 128)
    devices = lax.axis_size("slab") * lax.axis_size("brick")

    force, near, far = call(
        force_kernel,
        [(81,) + tile, (27,) + tile, (27,) + tile],
        *[pltpu.with_memory_space_constraint(x, pltpu.HBM) for x in (geometry, density, energy, material, mass_weight)],
        scratch=[
            pltpu.VMEM((648,) + tile, BF16),
            pltpu.VMEM((8,) + tile, F32),
            pltpu.VMEM((8,) + tile, F32),
            pltpu.VMEM(tile, jnp.int32),
            pltpu.VMEM((27,) + tile, F32),
            pltpu.SemaphoreType.DMA((7,)),
        ],
        place=pl.BlockSpec(memory_space=pltpu.HBM),
        dtypes=[F32, BF16, BF16],
    )
    (spread,) = call(spread_kernel, [(36,) + full], velocity)
    near, far = swap(near, far)
    own, to_low, to_high = call(
        rim_kernel,
        [(81,) + tile, (126,) + pair, (108,) + pair],
        force, near, far, mass_weight, spread,
        dtypes=[F32, BF16, BF16],
    )
    from_high = shift(to_low, "brick", -1)
    from_low = shift(to_high, "brick", 1)
    zeroth, weight, image, near, far, speeds = call(
        first_kernel,
        [(81,) + full, (27,) + full, (81,) + full, (32,) + full, (32,) + full, (54,) + full],
        own, from_low, from_high, mass_weight, spread,
        scratch=[pltpu.VMEM((81,) + full, F32)],
        dtypes=[F32, F32, F32, BF16, BF16, F32],
    )
    near, far = swap(near, far)
    first, image, near_out, far_out = call(
        second_kernel,
        [(81,) + full, (81,) + full, (18,) + full, (18,) + full],
        image, near, far, weight,
        dtypes=[F32, F32, BF16, BF16],
    )
    (energy_half,) = call(
        work_kernel, [(8,) + tile], geometry, density, energy, material, energy_mass, speeds, near, far
    )
    near, far = swap(near_out, far_out)
    (products,) = call(product_kernel, [(3,) + full], zeroth, first)
    second, moments = call(
        moment_kernel, [(81,) + full, (devices, 128)], image, near, far, weight, first, products
    )
    moments = pltpu.with_memory_space_constraint(moments, pltpu.VMEM)
    moments = lax.all_to_all(moments, ("slab", "brick"), 0, 0, tiled=True)
    (nodal,) = call(nodal_kernel, [(3, 48, 384)], zeroth, first, second)
    (velocity_half,) = call(last_kernel, [velocity.shape], moments, nodal, velocity)
    return (velocity_half, energy_half.reshape(8, 1, 4, 128))


def solution(mesh):
    nodes = P(None, "slab", "brick", None)
    return jax.shard_map(
        local,
        mesh=mesh,
        in_specs=(
            nodes,
            nodes,
            nodes,
            P("slab", "brick", None),
            P(None, None, "slab", "brick", None),
            nodes,
            nodes,
        ),
        out_specs=(nodes, nodes),
        check_vma=False,
    )
```

```python
import jax
import jax.numpy as jnp
import numpy as np
from jax import lax
from jax.experimental import pallas as pl
from jax.experimental.pallas import tpu as pltpu
from jax.sharding import PartitionSpec as P

HALF_STEP = 0.25
GRAVITY = 1.0
F32 = jnp.float32
BF16 = jnp.bfloat16

OFFSET = float(np.sqrt(0.6) / 2.0)
SIDE = 0.3
MIDDLE = 0.4
LINE_WEIGHTS = (5.0 / 18.0, 8.0 / 18.0, 5.0 / 18.0)
POINT_WEIGHT = [a * b * c for a in LINE_WEIGHTS for b in LINE_WEIGHTS for c in LINE_WEIGHTS]
OWN = 4
HALO = 2


def lines(direction):
    stride = (9, 3, 1)[direction]
    return [(n, n + stride, n + 2 * stride) for n in range(27) if (n // stride) % 3 == 0]


def to_points(values):
    values = list(values)
    for direction in range(3):
        for i, j, k in lines(direction):
            even = SIDE * (values[i] + values[k]) + MIDDLE * values[j]
            odd = OFFSET * (values[i] - values[k])
            values[i], values[k] = even + odd, even - odd
    return values


def from_points(values):
    values = list(values)
    for direction in range(3):
        for i, j, k in lines(direction):
            total = values[i] + values[k]
            odd = OFFSET * (values[i] - values[k])
            even = SIDE * total
            values[i], values[k] = even + odd, even - odd
            values[j] = values[j] + MIDDLE * total
    return values


def lane_of(shape):
    return lax.broadcasted_iota(jnp.int32, shape, len(shape) - 1)


def assemble_z(values, wall):
    values = list(values)
    lane = lane_of(values[0].shape)
    first, last = lane == 0, lane == 127
    for i, _, k in lines(2):
        total = values[i] + jnp.where(first, 0.0, pltpu.roll(values[k], 1, 1))
        top = values[k]
        if wall:
            total = jnp.where(first, 0.0, total)
            top = jnp.zeros_like(top)
        values[i] = total
        values[k] = jnp.where(last, top, pltpu.roll(total, 127, 1))
    return values


def assemble_y(values):
    values = list(values)
    for i, _, k in lines(1):
        values[i] = values[i] + pltpu.roll(values[k], 1, 0)
        values[k] = pltpu.roll(values[i], 7, 0)
    return values


def is_even(axis="slab"):
    return lax.axis_index(axis) % 2 == 0


def put(near, far, slot, left, right, even):
    near[slot] = jnp.where(even, right, left).astype(BF16)
    far[slot] = jnp.where(even, left, right).astype(BF16)


def get(near, far, slot, even):
    one, other = near[slot].astype(F32), far[slot].astype(F32)
    return jnp.where(even, other, one), jnp.where(even, one, other)


def pressure_of(density, energy, material):
    gamma = jnp.where(material[...] == 0, 2.0 / 3.0, 0.4).astype(F32)
    gamma = jnp.concatenate([gamma, gamma], axis=0)
    return (gamma[None] * density[...] * energy[...]).astype(BF16).astype(F32)


def force_kernel(
    geometry_in, density_in, energy_in, material_in, mass_weight_in,
    field, near, far,
    geometry, density, energy, material, mass_weight, sems,
):
    small = [
        pltpu.make_async_copy(source, target, sems.at[3 + i])
        for i, (source, target) in enumerate(
            [(density_in, density), (energy_in, energy), (material_in, material), (mass_weight_in, mass_weight)]
        )
    ]
    parts = [
        pltpu.make_async_copy(
            geometry_in.at[pl.ds(108 * comp, 108)], geometry.at[pl.ds(108 * comp, 108)], sems.at[comp]
        )
        for comp in range(3)
    ]
    for copy in small + parts:
        copy.start()
    for copy in small:
        copy.wait()
    pressure = pressure_of(density, energy, material)
    gravity = from_points([mass_weight[q] * POINT_WEIGHT[q] for q in range(27)])
    even = is_even()
    for comp in range(3):
        parts[comp].wait()
        values = []
        for n in range(27):
            r = 27 * comp + n
            value = jnp.sum(geometry[pl.ds(4 * r, 4)].astype(F32) * pressure, axis=0)
            value = -(value + pltpu.roll(value, OWN, 0))[:OWN]
            if comp == 2:
                value = value - GRAVITY * gravity[n]
            field[r] = value
            values.append(value)
        for n in range(9):
            put(near, far, 9 * comp + n, values[n], values[18 + n], even)


def spread_kernel(velocity, out):
    rows = velocity[...].astype(BF16).reshape(48, velocity.shape[3])
    low = rows[:, :256]
    high = rows[:, 256:257].astype(F32)
    node = lax.broadcasted_iota(jnp.int32, (256, 384), 0)
    lane = lax.broadcasted_iota(jnp.int32, (256, 384), 1)
    pick = (node == 2 * (lane % 128) + lane // 128).astype(F32).astype(BF16)
    spread = jnp.dot(low, pick, preferred_element_type=F32)
    top = jnp.where(lane_of((48, 128)) == 127, high, 0.0)
    spread = jnp.concatenate([spread[:, :256], spread[:, 256:] + top], axis=1)
    row = lax.broadcasted_iota(jnp.int32, (96, 48), 0)
    source = lax.broadcasted_iota(jnp.int32, (96, 48), 1)
    wanted = (row // 16) * 8 + 2 * (row % 8) + (row // 8) % 2
    move = ((source == wanted) & (row % 8 < OWN)).astype(F32).astype(BF16)
    moved = jnp.dot(move, spread.astype(BF16), preferred_element_type=F32)
    for group in range(12):
        for c in range(3):
            out[3 * group + c] = moved[8 * group : 8 * group + 8, 128 * c : 128 * c + 128]


def rim_kernel(field, far, near, mass_weight, spread, out, near_out, far_out):
    even = is_even()
    even_y = is_even("brick")
    for comp in range(3):
        values = [field[27 * comp + n] for n in range(27)]
        for n in range(9):
            left, right = get(near, far, 9 * comp + n, even)
            values[n] = values[n] + left
            values[18 + n] = values[18 + n] + right
        for n in range(27):
            r = 27 * comp + n
            out[r] = values[n]
            put(near_out, far_out, r, values[n][:HALO], values[n][OWN - HALO :], even_y)
    for q in range(27):
        put(near_out, far_out, 81 + q, mass_weight[q, :HALO], mass_weight[q, OWN - HALO :], even_y)
    row = lax.broadcasted_iota(jnp.int32, (8, 128), 0)
    for slot in range(9):
        first, second = [spread[12 * (k // 6) + 6 * (k // 3 % 2) + k % 3] for k in (2 * slot, 2 * slot + 1)]
        both = jnp.where(row == 0, first, pltpu.roll(second, 1, 0))[:HALO].astype(BF16)
        near_out[108 + slot] = both
        far_out[108 + slot] = both


def send_planes(values, comp, near, far, even):
    for b in range(2):
        for c in range(3):
            n = 3 * b + c
            put(near, far, 6 * comp + n, values[n], values[18 + n], even)


def apply_mass(values, weight, wall):
    points = to_points(values)
    points = [points[q] * weight[q] for q in range(27)]
    return assemble_y(assemble_z(from_points(points), wall))


def first_kernel(
    own, far_in, near_in, mass_weight, spread, field, weight, image, near, far, speeds, rows
):
    even = is_even()
    even_y = is_even("brick")
    for r in range(108):
        low, high = get(near_in, far_in, r, even_y)
        rows[r, :HALO] = low
        rows[r, HALO : HALO + OWN] = own[r] if r < 81 else mass_weight[r - 81]
        rows[r, HALO + OWN :] = high
    for q in range(27):
        weight[q] = rows[81 + q] * POINT_WEIGHT[q]
    for comp in range(3):
        values = [rows[27 * comp + n] for n in range(27)]
        values = assemble_y(assemble_z(values, comp == 2))
        for n in range(27):
            field[27 * comp + n] = values[n]
        values = apply_mass(values, weight, comp == 2)
        for n in range(27):
            image[27 * comp + n] = values[n]
        send_planes(values, comp, near, far, even)
    row = lax.broadcasted_iota(jnp.int32, (8, 128), 0)
    plane = []
    for comp in range(3):
        for a in range(2):
            speed = [spread[12 * comp + 6 * a + n] for n in range(6)]
            for c in range(3):
                k = 6 * comp + 3 * a + c
                beyond = get(near_in, far_in, 108 + k // 2, even_y)[1][k % 2 : k % 2 + 1]
                speed.append(jnp.where(row == OWN - 1, beyond, pltpu.roll(speed[c], 7, 0)))
            for n in range(9):
                speeds[18 * comp + 9 * a + n] = speed[n]
            if a == 0:
                plane += speed
    for n in range(0, 27, 2):
        upper = plane[n] if n == 26 else pltpu.roll(plane[n + 1], 4, 0)
        both = jnp.where(row < OWN, plane[n], upper).astype(BF16)
        near[18 + n // 2] = both
        far[18 + n // 2] = both


def take_planes(image, near, far, comp, even):
    values = [image[27 * comp + n] for n in range(27)]
    for b in range(2):
        for c in range(3):
            n = 3 * b + c
            left, right = get(near, far, 6 * comp + n, even)
            values[n] = values[n] + left
            values[18 + n] = values[18 + n] + right
    for a in (0, 18):
        for c in range(3):
            values[a + 6 + c] = pltpu.roll(values[a + c], 7, 0)
    return values


def second_kernel(image, far_in, near_in, weight, field, image_out, near, far):
    even = is_even()
    for comp in range(3):
        values = take_planes(image, near_in, far_in, comp, even)
        for n in range(27):
            field[27 * comp + n] = values[n]
        values = apply_mass(values, weight, comp == 2)
        for n in range(27):
            image_out[27 * comp + n] = values[n]
        send_planes(values, comp, near, far, even)


def work_kernel(geometry, density, energy, material, energy_mass, speeds, far, near, out):
    even = is_even()
    pressure = pressure_of(density, energy, material)
    work = jnp.zeros_like(pressure)
    upper = lax.broadcasted_iota(jnp.int32, (8, 128), 0) >= OWN
    for comp in range(3):
        for n in range(27):
            if n < 18:
                speed, odd = speeds[18 * comp + n], False
            else:
                k = 9 * comp + n - 18
                speed, odd = get(near, far, 18 + k // 2, even)[1], k % 2 == 1
            speed = jnp.where(upper == odd, speed, pltpu.roll(speed, OWN, 0))
            work = work + geometry[pl.ds(4 * (27 * comp + n), 4)].astype(F32) * speed[None]
    out[...] = energy[...] + HALF_STEP * pressure * work / energy_mass[...]


def dot_owned(first, second, comp, total):
    last = lane_of((8, 128)) == 127
    for a in range(2):
        for b in range(2):
            n = 27 * comp + 9 * a + 3 * b
            total = total + first[n] * second[n] + first[n + 1] * second[n + 1]
            total = total + jnp.where(last, first[n + 2] * second[n + 2], 0.0)
    return total


def product_kernel(zeroth, first, products):
    for k, (one, other) in enumerate([(zeroth, zeroth), (zeroth, first), (first, first)]):
        total = jnp.zeros((8, 128), F32)
        for comp in range(3):
            total = dot_owned(one, other, comp, total)
        products[k] = total


def moment_kernel(image, far, near, weight, first, products, second, moments):
    zero = jnp.zeros((8, 128), F32)
    cross, norm = zero, zero
    quadratic = [zero] * 3
    even = is_even()
    for comp in range(3):
        values = take_planes(image, near, far, comp, even)
        for n in range(27):
            second[27 * comp + n] = values[n]
        values_at = {27 * comp + n: values[n] for n in range(27)}
        cross = dot_owned(first, values_at, comp, cross)
        norm = dot_owned(values_at, values_at, comp, norm)
        points = to_points(values)
        for q in range(27):
            quadratic[q % 3] = quadratic[q % 3] + points[q] * points[q] * weight[q]
    quadratic = quadratic[0] + quadratic[1] + quadratic[2]
    row = lax.broadcasted_iota(jnp.int32, (8, 128), 0)
    mine = (row >= HALO) & (row < HALO + OWN)
    sums = jnp.zeros((8, 128), F32)
    for k, total in enumerate([products[0], products[1], products[2], cross, norm, quadratic]):
        total = jnp.sum(jnp.where(mine, total, 0.0), axis=0, keepdims=True)
        sums = jnp.where(row == k, total, sums)
    sums = jnp.sum(sums, axis=1, keepdims=True)
    line = jnp.sum(jnp.where(lane_of((8, 128)) == row, sums, 0.0), axis=0, keepdims=True)
    moments[...] = jnp.broadcast_to(line, moments.shape)


def solve(moments):
    def ratio(top, pivot, scale):
        good = pivot > 1e-7 * scale
        return jnp.where(good, top / jnp.where(good, pivot, 1.0), 0.0)

    m = moments
    l10 = ratio(m[2], m[1], 0.0)
    l20 = ratio(m[3], m[1], 0.0)
    d1 = m[3] - l10 * m[2]
    e1 = m[4] - l20 * m[2]
    l21 = ratio(e1, d1, m[3])
    d2 = m[5] - l20 * m[3] - l21 * e1
    y1 = m[1] - l10 * m[0]
    y2 = m[2] - l20 * m[0] - l21 * y1
    c2 = ratio(y2, d2, m[5])
    c1 = ratio(y1, d1, m[3]) - l21 * c2
    c0 = ratio(m[0], m[1], 0.0) - l10 * c1 - l20 * c2
    return c0, c1, c2


def halves(x):
    high = x.astype(BF16)
    return high, (x - high.astype(F32)).astype(BF16)


def nodal_kernel(zeroth, first, second, out):
    row = lax.broadcasted_iota(jnp.int32, (48, 96), 0)
    source = lax.broadcasted_iota(jnp.int32, (48, 96), 1)
    wanted = (row // 8) * 16 + (row % 2) * 8 + HALO + (row % 8) // 2
    move = (source == wanted).astype(F32).astype(BF16)
    source = lax.broadcasted_iota(jnp.int32, (384, 384), 0)
    node = lax.broadcasted_iota(jnp.int32, (384, 384), 1)
    wanted = jnp.where(node < 256, (node % 2) * 128 + node // 2, 383)
    place = ((source == wanted) & (node <= 256)).astype(F32).astype(BF16)
    for k, field in enumerate((zeroth, first, second)):
        blocks = []
        for c in range(3):
            column = []
            for comp in range(3):
                for a in range(2):
                    for b in range(2):
                        column.append(field[27 * comp + 9 * a + 3 * b + c])
            blocks.append(jnp.concatenate(column, axis=0))
        high, low = halves(jnp.concatenate(blocks, axis=1))
        moved = jnp.dot(move, high, preferred_element_type=F32) + jnp.dot(move, low, preferred_element_type=F32)
        high, low = halves(moved)
        out[k] = jnp.dot(high, place, preferred_element_type=F32) + jnp.dot(low, place, preferred_element_type=F32)


def last_kernel(moments, nodal, velocity, out):
    line = jnp.sum(moments[...], axis=0, keepdims=True)
    lane = lane_of((1, 128))
    mu = [jnp.sum(jnp.where(lane == k, line, 0.0), axis=1, keepdims=True) for k in range(6)]
    c0, c1, c2 = [HALF_STEP * c for c in solve(mu)]
    for comp in range(3):
        for x in range(2):
            start = 16 * comp + 8 * x
            part = [nodal[k, pl.ds(start, 8), : velocity.shape[3]] for k in range(3)]
            out[comp, x] = velocity[comp, x] + (c0 * part[0] + c1 * part[1] + c2 * part[2])


VMEM = pl.BlockSpec(memory_space=pltpu.VMEM)


def call(kernel, outs, *args, scratch=(), flops=100000, place=VMEM, dtypes=None):
    shapes = [jax.ShapeDtypeStruct(shape, dtype) for shape, dtype in zip(outs, dtypes or [F32] * len(outs))]
    moved = sum(a.size * a.dtype.itemsize for a in args) + sum(4 * int(np.prod(s)) for s in outs)
    return pl.pallas_call(
        kernel,
        out_shape=shapes,
        in_specs=[place] * len(args),
        out_specs=[VMEM] * len(outs),
        scratch_shapes=list(scratch),
        compiler_params=pltpu.CompilerParams(vmem_limit_bytes=32 * 1024 * 1024),
        cost_estimate=pl.CostEstimate(flops=flops, bytes_accessed=moved, transcendentals=0),
        name=kernel.__name__,
    )(*args)


def swap(near, far, axis="slab"):
    count = lax.axis_size(axis)
    far = lax.ppermute(far, axis, [(i, (i + (1 if i % 2 else -1)) % count) for i in range(count)])
    near = lax.ppermute(near, axis, [(i, i + (-1 if i % 2 else 1)) for i in range(count)])
    return near, far


def local(velocity, energy, density, material, geometry, mass_weight, energy_mass):
    tile = (4, 128)
    full = (8, 128)
    geometry = geometry.reshape((324,) + full)
    density = density.reshape((4,) + full)
    energy = energy.reshape((4,) + full)
    energy_mass = energy_mass.reshape((4,) + full)
    mass_weight = mass_weight.reshape((27,) + tile)
    material = material.reshape(tile)
    pair = (2, 128)
    devices = lax.axis_size("slab") * lax.axis_size("brick")

    force, near, far = call(
        force_kernel,
        [(81,) + tile, (27,) + tile, (27,) + tile],
        *[pltpu.with_memory_space_constraint(x, pltpu.HBM) for x in (geometry, density, energy, material, mass_weight)],
        scratch=[
            pltpu.VMEM((324,) + full, BF16),
            pltpu.VMEM((4,) + full, F32),
            pltpu.VMEM((4,) + full, F32),
            pltpu.VMEM(tile, jnp.int32),
            pltpu.VMEM((27,) + tile, F32),
            pltpu.SemaphoreType.DMA((7,)),
        ],
        place=pl.BlockSpec(memory_space=pltpu.HBM),
        dtypes=[F32, BF16, BF16],
    )
    (spread,) = call(spread_kernel, [(36,) + full], velocity)
    near, far = swap(near, far)
    own, near, far = call(
        rim_kernel,
        [(81,) + tile, (117,) + pair, (117,) + pair],
        force, far, near, mass_weight, spread,
        dtypes=[F32, BF16, BF16],
    )
    near, far = swap(near, far, "brick")
    zeroth, weight, image, near, far, speeds = call(
        first_kernel,
        [(81,) + full, (27,) + full, (81,) + full, (32,) + full, (32,) + full, (54,) + full],
        own, far, near, mass_weight, spread,
        scratch=[pltpu.VMEM((108,) + full, F32)],
        dtypes=[F32, F32, F32, BF16, BF16, F32],
    )
    near, far = swap(near, far)
    first, image, near_out, far_out = call(
        second_kernel,
        [(81,) + full, (81,) + full, (18,) + full, (18,) + full],
        image, far, near, weight,
        dtypes=[F32, F32, BF16, BF16],
    )
    (energy_half,) = call(
        work_kernel, [(4,) + full], geometry, density, energy, material, energy_mass, speeds, far, near
    )
    near, far = swap(near_out, far_out)
    (products,) = call(product_kernel, [(3,) + full], zeroth, first)
    second, moments = call(
        moment_kernel, [(81,) + full, (devices, 128)], image, far, near, weight, first, products
    )
    moments = pltpu.with_memory_space_constraint(moments, pltpu.VMEM)
    moments = lax.all_to_all(moments, ("slab", "brick"), 0, 0, tiled=True)
    (nodal,) = call(nodal_kernel, [(3, 48, 384)], zeroth, first, second)
    (velocity_half,) = call(last_kernel, [velocity.shape], moments, nodal, velocity)
    return (velocity_half, energy_half.reshape(8, 1, 4, 128))


def solution(mesh):
    nodes = P(None, "slab", "brick", None)
    return jax.shard_map(
        local,
        mesh=mesh,
        in_specs=(
            nodes,
            nodes,
            nodes,
            P("slab", "brick", None),
            P(None, None, "slab", "brick", None),
            nodes,
            nodes,
        ),
        out_specs=(nodes, nodes),
        check_vma=False,
    )
```

```python
import jax
import jax.numpy as jnp
import numpy as np
from jax import lax
from jax.experimental import pallas as pl
from jax.experimental.pallas import tpu as pltpu
from jax.sharding import PartitionSpec as P

HALF_STEP = 0.25
GRAVITY = 1.0
F32 = jnp.float32
BF16 = jnp.bfloat16

OFFSET = float(np.sqrt(0.6) / 2.0)
SIDE = 0.3
MIDDLE = 0.4
LINE_WEIGHTS = (5.0 / 18.0, 8.0 / 18.0, 5.0 / 18.0)
POINT_WEIGHT = [a * b * c for a in LINE_WEIGHTS for b in LINE_WEIGHTS for c in LINE_WEIGHTS]
OWN = 4
HALO = 2


def lines(direction):
    stride = (9, 3, 1)[direction]
    return [(n, n + stride, n + 2 * stride) for n in range(27) if (n // stride) % 3 == 0]


def to_points(values):
    values = list(values)
    for direction in range(3):
        for i, j, k in lines(direction):
            even = SIDE * (values[i] + values[k]) + MIDDLE * values[j]
            odd = OFFSET * (values[i] - values[k])
            values[i], values[k] = even + odd, even - odd
    return values


def from_points(values):
    values = list(values)
    for direction in range(3):
        for i, j, k in lines(direction):
            total = values[i] + values[k]
            odd = OFFSET * (values[i] - values[k])
            even = SIDE * total
            values[i], values[k] = even + odd, even - odd
            values[j] = values[j] + MIDDLE * total
    return values


def lane_of(shape):
    return lax.broadcasted_iota(jnp.int32, shape, len(shape) - 1)


def assemble_z(values, wall):
    values = list(values)
    lane = lane_of(values[0].shape)
    first, last = lane == 0, lane == 127
    for i, _, k in lines(2):
        total = values[i] + jnp.where(first, 0.0, pltpu.roll(values[k], 1, 1))
        top = values[k]
        if wall:
            total = jnp.where(first, 0.0, total)
            top = jnp.zeros_like(top)
        values[i] = total
        values[k] = jnp.where(last, top, pltpu.roll(total, 127, 1))
    return values


def assemble_y(values):
    values = list(values)
    for i, _, k in lines(1):
        values[i] = values[i] + pltpu.roll(values[k], 1, 0)
        values[k] = pltpu.roll(values[i], 7, 0)
    return values


def is_even(axis="slab"):
    return lax.axis_index(axis) % 2 == 0


def put(near, far, slot, left, right, even):
    near[slot] = jnp.where(even, right, left).astype(BF16)
    far[slot] = jnp.where(even, left, right).astype(BF16)


def get(near, far, slot, even):
    one, other = near[slot].astype(F32), far[slot].astype(F32)
    return jnp.where(even, other, one), jnp.where(even, one, other)


def pressure_of(density, energy, material):
    gamma = jnp.where(material[...] == 0, 2.0 / 3.0, 0.4).astype(F32)
    gamma = jnp.concatenate([gamma, gamma], axis=0)
    return (gamma[None] * density[...] * energy[...]).astype(BF16).astype(F32)


def to_lane(tile, lane, values, slot):
    return jnp.where(lane == slot, pltpu.roll(values, slot + 1, 1), tile)


def third_along_z(values, tops, lane, slot):
    return jnp.where(lane == 127, pltpu.roll(tops, 127 - slot, 1), pltpu.roll(values, 127, 1))


def double(values):
    return jnp.concatenate([values, values], axis=0)


def force_kernel(
    geometry_in, density_in, energy_in, material_in, mass_weight_in,
    field, near, far,
    geometry, density, energy, material, mass_weight, sems,
):
    small = [
        pltpu.make_async_copy(source, target, sems.at[3 + i])
        for i, (source, target) in enumerate(
            [(density_in, density), (energy_in, energy), (material_in, material), (mass_weight_in, mass_weight)]
        )
    ]
    parts = [
        pltpu.make_async_copy(
            geometry_in.at[pl.ds(108 * comp, 108)], geometry.at[pl.ds(108 * comp, 108)], sems.at[comp]
        )
        for comp in range(3)
    ]
    for copy in small + parts:
        copy.start()
    for copy in small:
        copy.wait()
    pressure = pressure_of(density, energy, material)
    gravity = from_points([double(mass_weight[q]) * POINT_WEIGHT[q] for q in range(27)])
    even = is_even()
    for comp in range(3):
        parts[comp].wait()
        values = []
        for n in range(27):
            r = 27 * comp + n
            value = jnp.sum(geometry[pl.ds(4 * r, 4)].astype(F32) * pressure, axis=0)
            value = -(value + pltpu.roll(value, OWN, 0))
            if comp == 2:
                value = value - GRAVITY * gravity[n]
            field[r] = value
            values.append(value)
        for n in range(9):
            put(near, far, 9 * comp + n, values[n][:OWN], values[18 + n][:OWN], even)


def spread_kernel(velocity, out):
    rows = velocity[...].astype(BF16).reshape(48, velocity.shape[3])
    low = rows[:, :256]
    high = rows[:, 256:257].astype(F32)
    node = lax.broadcasted_iota(jnp.int32, (256, 384), 0)
    lane = lax.broadcasted_iota(jnp.int32, (256, 384), 1)
    pick = (node == 2 * (lane % 128) + lane // 128).astype(F32).astype(BF16)
    spread = jnp.dot(low, pick, preferred_element_type=F32)
    top = jnp.where(lane_of((48, 128)) == 127, high, 0.0)
    spread = jnp.concatenate([spread[:, :256], spread[:, 256:] + top], axis=1)
    row = lax.broadcasted_iota(jnp.int32, (96, 48), 0)
    source = lax.broadcasted_iota(jnp.int32, (96, 48), 1)
    wanted = (row // 16) * 8 + 2 * (row % 8) + (row // 8) % 2
    move = ((source == wanted) & (row % 8 < OWN)).astype(F32).astype(BF16)
    moved = jnp.dot(move, spread.astype(BF16), preferred_element_type=F32)
    for group in range(12):
        for c in range(3):
            out[3 * group + c] = moved[8 * group : 8 * group + 8, 128 * c : 128 * c + 128]


TOPS, WEIGHTS, SPEEDS, MESSAGE = 45, 46, 73, 79
SPEED_LANE = 32


def rim_kernel(field, far, near, mass_weight, spread, out, near_out, far_out):
    even = is_even()
    even_y = is_even("brick")
    row = lax.broadcasted_iota(jnp.int32, (8, 128), 0)
    lane = lane_of((8, 128))
    tops = jnp.zeros((8, 128), F32)
    outer = []
    for comp in range(3):
        values = [field[27 * comp + n] for n in range(27)]
        for n in range(9):
            left, right = get(near, far, 9 * comp + n, even)
            values[n] = values[n] + double(left)
            values[18 + n] = values[18 + n] + double(right)
        values = assemble_z(values, comp == 2)
        for a in range(3):
            i = 3 * comp + a
            for b in range(3):
                tops = to_lane(tops, lane, values[9 * a + 3 * b + 2], 3 * i + b)
            for c in range(2):
                first, second, third = [values[9 * a + 3 * b + c] for b in range(3)]
                for b, value in enumerate((first, second, third)):
                    out[6 * i + 2 * b + c] = pltpu.roll(value, HALO, 0)
                first = first + jnp.where(row % 2 == 1, pltpu.roll(third, 1, 0), 0.0)
                for k, value in enumerate((first, second)):
                    put(near_out, far_out, 4 * i + 2 * k + c, value[:HALO], value[HALO:OWN], even_y)
                outer.append(third)
    out[54] = pltpu.roll(tops, HALO, 0)
    for slot in range(9):
        both = jnp.where(row % 2 == 1, outer[2 * slot + 1], pltpu.roll(outer[2 * slot], 7, 0))
        put(near_out, far_out, 36 + slot, both[:HALO], both[HALO:OWN], even_y)
    inner = jnp.where(lane % 3 == 0, pltpu.roll(pltpu.roll(tops, 126, 1), 1, 0), 0.0)
    tops = tops + jnp.where((row % 2 == 1) & (lane < 27), inner, 0.0)
    for k in range(6):
        speed = spread[6 * k + 2]
        tops = to_lane(tops, lane, jnp.where(row == 0, speed, 0.0), SPEED_LANE + k)
    put(near_out, far_out, TOPS, tops[:HALO], tops[HALO:OWN], even_y)
    for q in range(27):
        put(near_out, far_out, WEIGHTS + q, mass_weight[q, :HALO], mass_weight[q, HALO:], even_y)
    for k in range(6):
        both = jnp.where(row == 0, spread[6 * k], pltpu.roll(spread[6 * k + 1], 1, 0))[:HALO].astype(BF16)
        near_out[SPEEDS + k] = both
        far_out[SPEEDS + k] = both


def send_planes(planes, near, far, even, extra=None):
    lane = lane_of((8, 128))
    sides = [jnp.zeros((8, 128), F32) if extra is None else extra, jnp.zeros((8, 128), F32)]
    for comp in range(3):
        for b in range(2):
            left, right = [[planes[comp][9 * a + 3 * b + c] for c in range(3)] for a in (0, 2)]
            for c in range(2):
                put(near, far, 4 * comp + 2 * b + c, left[c], right[c], even)
            sides = [to_lane(side, lane, plane[2], 2 * comp + b) for side, plane in zip(sides, (left, right))]
    put(near, far, 12, sides[0], sides[1], even)


def apply_mass(values, weight, wall):
    points = to_points(values)
    points = [points[q] * weight[q] for q in range(27)]
    return assemble_y(assemble_z(from_points(points), wall))


def first_kernel(
    own, far_in, near_in, mass_weight, spread, field, weight, image, near, far, speeds, rows
):
    even = is_even()
    even_y = is_even("brick")
    row = lax.broadcasted_iota(jnp.int32, (8, 128), 0)
    lane = lane_of((8, 128))
    mine = (row >= HALO) & (row < HALO + OWN)
    for k in range(SPEEDS):
        low, high = get(near_in, far_in, k, even_y)
        rows[k, :HALO] = low
        rows[k, HALO + OWN :] = high
        if k >= WEIGHTS:
            rows[k, HALO : HALO + OWN] = mass_weight[k - WEIGHTS]
    for q in range(27):
        weight[q] = rows[WEIGHTS + q] * POINT_WEIGHT[q]
    edge = (row == 1) | (row == 7)
    tops = jnp.where((lane % 3 == 2) & ~edge, 0.0, rows[TOPS])
    tops = jnp.where(mine, own[54], tops)
    planes = []
    for comp in range(3):
        values = []
        for a in range(3):
            i = 3 * comp + a
            for b in range(3):
                for c in range(2):
                    if b < 2:
                        halo = rows[4 * i + 2 * b + c]
                    else:
                        k = 2 * i + c
                        halo = rows[36 + k // 2]
                        halo = jnp.where(edge, halo if k % 2 == 1 else pltpu.roll(halo, 1, 0), 0.0)
                    values.append(jnp.where(mine, own[6 * i + 2 * b + c], halo))
                values.append(third_along_z(values[-2], tops, lane, 3 * i + b))
        values = assemble_y(values)
        for n in range(27):
            field[27 * comp + n] = values[n]
        values = apply_mass(values, weight, comp == 2)
        for n in range(27):
            image[27 * comp + n] = values[n]
        planes.append(values)
    edge_tops = get(near_in, far_in, TOPS, even_y)[1]
    edge_tops = jnp.concatenate([edge_tops] * 4, axis=0)
    plane = []
    tops = jnp.zeros((8, 128), F32)
    for comp in range(3):
        for a in range(2):
            k = 2 * comp + a
            speed = [spread[6 * k + n] for n in range(6)]
            beyond = get(near_in, far_in, SPEEDS + k, even_y)[1]
            beyond = [beyond[c : c + 1] for c in range(2)]
            for c in range(2):
                speed.append(jnp.where(row == OWN - 1, beyond[c], pltpu.roll(speed[c], 7, 0)))
            third = third_along_z(jnp.broadcast_to(beyond[0], (8, 128)), edge_tops, lane, SPEED_LANE + k)[0:1]
            speed.append(jnp.where(row == OWN - 1, third, pltpu.roll(speed[2], 7, 0)))
            for n in range(9):
                speeds[18 * comp + 9 * a + n] = speed[n]
            if a == 0:
                for b in range(3):
                    plane += speed[3 * b : 3 * b + 2]
                    tops = to_lane(tops, lane, speed[3 * b + 2], SPEED_LANE + 3 * comp + b)
    send_planes(planes, near, far, even, tops)
    for k in range(9):
        both = jnp.where(row < OWN, plane[2 * k], pltpu.roll(plane[2 * k + 1], OWN, 0)).astype(BF16)
        near[13 + k] = both
        far[13 + k] = both


def take_planes(image, near, far, comp, even):
    values = [image[27 * comp + n] for n in range(27)]
    lane = lane_of((8, 128))
    tops = get(near, far, 12, even)
    for b in range(2):
        for c in range(2):
            n = 3 * b + c
            left, right = get(near, far, 4 * comp + 2 * b + c, even)
            values[n] = values[n] + left
            values[18 + n] = values[18 + n] + right
        for a, top in zip((0, 18), tops):
            n = a + 3 * b
            top = values[n + 2] + pltpu.roll(top, 127 - 2 * comp - b, 1)
            values[n + 2] = jnp.where(lane == 127, top, pltpu.roll(values[n], 127, 1))
    for a in (0, 18):
        for c in range(3):
            values[a + 6 + c] = pltpu.roll(values[a + c], 7, 0)
    return values


def second_kernel(image, far_in, near_in, weight, field, image_out, near, far):
    even = is_even()
    planes = []
    for comp in range(3):
        values = take_planes(image, near_in, far_in, comp, even)
        for n in range(27):
            field[27 * comp + n] = values[n]
        values = apply_mass(values, weight, comp == 2)
        for n in range(27):
            image_out[27 * comp + n] = values[n]
        planes.append(values)
    send_planes(planes, near, far, even)


def work_kernel(geometry, density, energy, material, energy_mass, speeds, far, near, out):
    even = is_even()
    pressure = pressure_of(density, energy, material)
    work = jnp.zeros_like(pressure)
    row = lax.broadcasted_iota(jnp.int32, (8, 128), 0)
    lane = lane_of((8, 128))
    tops = get(near, far, 12, even)[1]
    for comp in range(3):
        speed = [speeds[18 * comp + n] for n in range(18)]
        for b in range(3):
            both = get(near, far, 13 + 3 * comp + b, even)[1]
            speed += [both, pltpu.roll(both, OWN, 0)]
            speed.append(third_along_z(both, tops, lane, SPEED_LANE + 3 * comp + b))
        for n in range(27):
            value = jnp.where(row < OWN, speed[n], pltpu.roll(speed[n], OWN, 0))
            work = work + geometry[pl.ds(4 * (27 * comp + n), 4)].astype(F32) * value[None]
    out[...] = energy[...] + HALF_STEP * pressure * work / energy_mass[...]


def dot_owned(first, second, comp, total):
    last = lane_of((8, 128)) == 127
    for a in range(2):
        for b in range(2):
            n = 27 * comp + 9 * a + 3 * b
            total = total + first[n] * second[n] + first[n + 1] * second[n + 1]
            total = total + jnp.where(last, first[n + 2] * second[n + 2], 0.0)
    return total


def product_kernel(zeroth, first, products):
    for k, (one, other) in enumerate([(zeroth, zeroth), (zeroth, first), (first, first)]):
        total = jnp.zeros((8, 128), F32)
        for comp in range(3):
            total = dot_owned(one, other, comp, total)
        products[k] = total


def moment_kernel(image, far, near, weight, first, products, second, moments):
    zero = jnp.zeros((8, 128), F32)
    cross, norm = zero, zero
    quadratic = [zero] * 3
    even = is_even()
    for comp in range(3):
        values = take_planes(image, near, far, comp, even)
        for n in range(27):
            second[27 * comp + n] = values[n]
        values_at = {27 * comp + n: values[n] for n in range(27)}
        cross = dot_owned(first, values_at, comp, cross)
        norm = dot_owned(values_at, values_at, comp, norm)
        points = to_points(values)
        for q in range(27):
            quadratic[q % 3] = quadratic[q % 3] + points[q] * points[q] * weight[q]
    quadratic = quadratic[0] + quadratic[1] + quadratic[2]
    row = lax.broadcasted_iota(jnp.int32, (8, 128), 0)
    mine = (row >= HALO) & (row < HALO + OWN)
    sums = jnp.zeros((8, 128), F32)
    for k, total in enumerate([products[0], products[1], products[2], cross, norm, quadratic]):
        total = jnp.sum(jnp.where(mine, total, 0.0), axis=0, keepdims=True)
        sums = jnp.where(row == k, total, sums)
    sums = jnp.sum(sums, axis=1, keepdims=True)
    line = jnp.sum(jnp.where(lane_of((8, 128)) == row, sums, 0.0), axis=0, keepdims=True)
    moments[...] = jnp.broadcast_to(line, moments.shape)


def solve(moments):
    def ratio(top, pivot, scale):
        good = pivot > 1e-7 * scale
        return jnp.where(good, top / jnp.where(good, pivot, 1.0), 0.0)

    m = moments
    l10 = ratio(m[2], m[1], 0.0)
    l20 = ratio(m[3], m[1], 0.0)
    d1 = m[3] - l10 * m[2]
    e1 = m[4] - l20 * m[2]
    l21 = ratio(e1, d1, m[3])
    d2 = m[5] - l20 * m[3] - l21 * e1
    y1 = m[1] - l10 * m[0]
    y2 = m[2] - l20 * m[0] - l21 * y1
    c2 = ratio(y2, d2, m[5])
    c1 = ratio(y1, d1, m[3]) - l21 * c2
    c0 = ratio(m[0], m[1], 0.0) - l10 * c1 - l20 * c2
    return c0, c1, c2


def halves(x):
    high = x.astype(BF16)
    return high, (x - high.astype(F32)).astype(BF16)


def nodal_kernel(zeroth, first, second, out):
    row = lax.broadcasted_iota(jnp.int32, (48, 96), 0)
    source = lax.broadcasted_iota(jnp.int32, (48, 96), 1)
    wanted = (row // 8) * 16 + (row % 2) * 8 + HALO + (row % 8) // 2
    move = (source == wanted).astype(F32).astype(BF16)
    source = lax.broadcasted_iota(jnp.int32, (384, 384), 0)
    node = lax.broadcasted_iota(jnp.int32, (384, 384), 1)
    wanted = jnp.where(node < 256, (node % 2) * 128 + node // 2, 383)
    place = ((source == wanted) & (node <= 256)).astype(F32).astype(BF16)
    for k, field in enumerate((zeroth, first, second)):
        blocks = []
        for c in range(3):
            column = []
            for comp in range(3):
                for a in range(2):
                    for b in range(2):
                        column.append(field[27 * comp + 9 * a + 3 * b + c])
            blocks.append(jnp.concatenate(column, axis=0))
        high, low = halves(jnp.concatenate(blocks, axis=1))
        moved = jnp.dot(move, high, preferred_element_type=F32) + jnp.dot(move, low, preferred_element_type=F32)
        high, low = halves(moved)
        out[k] = jnp.dot(high, place, preferred_element_type=F32) + jnp.dot(low, place, preferred_element_type=F32)


def last_kernel(moments, nodal, velocity, out):
    line = jnp.sum(moments[...], axis=0, keepdims=True)
    lane = lane_of((1, 128))
    mu = [jnp.sum(jnp.where(lane == k, line, 0.0), axis=1, keepdims=True) for k in range(6)]
    c0, c1, c2 = [HALF_STEP * c for c in solve(mu)]
    for comp in range(3):
        for x in range(2):
            start = 16 * comp + 8 * x
            part = [nodal[k, pl.ds(start, 8), : velocity.shape[3]] for k in range(3)]
            out[comp, x] = velocity[comp, x] + (c0 * part[0] + c1 * part[1] + c2 * part[2])


VMEM = pl.BlockSpec(memory_space=pltpu.VMEM)


def call(kernel, outs, *args, scratch=(), flops=100000, place=VMEM, dtypes=None):
    shapes = [jax.ShapeDtypeStruct(shape, dtype) for shape, dtype in zip(outs, dtypes or [F32] * len(outs))]
    moved = sum(a.size * a.dtype.itemsize for a in args) + sum(4 * int(np.prod(s)) for s in outs)
    return pl.pallas_call(
        kernel,
        out_shape=shapes,
        in_specs=[place] * len(args),
        out_specs=[VMEM] * len(outs),
        scratch_shapes=list(scratch),
        compiler_params=pltpu.CompilerParams(vmem_limit_bytes=32 * 1024 * 1024),
        cost_estimate=pl.CostEstimate(flops=flops, bytes_accessed=moved, transcendentals=0),
        name=kernel.__name__,
    )(*args)


def swap(near, far, axis="slab"):
    count = lax.axis_size(axis)
    far = lax.ppermute(far, axis, [(i, (i + (1 if i % 2 else -1)) % count) for i in range(count)])
    near = lax.ppermute(near, axis, [(i, i + (-1 if i % 2 else 1)) for i in range(count)])
    return near, far


def local(velocity, energy, density, material, geometry, mass_weight, energy_mass):
    tile = (4, 128)
    full = (8, 128)
    geometry = geometry.reshape((324,) + full)
    density = density.reshape((4,) + full)
    energy = energy.reshape((4,) + full)
    energy_mass = energy_mass.reshape((4,) + full)
    mass_weight = mass_weight.reshape((27,) + tile)
    material = material.reshape(tile)
    pair = (2, 128)
    devices = lax.axis_size("slab") * lax.axis_size("brick")

    force, near, far = call(
        force_kernel,
        [(81,) + full, (27,) + tile, (27,) + tile],
        *[pltpu.with_memory_space_constraint(x, pltpu.HBM) for x in (geometry, density, energy, material, mass_weight)],
        scratch=[
            pltpu.VMEM((324,) + full, BF16),
            pltpu.VMEM((4,) + full, F32),
            pltpu.VMEM((4,) + full, F32),
            pltpu.VMEM(tile, jnp.int32),
            pltpu.VMEM((27,) + tile, F32),
            pltpu.SemaphoreType.DMA((7,)),
        ],
        place=pl.BlockSpec(memory_space=pltpu.HBM),
        dtypes=[F32, BF16, BF16],
    )
    (spread,) = call(spread_kernel, [(36,) + full], velocity)
    near, far = swap(near, far)
    own, near, far = call(
        rim_kernel,
        [(55,) + full, (MESSAGE,) + pair, (MESSAGE,) + pair],
        force, far, near, mass_weight, spread,
        dtypes=[F32, BF16, BF16],
    )
    near, far = swap(near, far, "brick")
    zeroth, weight, image, near, far, speeds = call(
        first_kernel,
        [(81,) + full, (27,) + full, (81,) + full, (22,) + full, (22,) + full, (54,) + full],
        own, far, near, mass_weight, spread,
        scratch=[pltpu.VMEM((SPEEDS,) + full, F32)],
        dtypes=[F32, F32, F32, BF16, BF16, F32],
    )
    near, far = swap(near, far)
    first, image, near_out, far_out = call(
        second_kernel,
        [(81,) + full, (81,) + full, (13,) + full, (13,) + full],
        image, far, near, weight,
        dtypes=[F32, F32, BF16, BF16],
    )
    (energy_half,) = call(
        work_kernel, [(4,) + full], geometry, density, energy, material, energy_mass, speeds, far, near
    )
    near, far = swap(near_out, far_out)
    (products,) = call(product_kernel, [(3,) + full], zeroth, first)
    second, moments = call(
        moment_kernel, [(81,) + full, (devices, 128)], image, far, near, weight, first, products
    )
    moments = lax.all_to_all(moments, ("slab", "brick"), 0, 0, tiled=True)
    (nodal,) = call(nodal_kernel, [(3, 48, 384)], zeroth, first, second)
    (velocity_half,) = call(last_kernel, [velocity.shape], moments, nodal, velocity)
    return (velocity_half, energy_half.reshape(8, 1, 4, 128))


def solution(mesh):
    nodes = P(None, "slab", "brick", None)
    return jax.shard_map(
        local,
        mesh=mesh,
        in_specs=(
            nodes,
            nodes,
            nodes,
            P("slab", "brick", None),
            P(None, None, "slab", "brick", None),
            nodes,
            nodes,
        ),
        out_specs=(nodes, nodes),
        check_vma=False,
    )
```

```python
import jax
import jax.numpy as jnp
import numpy as np
from jax import lax
from jax.experimental import pallas as pl
from jax.experimental.pallas import tpu as pltpu
from jax.sharding import PartitionSpec as P

HALF_STEP = 0.25
GRAVITY = 1.0
F32 = jnp.float32
BF16 = jnp.bfloat16

OFFSET = float(np.sqrt(0.6) / 2.0)
SIDE = 0.3
MIDDLE = 0.4
LINE_WEIGHTS = (5.0 / 18.0, 8.0 / 18.0, 5.0 / 18.0)
POINT_WEIGHT = [a * b * c for a in LINE_WEIGHTS for b in LINE_WEIGHTS for c in LINE_WEIGHTS]
OWN = 4
HALO = 2


def lines(direction):
    stride = (9, 3, 1)[direction]
    return [(n, n + stride, n + 2 * stride) for n in range(27) if (n // stride) % 3 == 0]


def to_points(values):
    values = list(values)
    for direction in range(3):
        for i, j, k in lines(direction):
            even = SIDE * (values[i] + values[k]) + MIDDLE * values[j]
            odd = OFFSET * (values[i] - values[k])
            values[i], values[k] = even + odd, even - odd
    return values


def from_points(values):
    values = list(values)
    for direction in range(3):
        for i, j, k in lines(direction):
            total = values[i] + values[k]
            odd = OFFSET * (values[i] - values[k])
            even = SIDE * total
            values[i], values[k] = even + odd, even - odd
            values[j] = values[j] + MIDDLE * total
    return values


def lane_of(shape):
    return lax.broadcasted_iota(jnp.int32, shape, len(shape) - 1)


def assemble_z(values, wall):
    values = list(values)
    lane = lane_of(values[0].shape)
    first, last = lane == 0, lane == 127
    for i, k in [(n, n + 2) for n in range(0, len(values), 3)]:
        total = values[i] + jnp.where(first, 0.0, pltpu.roll(values[k], 1, 1))
        top = values[k]
        if wall:
            total = jnp.where(first, 0.0, total)
            top = jnp.zeros_like(top)
        values[i] = total
        values[k] = jnp.where(last, top, pltpu.roll(total, 127, 1))
    return values


def assemble_y(values):
    values = list(values)
    for i, _, k in lines(1):
        values[i] = values[i] + pltpu.roll(values[k], 1, 0)
        values[k] = pltpu.roll(values[i], 7, 0)
    return values


def is_even(axis="slab"):
    return lax.axis_index(axis) % 2 == 0


def put(near, far, slot, left, right, even):
    near[slot] = jnp.where(even, right, left).astype(BF16)
    far[slot] = jnp.where(even, left, right).astype(BF16)


def get(near, far, slot, even):
    one, other = near[slot].astype(F32), far[slot].astype(F32)
    return jnp.where(even, other, one), jnp.where(even, one, other)


def pressure_of(density, energy, material):
    gamma = jnp.where(material[...] == 0, 2.0 / 3.0, 0.4).astype(F32)
    gamma = jnp.concatenate([gamma, gamma], axis=0)
    return (gamma[None] * density[...] * energy[...]).astype(BF16).astype(F32)


def to_lane(tile, lane, values, slot):
    return jnp.where(lane == slot, pltpu.roll(values, slot + 1, 1), tile)


def third_along_z(values, tops, lane, slot):
    return jnp.where(lane == 127, pltpu.roll(tops, 127 - slot, 1), pltpu.roll(values, 127, 1))


def double(values):
    return jnp.concatenate([values, values], axis=0)


def force_kernel(
    geometry_in, density_in, energy_in, material_in, mass_weight_in,
    field, near, far,
    geometry, density, energy, material, mass_weight, sems,
):
    small = [
        pltpu.make_async_copy(source, target, sems.at[3 + i])
        for i, (source, target) in enumerate(
            [(density_in, density), (energy_in, energy), (material_in, material), (mass_weight_in, mass_weight)]
        )
    ]
    parts = [
        pltpu.make_async_copy(
            geometry_in.at[pl.ds(108 * comp, 108)], geometry.at[pl.ds(108 * comp, 108)], sems.at[comp]
        )
        for comp in range(3)
    ]
    for copy in small + parts:
        copy.start()
    for copy in small:
        copy.wait()
    pressure = pressure_of(density, energy, material)
    gravity = from_points([double(mass_weight[q]) * POINT_WEIGHT[q] for q in range(27)])
    even = is_even()
    for comp in range(3):
        parts[comp].wait()
        values = []
        for n in range(27):
            r = 27 * comp + n
            value = jnp.sum(geometry[pl.ds(4 * r, 4)].astype(F32) * pressure, axis=0)
            value = -(value + pltpu.roll(value, OWN, 0))
            if comp == 2:
                value = value - GRAVITY * gravity[n]
            field[r] = value
            values.append(value)
        for n in range(9):
            put(near, far, 9 * comp + n, values[n][:OWN], values[18 + n][:OWN], even)


def spread_velocity(velocity, out):
    rows = velocity[...].astype(BF16).reshape(48, velocity.shape[3])
    low = rows[:, :256]
    high = rows[:, 256:257].astype(F32)
    node = lax.broadcasted_iota(jnp.int32, (256, 384), 0)
    lane = lax.broadcasted_iota(jnp.int32, (256, 384), 1)
    pick = (node == 2 * (lane % 128) + lane // 128).astype(F32).astype(BF16)
    spread = jnp.dot(low, pick, preferred_element_type=F32)
    top = jnp.where(lane_of((48, 128)) == 127, high, 0.0)
    spread = jnp.concatenate([spread[:, :256], spread[:, 256:] + top], axis=1)
    row = lax.broadcasted_iota(jnp.int32, (96, 48), 0)
    source = lax.broadcasted_iota(jnp.int32, (96, 48), 1)
    wanted = (row // 16) * 8 + 2 * (row % 8) + (row // 8) % 2
    move = ((source == wanted) & (row % 8 < OWN)).astype(F32).astype(BF16)
    moved = jnp.dot(move, spread.astype(BF16), preferred_element_type=F32)
    for group in range(12):
        for c in range(3):
            out[3 * group + c] = moved[8 * group : 8 * group + 8, 128 * c : 128 * c + 128]


TOPS, WEIGHTS, SPEEDS, MESSAGE = 45, 46, 73, 79
SPEED_LANE = 32


def fill_plane(values, comp, a, tops, out, near, far, even_y):
    row = lax.broadcasted_iota(jnp.int32, (8, 128), 0)
    lane = lane_of((8, 128))
    i = 3 * comp + a
    outer = []
    for b in range(3):
        tops = to_lane(tops, lane, values[9 * a + 3 * b + 2], 3 * i + b)
    for c in range(2):
        first, second, third = [values[9 * a + 3 * b + c] for b in range(3)]
        for b, value in enumerate((first, second, third)):
            out[6 * i + 2 * b + c] = pltpu.roll(value, HALO, 0)
        first = first + jnp.where(row % 2 == 1, pltpu.roll(third, 1, 0), 0.0)
        for k, value in enumerate((first, second)):
            put(near, far, 4 * i + 2 * k + c, value[:HALO], value[HALO:OWN], even_y)
        outer.append(third)
    both = jnp.where(row % 2 == 1, outer[1], pltpu.roll(outer[0], 7, 0))
    put(near, far, 36 + i, both[:HALO], both[HALO:OWN], even_y)
    return tops


def spread_kernel(velocity, field, mass_weight, spread, middle, near, far):
    even_y = is_even("brick")
    row = lax.broadcasted_iota(jnp.int32, (8, 128), 0)
    lane = lane_of((8, 128))
    spread_velocity(velocity, spread)
    tops = jnp.zeros((8, 128), F32)
    for comp in range(3):
        values = [field[27 * comp + 9 + n] for n in range(9)]
        values = [None] * 9 + assemble_z(values, comp == 2)
        tops = fill_plane(values, comp, 1, tops, middle, near, far, even_y)
    for k in range(6):
        tops = to_lane(tops, lane, jnp.where(row == 0, spread[6 * k + 2], 0.0), SPEED_LANE + k)
    middle[54] = tops
    for q in range(27):
        put(near, far, WEIGHTS + q, mass_weight[q, :HALO], mass_weight[q, HALO:], even_y)
    for k in range(6):
        both = jnp.where(row == 0, spread[6 * k], pltpu.roll(spread[6 * k + 1], 1, 0))[:HALO].astype(BF16)
        near[SPEEDS + k] = both
        far[SPEEDS + k] = both


def rim_kernel(field, far, near, middle, near_in, far_in, out, near_out, far_out):
    even = is_even()
    even_y = is_even("brick")
    row = lax.broadcasted_iota(jnp.int32, (8, 128), 0)
    lane = lane_of((8, 128))
    tops = middle[54]
    for comp in range(3):
        i = 3 * comp + 1
        for k in range(6):
            out[6 * i + k] = middle[6 * i + k]
        for k in [4 * i, 4 * i + 1, 4 * i + 2, 4 * i + 3, 36 + i]:
            near_out[k] = near_in[k]
            far_out[k] = far_in[k]
        values = [field[27 * comp + n] for n in range(27)]
        for n in range(9):
            left, right = get(near, far, 9 * comp + n, even)
            values[n] = values[n] + double(left)
            values[18 + n] = values[18 + n] + double(right)
        values = assemble_z(values[:9] + values[18:], comp == 2)
        values = values[:9] + [None] * 9 + values[9:]
        for a in (0, 2):
            tops = fill_plane(values, comp, a, tops, out, near_out, far_out, even_y)
    out[54] = pltpu.roll(tops, HALO, 0)
    inner = jnp.where(lane % 3 == 0, pltpu.roll(pltpu.roll(tops, 126, 1), 1, 0), 0.0)
    tops = tops + jnp.where((row % 2 == 1) & (lane < 27), inner, 0.0)
    put(near_out, far_out, TOPS, tops[:HALO], tops[HALO:OWN], even_y)
    for k in range(WEIGHTS, MESSAGE):
        near_out[k] = near_in[k]
        far_out[k] = far_in[k]


def send_planes(planes, near, far, even):
    lane = lane_of((8, 128))
    sides = [jnp.zeros((8, 128), F32)] * 2
    for comp in range(3):
        for b in range(2):
            left, right = [[planes[comp][9 * a + 3 * b + c] for c in range(3)] for a in (0, 2)]
            for c in range(2):
                put(near, far, 4 * comp + 2 * b + c, left[c], right[c], even)
            sides = [to_lane(side, lane, plane[2], 2 * comp + b) for side, plane in zip(sides, (left, right))]
    put(near, far, 12, sides[0], sides[1], even)


def apply_mass(values, weight, wall):
    points = to_points(values)
    points = [points[q] * weight[q] for q in range(27)]
    return assemble_y(assemble_z(from_points(points), wall))


def first_kernel(
    own, far_in, near_in, mass_weight, field, weight, image, near, far, rows
):
    even = is_even()
    even_y = is_even("brick")
    row = lax.broadcasted_iota(jnp.int32, (8, 128), 0)
    lane = lane_of((8, 128))
    mine = (row >= HALO) & (row < HALO + OWN)
    for k in range(SPEEDS):
        low, high = get(near_in, far_in, k, even_y)
        rows[k, :HALO] = low
        rows[k, HALO + OWN :] = high
        if k >= WEIGHTS:
            rows[k, HALO : HALO + OWN] = mass_weight[k - WEIGHTS]
    for q in range(27):
        weight[q] = rows[WEIGHTS + q] * POINT_WEIGHT[q]
    edge = (row == 1) | (row == 7)
    tops = jnp.where((lane % 3 == 2) & ~edge, 0.0, rows[TOPS])
    tops = jnp.where(mine, own[54], tops)
    planes = []
    for comp in range(3):
        values = []
        for a in range(3):
            i = 3 * comp + a
            for b in range(3):
                for c in range(2):
                    if b < 2:
                        halo = rows[4 * i + 2 * b + c]
                    else:
                        k = 2 * i + c
                        halo = rows[36 + k // 2]
                        halo = jnp.where(edge, halo if k % 2 == 1 else pltpu.roll(halo, 1, 0), 0.0)
                    values.append(jnp.where(mine, own[6 * i + 2 * b + c], halo))
                values.append(third_along_z(values[-2], tops, lane, 3 * i + b))
        values = assemble_y(values)
        for n in range(27):
            field[27 * comp + n] = values[n]
        values = apply_mass(values, weight, comp == 2)
        for n in range(27):
            image[27 * comp + n] = values[n]
        planes.append(values)
    send_planes(planes, near, far, even)


def speed_kernel(far_in, near_in, spread, speeds, plane_out):
    even_y = is_even("brick")
    row = lax.broadcasted_iota(jnp.int32, (8, 128), 0)
    lane = lane_of((8, 128))
    edge_tops = get(near_in, far_in, TOPS, even_y)[1]
    edge_tops = jnp.concatenate([edge_tops] * 4, axis=0)
    plane = []
    tops = jnp.zeros((8, 128), F32)
    for comp in range(3):
        for a in range(2):
            k = 2 * comp + a
            speed = [spread[6 * k + n] for n in range(6)]
            beyond = get(near_in, far_in, SPEEDS + k, even_y)[1]
            beyond = [beyond[c : c + 1] for c in range(2)]
            for c in range(2):
                speed.append(jnp.where(row == OWN - 1, beyond[c], pltpu.roll(speed[c], 7, 0)))
            third = third_along_z(jnp.broadcast_to(beyond[0], (8, 128)), edge_tops, lane, SPEED_LANE + k)[0:1]
            speed.append(jnp.where(row == OWN - 1, third, pltpu.roll(speed[2], 7, 0)))
            for n in range(9):
                speeds[18 * comp + 9 * a + n] = speed[n]
            if a == 0:
                for b in range(3):
                    plane += speed[3 * b : 3 * b + 2]
                    tops = to_lane(tops, lane, speed[3 * b + 2], SPEED_LANE + 3 * comp + b)
    for k in range(9):
        plane_out[k] = jnp.where(row < OWN, plane[2 * k], pltpu.roll(plane[2 * k + 1], OWN, 0))
    plane_out[9] = tops


def send_own(planes, speeds, near, far, even):
    row = lax.broadcasted_iota(jnp.int32, (8, 128), 0)
    lane = lane_of((8, 128))
    sides = [speeds[9], jnp.zeros((8, 128), F32)]
    after = [jnp.zeros((8, 128), F32)] * 2
    for comp in range(3):
        for b in range(2):
            both = []
            for side, a in enumerate((0, 2)):
                plane = [planes[comp][9 * a + 3 * b + c] for c in range(3)]
                both.append(jnp.where(row < OWN, pltpu.roll(plane[0], 6, 0), pltpu.roll(plane[1], 2, 0)))
                sides[side] = to_lane(sides[side], lane, plane[2], 2 * comp + b)
                if b == 0:
                    for c in range(2):
                        k = 2 * comp + c
                        after[side] = jnp.where(row == k, pltpu.roll(plane[c], (k + 2) % 8, 0), after[side])
            put(near, far, 2 * comp + b, both[0], both[1], even)
    put(near, far, 6, after[0], after[1], even)
    put(near, far, 7, sides[0], sides[1], even)
    for k in range(9):
        near[8 + k] = speeds[k].astype(BF16)
        far[8 + k] = speeds[k].astype(BF16)


def take_planes(image, near, far, comp, even):
    def read(b):
        tiles = [get(near, far, 4 * comp + 2 * b + c, even) for c in range(2)]
        return [[tile[side] for tile in tiles] for side in range(2)]

    return add_planes(image, read, get(near, far, 12, even), comp)


def take_own(image, near, far, comp, even):
    row = lax.broadcasted_iota(jnp.int32, (8, 128), 0)
    after = get(near, far, 6, even)

    def read(b):
        sides = []
        for side, both in enumerate(get(near, far, 2 * comp + b, even)):
            plane = [pltpu.roll(both, 2, 0), pltpu.roll(both, 6, 0)]
            if b == 0:
                for c in range(2):
                    k = 2 * comp + c
                    plane[c] = jnp.where(row == 6, pltpu.roll(after[side], 6 - k, 0), plane[c])
            sides.append(plane)
        return sides

    return add_planes(image, read, get(near, far, 7, even), comp)


def add_planes(image, read, tops, comp):
    values = [image[27 * comp + n] for n in range(27)]
    lane = lane_of((8, 128))
    for b in range(2):
        for a, plane, top in zip((0, 18), read(b), tops):
            n = a + 3 * b
            for c in range(2):
                values[n + c] = values[n + c] + plane[c]
            top = values[n + 2] + pltpu.roll(top, 127 - 2 * comp - b, 1)
            values[n + 2] = jnp.where(lane == 127, top, pltpu.roll(values[n], 127, 1))
    for a in (0, 18):
        for c in range(3):
            values[a + 6 + c] = pltpu.roll(values[a + c], 7, 0)
    return values


def second_kernel(image, far_in, near_in, weight, speeds, field, image_out, near, far):
    even = is_even()
    planes = []
    for comp in range(3):
        values = take_planes(image, near_in, far_in, comp, even)
        for n in range(27):
            field[27 * comp + n] = values[n]
        values = apply_mass(values, weight, comp == 2)
        for n in range(27):
            image_out[27 * comp + n] = values[n]
        planes.append(values)
    send_own(planes, speeds, near, far, even)


def work_kernel(geometry, density, energy, material, energy_mass, speeds, far, near, out):
    even = is_even()
    pressure = pressure_of(density, energy, material)
    work = jnp.zeros_like(pressure)
    row = lax.broadcasted_iota(jnp.int32, (8, 128), 0)
    lane = lane_of((8, 128))
    tops = get(near, far, 7, even)[1]
    for comp in range(3):
        speed = [speeds[18 * comp + n] for n in range(18)]
        for b in range(3):
            both = get(near, far, 8 + 3 * comp + b, even)[1]
            speed += [both, pltpu.roll(both, OWN, 0)]
            speed.append(third_along_z(both, tops, lane, SPEED_LANE + 3 * comp + b))
        for n in range(27):
            value = jnp.where(row < OWN, speed[n], pltpu.roll(speed[n], OWN, 0))
            work = work + geometry[pl.ds(4 * (27 * comp + n), 4)].astype(F32) * value[None]
    out[...] = energy[...] + HALF_STEP * pressure * work / energy_mass[...]


def dot_owned(first, second, comp, total):
    last = lane_of((8, 128)) == 127
    for a in range(2):
        for b in range(2):
            n = 27 * comp + 9 * a + 3 * b
            total = total + first[n] * second[n] + first[n + 1] * second[n + 1]
            total = total + jnp.where(last, first[n + 2] * second[n + 2], 0.0)
    return total


def product_kernel(zeroth, first, products):
    for k, (one, other) in enumerate([(zeroth, zeroth), (zeroth, first), (first, first)]):
        total = jnp.zeros((8, 128), F32)
        for comp in range(3):
            total = dot_owned(one, other, comp, total)
        products[k] = total


def moment_kernel(image, far, near, weight, first, products, second, moments):
    zero = jnp.zeros((8, 128), F32)
    cross, norm = zero, zero
    quadratic = [zero] * 3
    even = is_even()
    for comp in range(3):
        values = take_own(image, near, far, comp, even)
        for n in range(27):
            second[27 * comp + n] = values[n]
        values_at = {27 * comp + n: values[n] for n in range(27)}
        cross = dot_owned(first, values_at, comp, cross)
        norm = dot_owned(values_at, values_at, comp, norm)
        points = to_points(values)
        for q in range(27):
            quadratic[q % 3] = quadratic[q % 3] + points[q] * points[q] * weight[q]
    quadratic = quadratic[0] + quadratic[1] + quadratic[2]
    row = lax.broadcasted_iota(jnp.int32, (8, 128), 0)
    mine = (row >= HALO) & (row < HALO + OWN)
    sums = jnp.zeros((8, 128), F32)
    for k, total in enumerate([products[0], products[1], products[2], cross, norm, quadratic]):
        total = jnp.sum(jnp.where(mine, total, 0.0), axis=0, keepdims=True)
        sums = jnp.where(row == k, total, sums)
    sums = jnp.sum(sums, axis=1, keepdims=True)
    line = jnp.sum(jnp.where(lane_of((8, 128)) == row, sums, 0.0), axis=0, keepdims=True)
    moments[...] = jnp.broadcast_to(line, moments.shape)


def solve(moments):
    def ratio(top, pivot, scale):
        good = pivot > 1e-7 * scale
        return jnp.where(good, top / jnp.where(good, pivot, 1.0), 0.0)

    m = moments
    l10 = ratio(m[2], m[1], 0.0)
    l20 = ratio(m[3], m[1], 0.0)
    d1 = m[3] - l10 * m[2]
    e1 = m[4] - l20 * m[2]
    l21 = ratio(e1, d1, m[3])
    d2 = m[5] - l20 * m[3] - l21 * e1
    y1 = m[1] - l10 * m[0]
    y2 = m[2] - l20 * m[0] - l21 * y1
    c2 = ratio(y2, d2, m[5])
    c1 = ratio(y1, d1, m[3]) - l21 * c2
    c0 = ratio(m[0], m[1], 0.0) - l10 * c1 - l20 * c2
    return c0, c1, c2


def halves(x):
    high = x.astype(BF16)
    return high, (x - high.astype(F32)).astype(BF16)


def nodal_kernel(zeroth, first, second, out):
    row = lax.broadcasted_iota(jnp.int32, (48, 96), 0)
    source = lax.broadcasted_iota(jnp.int32, (48, 96), 1)
    wanted = (row // 8) * 16 + (row % 2) * 8 + HALO + (row % 8) // 2
    move = (source == wanted).astype(F32).astype(BF16)
    source = lax.broadcasted_iota(jnp.int32, (384, 384), 0)
    node = lax.broadcasted_iota(jnp.int32, (384, 384), 1)
    wanted = jnp.where(node < 256, (node % 2) * 128 + node // 2, 383)
    place = ((source == wanted) & (node <= 256)).astype(F32).astype(BF16)
    for k, field in enumerate((zeroth, first, second)):
        blocks = []
        for c in range(3):
            column = []
            for comp in range(3):
                for a in range(2):
                    for b in range(2):
                        column.append(field[27 * comp + 9 * a + 3 * b + c])
            blocks.append(jnp.concatenate(column, axis=0))
        high, low = halves(jnp.concatenate(blocks, axis=1))
        moved = jnp.dot(move, high, preferred_element_type=F32) + jnp.dot(move, low, preferred_element_type=F32)
        high, low = halves(moved)
        out[k] = jnp.dot(high, place, preferred_element_type=F32) + jnp.dot(low, place, preferred_element_type=F32)


def last_kernel(moments, nodal, velocity, out):
    line = jnp.sum(moments[...], axis=0, keepdims=True)
    lane = lane_of((1, 128))
    mu = [jnp.sum(jnp.where(lane == k, line, 0.0), axis=1, keepdims=True) for k in range(6)]
    c0, c1, c2 = [HALF_STEP * c for c in solve(mu)]
    for comp in range(3):
        for x in range(2):
            start = 16 * comp + 8 * x
            part = [nodal[k, pl.ds(start, 8), : velocity.shape[3]] for k in range(3)]
            out[comp, x] = velocity[comp, x] + (c0 * part[0] + c1 * part[1] + c2 * part[2])


VMEM = pl.BlockSpec(memory_space=pltpu.VMEM)


def call(kernel, outs, *args, scratch=(), flops=100000, place=VMEM, dtypes=None):
    shapes = [jax.ShapeDtypeStruct(shape, dtype) for shape, dtype in zip(outs, dtypes or [F32] * len(outs))]
    moved = sum(a.size * a.dtype.itemsize for a in args) + sum(4 * int(np.prod(s)) for s in outs)
    return pl.pallas_call(
        kernel,
        out_shape=shapes,
        in_specs=[place] * len(args),
        out_specs=[VMEM] * len(outs),
        scratch_shapes=list(scratch),
        compiler_params=pltpu.CompilerParams(vmem_limit_bytes=32 * 1024 * 1024),
        cost_estimate=pl.CostEstimate(flops=flops, bytes_accessed=moved, transcendentals=0),
        name=kernel.__name__,
    )(*args)


def swap(near, far, axis="slab"):
    count = lax.axis_size(axis)
    far = lax.ppermute(far, axis, [(i, (i + (1 if i % 2 else -1)) % count) for i in range(count)])
    near = lax.ppermute(near, axis, [(i, i + (-1 if i % 2 else 1)) for i in range(count)])
    return near, far


def local(velocity, energy, density, material, geometry, mass_weight, energy_mass):
    tile = (4, 128)
    full = (8, 128)
    geometry = geometry.reshape((324,) + full)
    density = density.reshape((4,) + full)
    energy = energy.reshape((4,) + full)
    energy_mass = energy_mass.reshape((4,) + full)
    mass_weight = mass_weight.reshape((27,) + tile)
    material = material.reshape(tile)
    pair = (2, 128)
    devices = lax.axis_size("slab") * lax.axis_size("brick")

    force, near, far = call(
        force_kernel,
        [(81,) + full, (27,) + tile, (27,) + tile],
        *[pltpu.with_memory_space_constraint(x, pltpu.HBM) for x in (geometry, density, energy, material, mass_weight)],
        scratch=[
            pltpu.VMEM((324,) + full, BF16),
            pltpu.VMEM((4,) + full, F32),
            pltpu.VMEM((4,) + full, F32),
            pltpu.VMEM(tile, jnp.int32),
            pltpu.VMEM((27,) + tile, F32),
            pltpu.SemaphoreType.DMA((7,)),
        ],
        place=pl.BlockSpec(memory_space=pltpu.HBM),
        dtypes=[F32, BF16, BF16],
    )
    spread, middle, near_part, far_part = call(
        spread_kernel,
        [(36,) + full, (55,) + full, (MESSAGE,) + pair, (MESSAGE,) + pair],
        velocity, force, mass_weight,
        dtypes=[F32, F32, BF16, BF16],
    )
    near, far = swap(near, far)
    own, near, far = call(
        rim_kernel,
        [(55,) + full, (MESSAGE,) + pair, (MESSAGE,) + pair],
        force, far, near, middle, near_part, far_part,
        dtypes=[F32, BF16, BF16],
    )
    near_rim, far_rim = swap(near, far, "brick")
    zeroth, weight, image, near, far = call(
        first_kernel,
        [(81,) + full, (27,) + full, (81,) + full, (13,) + full, (13,) + full],
        own, far_rim, near_rim, mass_weight,
        scratch=[pltpu.VMEM((SPEEDS,) + full, F32)],
        dtypes=[F32, F32, F32, BF16, BF16],
    )
    near, far = swap(near, far)
    speeds, plane = call(speed_kernel, [(54,) + full, (10,) + full], far_rim, near_rim, spread)
    first, image, near, far = call(
        second_kernel,
        [(81,) + full, (81,) + full, (17,) + full, (17,) + full],
        image, far, near, weight, plane,
        dtypes=[F32, F32, BF16, BF16],
    )
    near, far = swap(near, far)
    (energy_half,) = call(
        work_kernel, [(4,) + full], geometry, density, energy, material, energy_mass, speeds, far, near
    )
    (products,) = call(product_kernel, [(3,) + full], zeroth, first)
    second, moments = call(
        moment_kernel, [(81,) + full, (devices, 128)], image, far, near, weight, first, products
    )
    moments = lax.all_to_all(moments, ("slab", "brick"), 0, 0, tiled=True)
    (nodal,) = call(nodal_kernel, [(3, 48, 384)], zeroth, first, second)
    (velocity_half,) = call(last_kernel, [velocity.shape], moments, nodal, velocity)
    return (velocity_half, energy_half.reshape(8, 1, 4, 128))


def solution(mesh):
    nodes = P(None, "slab", "brick", None)
    return jax.shard_map(
        local,
        mesh=mesh,
        in_specs=(
            nodes,
            nodes,
            nodes,
            P("slab", "brick", None),
            P(None, None, "slab", "brick", None),
            nodes,
            nodes,
        ),
        out_specs=(nodes, nodes),
        check_vma=False,
    )
```

```python
import jax
import jax.numpy as jnp
import numpy as np
from jax import lax
from jax.experimental import pallas as pl
from jax.experimental.pallas import tpu as pltpu
from jax.sharding import PartitionSpec as P

HALF_STEP = 0.25
GRAVITY = 1.0
F32 = jnp.float32
BF16 = jnp.bfloat16

OFFSET = float(np.sqrt(0.6) / 2.0)
SIDE = 0.3
MIDDLE = 0.4
ODD, EVEN = OFFSET / SIDE, MIDDLE / SIDE
LINE_WEIGHTS = (5.0 / 18.0, 8.0 / 18.0, 5.0 / 18.0)
POINT_WEIGHT = [a * b * c for a in LINE_WEIGHTS for b in LINE_WEIGHTS for c in LINE_WEIGHTS]
POINT_SCALE = [a * b * c for a in (SIDE, 1.0, SIDE) for b in (SIDE, 1.0, SIDE) for c in (SIDE, 1.0, SIDE)]
OWN = 4
HALO = 2


def lines(direction):
    stride = (9, 3, 1)[direction]
    return [(n, n + stride, n + 2 * stride) for n in range(27) if (n // stride) % 3 == 0]


def to_points(values):
    values = list(values)
    for direction in range(3):
        for i, j, k in lines(direction):
            even = (values[i] + values[k]) + EVEN * values[j]
            odd = ODD * (values[i] - values[k])
            values[i], values[k] = even + odd, even - odd
    return values


def from_points(values):
    values = list(values)
    for direction in range(3):
        for i, j, k in lines(direction):
            total = values[i] + values[k]
            odd = ODD * (values[i] - values[k])
            values[i], values[k] = total + odd, total - odd
            values[j] = values[j] + EVEN * total
    return values


def lane_of(shape):
    return lax.broadcasted_iota(jnp.int32, shape, len(shape) - 1)


def assemble_z(values, wall):
    values = list(values)
    lane = lane_of(values[0].shape)
    first, last = lane == 0, lane == 127
    for i, k in [(n, n + 2) for n in range(0, len(values), 3)]:
        total = values[i] + jnp.where(first, 0.0, pltpu.roll(values[k], 1, 1))
        top = values[k]
        if wall:
            total = jnp.where(first, 0.0, total)
            top = jnp.zeros_like(top)
        values[i] = total
        values[k] = jnp.where(last, top, pltpu.roll(total, 127, 1))
    return values


def fold(values, wall):
    lane = lane_of(values[0].shape)
    folded = []
    for a in (0, 9, 18):
        columns = [[values[a + c] + pltpu.roll(values[a + 6 + c], 1, 0), values[a + 3 + c]] for c in range(3)]
        for b in range(2):
            first = columns[0][b] + jnp.where(lane == 0, 0.0, pltpu.roll(columns[2][b], 1, 1))
            if wall:
                first = jnp.where(lane == 0, 0.0, first)
            folded += [first, columns[1][b], jnp.zeros_like(first) if wall else columns[2][b]]
    return folded


def unfold(folded):
    lane = lane_of(folded[0].shape)
    values = []
    for a in (0, 6, 12):
        planes = []
        for b in (0, 3):
            first, second, top = folded[a + b : a + b + 3]
            planes.append([first, second, jnp.where(lane == 127, top, pltpu.roll(first, 127, 1))])
        planes.append([pltpu.roll(value, 7, 0) for value in planes[0]])
        values += planes[0] + planes[1] + planes[2]
    return values


def is_even(axis="slab"):
    return lax.axis_index(axis) % 2 == 0


def put(near, far, slot, left, right, even):
    near[slot] = jnp.where(even, right, left).astype(BF16)
    far[slot] = jnp.where(even, left, right).astype(BF16)


def get(near, far, slot, even):
    one, other = near[slot].astype(F32), far[slot].astype(F32)
    return jnp.where(even, other, one), jnp.where(even, one, other)


def pressure_of(density, energy, material):
    gamma = jnp.where(material[...] == 0, 2.0 / 3.0, 0.4).astype(F32)
    gamma = jnp.concatenate([gamma, gamma], axis=0)
    return (gamma[None] * density[...] * energy[...]).astype(BF16).astype(F32)


def to_lane(tile, lane, values, slot):
    return jnp.where(lane == slot, pltpu.roll(values, slot + 1, 1), tile)


def third_along_z(values, tops, lane, slot):
    return jnp.where(lane == 127, pltpu.roll(tops, 127 - slot, 1), pltpu.roll(values, 127, 1))


def double(values):
    return jnp.concatenate([values, values], axis=0)


def force_of(geometry, r, pressure):
    value = jnp.sum(geometry[pl.ds(4 * r, 4)].astype(F32) * pressure, axis=0)
    return -(value + pltpu.roll(value, OWN, 0))


def force_kernel(
    geometry_in, density_in, energy_in, material_in, mass_weight_in,
    field, near, far, pressure_out, gravity_out,
    geometry, density, energy, material, mass_weight, sems,
):
    small = [
        pltpu.make_async_copy(source, target, sems.at[6 + i])
        for i, (source, target) in enumerate(
            [(density_in, density), (energy_in, energy), (material_in, material), (mass_weight_in, mass_weight)]
        )
    ]
    parts = [
        pltpu.make_async_copy(
            geometry_in.at[pl.ds(108 * comp + 36 * a, 36)], geometry.at[pl.ds(72 * comp + 18 * a, 36)], sems.at[2 * comp + a // 2]
        )
        for comp in range(3)
        for a in (0, 2)
    ]
    for copy in small + parts:
        copy.start()
    for copy in small:
        copy.wait()
    pressure = pressure_of(density, energy, material)
    gravity = from_points([double(mass_weight[q]) * (POINT_WEIGHT[q] * POINT_SCALE[q]) for q in range(27)])
    pressure_out[...] = pressure
    for n in range(9):
        gravity_out[n] = GRAVITY * gravity[9 + n]
    even = is_even()
    for comp in range(3):
        parts[2 * comp].wait()
        parts[2 * comp + 1].wait()
        values = []
        for n in range(18):
            value = force_of(geometry, 18 * comp + n, pressure)
            if comp == 2:
                value = value - GRAVITY * gravity[n if n < 9 else n + 9]
            field[18 * comp + n] = value
            values.append(value)
        for n in range(9):
            put(near, far, 9 * comp + n, values[n][:OWN], values[9 + n][:OWN], even)


def spread_velocity(velocity, out):
    rows = velocity[...].astype(BF16).reshape(48, velocity.shape[3])
    low = rows[:, :256]
    high = rows[:, 256:257].astype(F32)
    node = lax.broadcasted_iota(jnp.int32, (256, 384), 0)
    lane = lax.broadcasted_iota(jnp.int32, (256, 384), 1)
    pick = (node == 2 * (lane % 128) + lane // 128).astype(F32).astype(BF16)
    spread = jnp.dot(low, pick, preferred_element_type=F32)
    top = jnp.where(lane_of((48, 128)) == 127, high, 0.0)
    spread = jnp.concatenate([spread[:, :256], spread[:, 256:] + top], axis=1)
    row = lax.broadcasted_iota(jnp.int32, (96, 48), 0)
    source = lax.broadcasted_iota(jnp.int32, (96, 48), 1)
    wanted = (row // 16) * 8 + 2 * (row % 8) + (row // 8) % 2
    move = ((source == wanted) & (row % 8 < OWN)).astype(F32).astype(BF16)
    moved = jnp.dot(move, spread.astype(BF16), preferred_element_type=F32)
    for group in range(12):
        for c in range(3):
            out[3 * group + c] = moved[8 * group : 8 * group + 8, 128 * c : 128 * c + 128]


TOPS, WEIGHTS, SPEEDS, MESSAGE = 45, 46, 73, 79
SPEED_LANE = 32


def add_tops(values, comp, a, tops, sent):
    if comp == 2:
        return tops, sent
    row = lax.broadcasted_iota(jnp.int32, (8, 128), 0)
    lane = lane_of((8, 128))
    i = 3 * comp + a
    first, second, third = [values[3 * b + 2] for b in range(3)]
    for b, value in enumerate((first, second, third)):
        tops = to_lane(tops, lane, value, 3 * i + b)
    first = first + jnp.where(row % 2 == 1, pltpu.roll(third, 1, 0), 0.0)
    return tops, to_lane(sent, lane, first, 3 * i)


def fill_plane(values, comp, a, out, near, far, even_y):
    row = lax.broadcasted_iota(jnp.int32, (8, 128), 0)
    i = 3 * comp + a
    outer = []
    for c in range(2):
        first, second, third = [values[3 * b + c] for b in range(3)]
        for b, value in enumerate((first, second, third)):
            out[6 * i + 2 * b + c] = pltpu.roll(value, HALO, 0)
        first = first + jnp.where(row % 2 == 1, pltpu.roll(third, 1, 0), 0.0)
        for k, value in enumerate((first, second)):
            put(near, far, 4 * i + 2 * k + c, value[:HALO], value[HALO:OWN], even_y)
        outer.append(third)
    both = jnp.where(row % 2 == 1, outer[1], pltpu.roll(outer[0], 7, 0))
    put(near, far, 36 + i, both[:HALO], both[HALO:OWN], even_y)


def spread_kernel(
    geometry_in, velocity, pressure_in, gravity, mass_weight, spread, middle, near, far, geometry, sems
):
    parts = [
        pltpu.make_async_copy(
            geometry_in.at[pl.ds(108 * comp + 36, 36)], geometry.at[pl.ds(36 * comp, 36)], sems.at[comp]
        )
        for comp in range(3)
    ]
    for copy in parts:
        copy.start()
    even_y = is_even("brick")
    row = lax.broadcasted_iota(jnp.int32, (8, 128), 0)
    lane = lane_of((8, 128))
    spread_velocity(velocity, spread)
    tops = jnp.zeros((8, 128), F32)
    sent = tops
    for k in range(6):
        tops = to_lane(tops, lane, jnp.where(row == 0, spread[6 * k + 2], 0.0), SPEED_LANE + k)
    for q in range(27):
        put(near, far, WEIGHTS + q, mass_weight[q, :HALO], mass_weight[q, HALO:], even_y)
    for k in range(6):
        both = jnp.where(row == 0, spread[6 * k], pltpu.roll(spread[6 * k + 1], 1, 0))[:HALO].astype(BF16)
        near[SPEEDS + k] = both
        far[SPEEDS + k] = both
    pressure = pressure_in[...]
    for comp in range(3):
        parts[comp].wait()
        values = []
        for n in range(9):
            value = force_of(geometry, 9 * comp + n, pressure)
            values.append(value - gravity[n] if comp == 2 else value)
        tops, sent = add_tops(values, comp, 1, tops, sent)
        fill_plane(assemble_z(values, comp == 2), comp, 1, middle, near, far, even_y)
    middle[54] = tops
    middle[55] = sent


def rim_kernel(field, far, near, middle, near_in, far_in, out, near_out, far_out):
    even = is_even()
    even_y = is_even("brick")
    lane = lane_of((8, 128))
    tops, sent = middle[54], middle[55]
    for comp in range(3):
        i = 3 * comp + 1
        for k in range(6):
            out[6 * i + k] = middle[6 * i + k]
        for k in [4 * i, 4 * i + 1, 4 * i + 2, 4 * i + 3, 36 + i]:
            near_out[k] = near_in[k]
            far_out[k] = far_in[k]
        values = [field[18 * comp + n] for n in range(18)]
        for n in range(9):
            left, right = get(near, far, 9 * comp + n, even)
            values[n] = values[n] + double(left)
            values[9 + n] = values[9 + n] + double(right)
        for a, plane in ((0, values[:9]), (2, values[9:])):
            tops, sent = add_tops(plane, comp, a, tops, sent)
            fill_plane(assemble_z(plane, comp == 2), comp, a, out, near_out, far_out, even_y)
    out[54] = pltpu.roll(tops, HALO, 0)
    tops = jnp.where((lane % 3 == 0) & (lane < 27), sent, tops)
    put(near_out, far_out, TOPS, tops[:HALO], tops[HALO:OWN], even_y)
    for k in range(WEIGHTS, MESSAGE):
        near_out[k] = near_in[k]
        far_out[k] = far_in[k]


def send_planes(planes, near, far, even):
    lane = lane_of((8, 128))
    sides = [jnp.zeros((8, 128), F32)] * 2
    for comp in range(3):
        for b in range(2):
            left, right = [planes[comp][a + 3 * b : a + 3 * b + 3] for a in (0, 12)]
            for c in range(2):
                put(near, far, 4 * comp + 2 * b + c, left[c], right[c], even)
            sides = [to_lane(side, lane, plane[2], 2 * comp + b) for side, plane in zip(sides, (left, right))]
    put(near, far, 12, sides[0], sides[1], even)


def apply_mass(values, weight, wall):
    points = to_points(values)
    points = [points[q] * weight[q] for q in range(27)]
    return fold(from_points(points), wall)


def first_kernel(
    own, far_in, near_in, mass_weight, field, weight, image, near, far, rows
):
    even = is_even()
    even_y = is_even("brick")
    row = lax.broadcasted_iota(jnp.int32, (8, 128), 0)
    lane = lane_of((8, 128))
    mine = (row >= HALO) & (row < HALO + OWN)
    for k in range(SPEEDS):
        low, high = get(near_in, far_in, k, even_y)
        rows[k, :HALO] = low
        rows[k, HALO + OWN :] = high
        if k >= WEIGHTS:
            rows[k, HALO : HALO + OWN] = mass_weight[k - WEIGHTS]
    for q in range(27):
        weight[q] = rows[WEIGHTS + q] * (POINT_WEIGHT[q] * POINT_SCALE[q] ** 2)
    edge = (row == 1) | (row == 7)
    tops = jnp.where((lane % 3 == 2) & ~edge, 0.0, rows[TOPS])
    tops = jnp.where(mine, own[54], tops)
    tops = tops + jnp.where(lane % 3 == 0, pltpu.roll(pltpu.roll(tops, 126, 1), 1, 0), 0.0)
    planes = []
    for comp in range(3):
        values = []
        for a in range(3):
            i = 3 * comp + a
            columns = []
            for c in range(2):
                k = 2 * i + c
                halos = [rows[4 * i + c], rows[4 * i + 2 + c], rows[36 + k // 2]]
                halos[2] = jnp.where(edge, halos[2] if k % 2 == 1 else pltpu.roll(halos[2], 1, 0), 0.0)
                column = [jnp.where(mine, own[6 * i + 2 * b + c], halos[b]) for b in range(3)]
                columns.append([column[0] + pltpu.roll(column[2], 1, 0), column[1]])
            for b in range(2):
                values += [columns[0][b], columns[1][b], pltpu.roll(tops, 127 - 3 * i - b, 1)]
        for n in range(18):
            field[18 * comp + n] = values[n]
        values = apply_mass(unfold(values), weight, comp == 2)
        for n in range(18):
            image[18 * comp + n] = values[n]
        planes.append(values)
    send_planes(planes, near, far, even)


def speed_kernel(far_in, near_in, spread, speeds, plane_out):
    even_y = is_even("brick")
    row = lax.broadcasted_iota(jnp.int32, (8, 128), 0)
    lane = lane_of((8, 128))
    edge_tops = get(near_in, far_in, TOPS, even_y)[1]
    edge_tops = jnp.concatenate([edge_tops] * 4, axis=0)
    plane = []
    tops = jnp.zeros((8, 128), F32)
    for comp in range(3):
        for a in range(2):
            k = 2 * comp + a
            speed = [spread[6 * k + n] for n in range(6)]
            beyond = get(near_in, far_in, SPEEDS + k, even_y)[1]
            beyond = [beyond[c : c + 1] for c in range(2)]
            for c in range(2):
                speed.append(jnp.where(row == OWN - 1, beyond[c], pltpu.roll(speed[c], 7, 0)))
            third = third_along_z(jnp.broadcast_to(beyond[0], (8, 128)), edge_tops, lane, SPEED_LANE + k)[0:1]
            speed.append(jnp.where(row == OWN - 1, third, pltpu.roll(speed[2], 7, 0)))
            for n in range(9):
                speeds[18 * comp + 9 * a + n] = speed[n]
            if a == 0:
                for b in range(3):
                    plane += speed[3 * b : 3 * b + 2]
                    tops = to_lane(tops, lane, speed[3 * b + 2], SPEED_LANE + 3 * comp + b)
    for k in range(9):
        plane_out[k] = jnp.where(row < OWN, plane[2 * k], pltpu.roll(plane[2 * k + 1], OWN, 0))
    plane_out[9] = tops


def send_own(planes, speeds, near, far, even):
    row = lax.broadcasted_iota(jnp.int32, (8, 128), 0)
    lane = lane_of((8, 128))
    sides = [speeds[9], jnp.zeros((8, 128), F32)]
    after = [jnp.zeros((8, 128), F32)] * 2
    for comp in range(3):
        for b in range(2):
            both = []
            for side, a in enumerate((0, 12)):
                plane = planes[comp][a + 3 * b : a + 3 * b + 3]
                both.append(jnp.where(row < OWN, pltpu.roll(plane[0], 6, 0), pltpu.roll(plane[1], 2, 0)))
                sides[side] = to_lane(sides[side], lane, plane[2], 2 * comp + b)
                if b == 0:
                    for c in range(2):
                        k = 2 * comp + c
                        after[side] = jnp.where(row == k, pltpu.roll(plane[c], (k + 2) % 8, 0), after[side])
            put(near, far, 2 * comp + b, both[0], both[1], even)
    put(near, far, 6, after[0], after[1], even)
    put(near, far, 7, sides[0], sides[1], even)
    for k in range(9):
        near[8 + k] = speeds[k].astype(BF16)
        far[8 + k] = speeds[k].astype(BF16)


def take_planes(image, near, far, comp, even):
    def read(b):
        tiles = [get(near, far, 4 * comp + 2 * b + c, even) for c in range(2)]
        return [[tile[side] for tile in tiles] for side in range(2)]

    return add_planes(image, read, get(near, far, 12, even), comp)


def take_own(image, near, far, comp, even):
    row = lax.broadcasted_iota(jnp.int32, (8, 128), 0)
    after = get(near, far, 6, even)

    def read(b):
        sides = []
        for side, both in enumerate(get(near, far, 2 * comp + b, even)):
            plane = [pltpu.roll(both, 2, 0), pltpu.roll(both, 6, 0)]
            if b == 0:
                for c in range(2):
                    k = 2 * comp + c
                    plane[c] = jnp.where(row == 6, pltpu.roll(after[side], 6 - k, 0), plane[c])
            sides.append(plane)
        return sides

    return add_planes(image, read, get(near, far, 7, even), comp)


def add_planes(image, read, tops, comp):
    values = [image[18 * comp + n] for n in range(18)]
    for b in range(2):
        for a, plane, top in zip((0, 12), read(b), tops):
            n = a + 3 * b
            for c in range(2):
                values[n + c] = values[n + c] + plane[c]
            values[n + 2] = values[n + 2] + pltpu.roll(top, 127 - 2 * comp - b, 1)
    return values


def second_kernel(image, far_in, near_in, weight, speeds, field, image_out, near, far):
    even = is_even()
    planes = []
    for comp in range(3):
        values = take_planes(image, near_in, far_in, comp, even)
        for n in range(18):
            field[18 * comp + n] = values[n]
        values = apply_mass(unfold(values), weight, comp == 2)
        for n in range(18):
            image_out[18 * comp + n] = values[n]
        planes.append(values)
    send_own(planes, speeds, near, far, even)


def work_kernel(geometry, density, energy, material, energy_mass, speeds, far, near, out):
    even = is_even()
    pressure = pressure_of(density, energy, material)
    work = jnp.zeros_like(pressure)
    row = lax.broadcasted_iota(jnp.int32, (8, 128), 0)
    lane = lane_of((8, 128))
    tops = get(near, far, 7, even)[1]
    for comp in range(3):
        speed = [speeds[18 * comp + n] for n in range(18)]
        for b in range(3):
            both = get(near, far, 8 + 3 * comp + b, even)[1]
            speed += [both, pltpu.roll(both, OWN, 0)]
            speed.append(third_along_z(both, tops, lane, SPEED_LANE + 3 * comp + b))
        for n in range(27):
            value = jnp.where(row < OWN, speed[n], pltpu.roll(speed[n], OWN, 0))
            work = work + geometry[pl.ds(4 * (27 * comp + n), 4)].astype(F32) * value[None]
    out[...] = energy[...] + HALF_STEP * pressure * work / energy_mass[...]


def dot_owned(first, second, comp, total):
    last = lane_of((8, 128)) == 127
    for a in range(2):
        for b in range(2):
            n = 18 * comp + 6 * a + 3 * b
            total = total + first[n] * second[n] + first[n + 1] * second[n + 1]
            total = total + jnp.where(last, first[n + 2] * second[n + 2], 0.0)
    return total


def product_kernel(zeroth, first, products):
    for k, (one, other) in enumerate([(zeroth, zeroth), (zeroth, first), (first, first)]):
        total = jnp.zeros((8, 128), F32)
        for comp in range(3):
            total = dot_owned(one, other, comp, total)
        products[k] = total


def moment_kernel(image, far, near, weight, first, products, second, moments):
    zero = jnp.zeros((8, 128), F32)
    cross, norm = zero, zero
    quadratic = [zero] * 3
    even = is_even()
    for comp in range(3):
        values = take_own(image, near, far, comp, even)
        for n in range(18):
            second[18 * comp + n] = values[n]
        values_at = {18 * comp + n: values[n] for n in range(18)}
        cross = dot_owned(first, values_at, comp, cross)
        norm = dot_owned(values_at, values_at, comp, norm)
        points = to_points(unfold(values))
        for q in range(27):
            quadratic[q % 3] = quadratic[q % 3] + points[q] * points[q] * weight[q]
    quadratic = quadratic[0] + quadratic[1] + quadratic[2]
    row = lax.broadcasted_iota(jnp.int32, (8, 128), 0)
    mine = (row >= HALO) & (row < HALO + OWN)
    sums = jnp.zeros((8, 128), F32)
    for k, total in enumerate([products[0], products[1], products[2], cross, norm, quadratic]):
        total = jnp.sum(jnp.where(mine, total, 0.0), axis=0, keepdims=True)
        sums = jnp.where(row == k, total, sums)
    sums = jnp.sum(sums, axis=1, keepdims=True)
    line = jnp.sum(jnp.where(lane_of((8, 128)) == row, sums, 0.0), axis=0, keepdims=True)
    moments[...] = jnp.broadcast_to(line, moments.shape)


def solve(moments):
    def ratio(top, pivot, scale):
        good = pivot > 1e-7 * scale
        return jnp.where(good, top / jnp.where(good, pivot, 1.0), 0.0)

    m = moments
    l10 = ratio(m[2], m[1], 0.0)
    l20 = ratio(m[3], m[1], 0.0)
    d1 = m[3] - l10 * m[2]
    e1 = m[4] - l20 * m[2]
    l21 = ratio(e1, d1, m[3])
    d2 = m[5] - l20 * m[3] - l21 * e1
    y1 = m[1] - l10 * m[0]
    y2 = m[2] - l20 * m[0] - l21 * y1
    c2 = ratio(y2, d2, m[5])
    c1 = ratio(y1, d1, m[3]) - l21 * c2
    c0 = ratio(m[0], m[1], 0.0) - l10 * c1 - l20 * c2
    return c0, c1, c2


def halves(x):
    high = x.astype(BF16)
    return high, (x - high.astype(F32)).astype(BF16)


def nodal_kernel(zeroth, first, second, out):
    row = lax.broadcasted_iota(jnp.int32, (48, 96), 0)
    source = lax.broadcasted_iota(jnp.int32, (48, 96), 1)
    wanted = (row // 8) * 16 + (row % 2) * 8 + HALO + (row % 8) // 2
    move = (source == wanted).astype(F32).astype(BF16)
    source = lax.broadcasted_iota(jnp.int32, (384, 384), 0)
    node = lax.broadcasted_iota(jnp.int32, (384, 384), 1)
    wanted = jnp.where(node < 256, (node % 2) * 128 + node // 2, 383)
    place = ((source == wanted) & (node <= 256)).astype(F32).astype(BF16)
    for k, field in enumerate((zeroth, first, second)):
        blocks = []
        for c in range(3):
            column = []
            for comp in range(3):
                for a in range(2):
                    for b in range(2):
                        column.append(field[18 * comp + 6 * a + 3 * b + c])
            blocks.append(jnp.concatenate(column, axis=0))
        high, low = halves(jnp.concatenate(blocks, axis=1))
        moved = jnp.dot(move, high, preferred_element_type=F32) + jnp.dot(move, low, preferred_element_type=F32)
        high, low = halves(moved)
        out[k] = jnp.dot(high, place, preferred_element_type=F32) + jnp.dot(low, place, preferred_element_type=F32)


def last_kernel(moments, nodal, velocity, out):
    line = jnp.sum(moments[...], axis=0, keepdims=True)
    lane = lane_of((1, 128))
    mu = [jnp.sum(jnp.where(lane == k, line, 0.0), axis=1, keepdims=True) for k in range(6)]
    c0, c1, c2 = [HALF_STEP * c for c in solve(mu)]
    for comp in range(3):
        for x in range(2):
            start = 16 * comp + 8 * x
            part = [nodal[k, pl.ds(start, 8), : velocity.shape[3]] for k in range(3)]
            out[comp, x] = velocity[comp, x] + (c0 * part[0] + c1 * part[1] + c2 * part[2])


VMEM = pl.BlockSpec(memory_space=pltpu.VMEM)


HBM = pl.BlockSpec(memory_space=pltpu.HBM)


def call(kernel, outs, *args, scratch=(), flops=100000, in_hbm=0, dtypes=None):
    shapes = [jax.ShapeDtypeStruct(shape, dtype) for shape, dtype in zip(outs, dtypes or [F32] * len(outs))]
    moved = sum(a.size * a.dtype.itemsize for a in args) + sum(4 * int(np.prod(s)) for s in outs)
    return pl.pallas_call(
        kernel,
        out_shape=shapes,
        in_specs=[HBM] * in_hbm + [VMEM] * (len(args) - in_hbm),
        out_specs=[VMEM] * len(outs),
        scratch_shapes=list(scratch),
        compiler_params=pltpu.CompilerParams(vmem_limit_bytes=32 * 1024 * 1024),
        cost_estimate=pl.CostEstimate(flops=flops, bytes_accessed=moved, transcendentals=0),
        name=kernel.__name__,
    )(*args)


def swap(near, far, axis="slab"):
    count = lax.axis_size(axis)
    far = lax.ppermute(far, axis, [(i, (i + (1 if i % 2 else -1)) % count) for i in range(count)])
    near = lax.ppermute(near, axis, [(i, i + (-1 if i % 2 else 1)) for i in range(count)])
    return near, far


def local(velocity, energy, density, material, geometry, mass_weight, energy_mass):
    tile = (4, 128)
    full = (8, 128)
    geometry = geometry.reshape((324,) + full)
    density = density.reshape((4,) + full)
    energy = energy.reshape((4,) + full)
    energy_mass = energy_mass.reshape((4,) + full)
    mass_weight = mass_weight.reshape((27,) + tile)
    material = material.reshape(tile)
    pair = (2, 128)
    devices = lax.axis_size("slab") * lax.axis_size("brick")

    stays = [
        pltpu.with_memory_space_constraint(x, pltpu.HBM) for x in (geometry, density, energy, material, mass_weight)
    ]
    force, near, far, pressure, gravity = call(
        force_kernel,
        [(54,) + full, (27,) + tile, (27,) + tile, (4,) + full, (9,) + full],
        *stays,
        scratch=[
            pltpu.VMEM((216,) + full, BF16),
            pltpu.VMEM((4,) + full, F32),
            pltpu.VMEM((4,) + full, F32),
            pltpu.VMEM(tile, jnp.int32),
            pltpu.VMEM((27,) + tile, F32),
            pltpu.SemaphoreType.DMA((10,)),
        ],
        in_hbm=5,
        dtypes=[F32, BF16, BF16, F32, F32],
    )
    spread, middle, near_part, far_part = call(
        spread_kernel,
        [(36,) + full, (56,) + full, (MESSAGE,) + pair, (MESSAGE,) + pair],
        stays[0], velocity, pressure, gravity, mass_weight,
        scratch=[pltpu.VMEM((108,) + full, BF16), pltpu.SemaphoreType.DMA((3,))],
        in_hbm=1,
        dtypes=[F32, F32, BF16, BF16],
    )
    near, far = swap(near, far)
    own, near, far = call(
        rim_kernel,
        [(55,) + full, (MESSAGE,) + pair, (MESSAGE,) + pair],
        force, far, near, middle, near_part, far_part,
        dtypes=[F32, BF16, BF16],
    )
    near_rim, far_rim = swap(near, far, "brick")
    zeroth, weight, image, near, far = call(
        first_kernel,
        [(54,) + full, (27,) + full, (54,) + full, (13,) + full, (13,) + full],
        own, far_rim, near_rim, mass_weight,
        scratch=[pltpu.VMEM((SPEEDS,) + full, F32)],
        dtypes=[F32, F32, F32, BF16, BF16],
    )
    near, far = swap(near, far)
    speeds, plane = call(speed_kernel, [(54,) + full, (10,) + full], far_rim, near_rim, spread)
    first, image, near, far = call(
        second_kernel,
        [(54,) + full, (54,) + full, (17,) + full, (17,) + full],
        image, far, near, weight, plane,
        dtypes=[F32, F32, BF16, BF16],
    )
    near, far = swap(near, far)
    (energy_half,) = call(
        work_kernel, [(4,) + full], geometry, density, energy, material, energy_mass, speeds, far, near
    )
    (products,) = call(product_kernel, [(3,) + full], zeroth, first)
    second, moments = call(
        moment_kernel, [(54,) + full, (devices, 128)], image, far, near, weight, first, products
    )
    moments = lax.all_to_all(moments, ("slab", "brick"), 0, 0, tiled=True)
    (nodal,) = call(nodal_kernel, [(3, 48, 384)], zeroth, first, second)
    (velocity_half,) = call(last_kernel, [velocity.shape], moments, nodal, velocity)
    return (velocity_half, energy_half.reshape(8, 1, 4, 128))


def solution(mesh):
    nodes = P(None, "slab", "brick", None)
    return jax.shard_map(
        local,
        mesh=mesh,
        in_specs=(
            nodes,
            nodes,
            nodes,
            P("slab", "brick", None),
            P(None, None, "slab", "brick", None),
            nodes,
            nodes,
        ),
        out_specs=(nodes, nodes),
        check_vma=False,
    )
```

```python
import jax
import jax.numpy as jnp
import numpy as np
from jax import lax
from jax.experimental import pallas as pl
from jax.experimental.pallas import tpu as pltpu
from jax.sharding import PartitionSpec as P

HALF_STEP = 0.25
GRAVITY = 1.0
F32 = jnp.float32
BF16 = jnp.bfloat16

OFFSET = float(np.sqrt(0.6) / 2.0)
SIDE = 0.3
MIDDLE = 0.4
ODD, EVEN = OFFSET / SIDE, MIDDLE / SIDE
LINE_WEIGHTS = (5.0 / 18.0, 8.0 / 18.0, 5.0 / 18.0)
POINT_WEIGHT = [a * b * c for a in LINE_WEIGHTS for b in LINE_WEIGHTS for c in LINE_WEIGHTS]
POINT_SCALE = [a * b * c for a in (SIDE, 1.0, SIDE) for b in (SIDE, 1.0, SIDE) for c in (SIDE, 1.0, SIDE)]
OWN = 4
HALO = 2


def lines(direction):
    stride = (9, 3, 1)[direction]
    return [(n, n + stride, n + 2 * stride) for n in range(27) if (n // stride) % 3 == 0]


def to_points(values):
    values = list(values)
    for direction in range(3):
        for i, j, k in lines(direction):
            even = (values[i] + values[k]) + EVEN * values[j]
            odd = ODD * (values[i] - values[k])
            values[i], values[k] = even + odd, even - odd
    return values


def from_points(values):
    values = list(values)
    for direction in range(3):
        for i, j, k in lines(direction):
            total = values[i] + values[k]
            odd = ODD * (values[i] - values[k])
            values[i], values[k] = total + odd, total - odd
            values[j] = values[j] + EVEN * total
    return values


def lane_of(shape):
    return lax.broadcasted_iota(jnp.int32, shape, len(shape) - 1)


def assemble_z(values, wall):
    values = list(values)
    lane = lane_of(values[0].shape)
    first, last = lane == 0, lane == 127
    for i, k in [(n, n + 2) for n in range(0, len(values), 3)]:
        total = values[i] + jnp.where(first, 0.0, pltpu.roll(values[k], 1, 1))
        top = values[k]
        if wall:
            total = jnp.where(first, 0.0, total)
            top = jnp.zeros_like(top)
        values[i] = total
        values[k] = jnp.where(last, top, pltpu.roll(total, 127, 1))
    return values


def fold(values, wall):
    lane = lane_of(values[0].shape)
    folded = []
    for a in (0, 9, 18):
        columns = [[values[a + c] + pltpu.roll(values[a + 6 + c], 1, 0), values[a + 3 + c]] for c in range(3)]
        for b in range(2):
            first = columns[0][b] + jnp.where(lane == 0, 0.0, pltpu.roll(columns[2][b], 1, 1))
            if wall:
                first = jnp.where(lane == 0, 0.0, first)
            folded += [first, columns[1][b], jnp.zeros_like(first) if wall else columns[2][b]]
    return folded


def unfold(folded):
    lane = lane_of(folded[0].shape)
    values = []
    for a in (0, 6, 12):
        planes = []
        for b in (0, 3):
            first, second, top = folded[a + b : a + b + 3]
            planes.append([first, second, jnp.where(lane == 127, top, pltpu.roll(first, 127, 1))])
        planes.append([pltpu.roll(value, 7, 0) for value in planes[0]])
        values += planes[0] + planes[1] + planes[2]
    return values


def is_even(axis="slab"):
    return lax.axis_index(axis) % 2 == 0


def put(near, far, slot, left, right, even):
    near[slot] = jnp.where(even, right, left).astype(BF16)
    far[slot] = jnp.where(even, left, right).astype(BF16)


def get(near, far, slot, even):
    one, other = near[slot].astype(F32), far[slot].astype(F32)
    return jnp.where(even, other, one), jnp.where(even, one, other)


def pressure_of(density, energy, material):
    gamma = jnp.where(material[...] == 0, 2.0 / 3.0, 0.4).astype(F32)
    gamma = jnp.concatenate([gamma, gamma], axis=0)
    return (gamma[None] * density[...] * energy[...]).astype(BF16).astype(F32)


def to_lane(tile, lane, values, slot):
    return jnp.where(lane == slot, pltpu.roll(values, slot + 1, 1), tile)


def third_along_z(values, tops, lane, slot):
    return jnp.where(lane == 127, pltpu.roll(tops, 127 - slot, 1), pltpu.roll(values, 127, 1))


def double(values):
    return jnp.concatenate([values, values], axis=0)


def force_of(geometry, r, pressure):
    value = jnp.sum(geometry[pl.ds(4 * r, 4)].astype(F32) * pressure, axis=0)
    return -(value + pltpu.roll(value, OWN, 0))


def force_kernel(
    geometry_in, density_in, energy_in, material_in, mass_weight_in,
    field, near, far, pressure_out, gravity_out,
    geometry, density, energy, material, mass_weight, sems,
):
    small = [
        pltpu.make_async_copy(source, target, sems.at[6 + i])
        for i, (source, target) in enumerate(
            [(density_in, density), (energy_in, energy), (material_in, material), (mass_weight_in, mass_weight)]
        )
    ]
    parts = [
        pltpu.make_async_copy(
            geometry_in.at[pl.ds(108 * comp + 36 * a, 36)], geometry.at[pl.ds(72 * comp + 18 * a, 36)], sems.at[2 * comp + a // 2]
        )
        for comp in range(3)
        for a in (0, 2)
    ]
    for copy in small + parts:
        copy.start()
    for copy in small:
        copy.wait()
    pressure = pressure_of(density, energy, material)
    gravity = from_points([double(mass_weight[q]) * (POINT_WEIGHT[q] * POINT_SCALE[q]) for q in range(27)])
    pressure_out[...] = pressure
    for n in range(9):
        gravity_out[n] = GRAVITY * gravity[9 + n]
    even = is_even()
    for comp in range(3):
        parts[2 * comp].wait()
        parts[2 * comp + 1].wait()
        values = []
        for n in range(18):
            value = force_of(geometry, 18 * comp + n, pressure)
            if comp == 2:
                value = value - GRAVITY * gravity[n if n < 9 else n + 9]
            field[18 * comp + n] = value
            values.append(value)
        for n in range(9):
            put(near, far, 9 * comp + n, values[n][:OWN], values[9 + n][:OWN], even)


def spread_velocity(velocity, out):
    rows = velocity[...].astype(BF16).reshape(48, velocity.shape[3])
    low = rows[:, :256]
    high = rows[:, 256:257].astype(F32)
    node = lax.broadcasted_iota(jnp.int32, (256, 384), 0)
    lane = lax.broadcasted_iota(jnp.int32, (256, 384), 1)
    pick = (node == 2 * (lane % 128) + lane // 128).astype(F32).astype(BF16)
    spread = jnp.dot(low, pick, preferred_element_type=F32)
    top = jnp.where(lane_of((48, 128)) == 127, high, 0.0)
    spread = jnp.concatenate([spread[:, :256], spread[:, 256:] + top], axis=1)
    row = lax.broadcasted_iota(jnp.int32, (96, 48), 0)
    source = lax.broadcasted_iota(jnp.int32, (96, 48), 1)
    wanted = (row // 16) * 8 + 2 * (row % 8) + (row // 8) % 2
    move = ((source == wanted) & (row % 8 < OWN)).astype(F32).astype(BF16)
    moved = jnp.dot(move, spread.astype(BF16), preferred_element_type=F32)
    for group in range(12):
        for c in range(3):
            out[3 * group + c] = moved[8 * group : 8 * group + 8, 128 * c : 128 * c + 128]


TOPS, WEIGHTS, SPEEDS, MESSAGE = 45, 46, 73, 79
SPEED_LANE = 32


def add_tops(values, comp, a, tops, sent):
    if comp == 2:
        return tops, sent
    row = lax.broadcasted_iota(jnp.int32, (8, 128), 0)
    lane = lane_of((8, 128))
    i = 3 * comp + a
    first, second, third = [values[3 * b + 2] for b in range(3)]
    for b, value in enumerate((first, second, third)):
        tops = to_lane(tops, lane, value, 3 * i + b)
    first = first + jnp.where(row % 2 == 1, pltpu.roll(third, 1, 0), 0.0)
    return tops, to_lane(sent, lane, first, 3 * i)


def fill_plane(values, comp, a, out, near, far, even_y):
    row = lax.broadcasted_iota(jnp.int32, (8, 128), 0)
    i = 3 * comp + a
    outer = []
    for c in range(2):
        first, second, third = [values[3 * b + c] for b in range(3)]
        for b, value in enumerate((first, second, third)):
            out[6 * i + 2 * b + c] = pltpu.roll(value, HALO, 0)
        first = first + jnp.where(row % 2 == 1, pltpu.roll(third, 1, 0), 0.0)
        for k, value in enumerate((first, second)):
            put(near, far, 4 * i + 2 * k + c, value[:HALO], value[HALO:OWN], even_y)
        outer.append(third)
    both = jnp.where(row % 2 == 1, outer[1], pltpu.roll(outer[0], 7, 0))
    put(near, far, 36 + i, both[:HALO], both[HALO:OWN], even_y)


def spread_kernel(
    geometry_in, velocity, pressure_in, gravity, mass_weight, spread, middle, near, far, geometry, sems
):
    parts = [
        pltpu.make_async_copy(
            geometry_in.at[pl.ds(108 * comp + 36, 36)], geometry.at[pl.ds(36 * comp, 36)], sems.at[comp]
        )
        for comp in range(3)
    ]
    for copy in parts:
        copy.start()
    even_y = is_even("brick")
    row = lax.broadcasted_iota(jnp.int32, (8, 128), 0)
    lane = lane_of((8, 128))
    spread_velocity(velocity, spread)
    tops = jnp.zeros((8, 128), F32)
    sent = tops
    for k in range(6):
        tops = to_lane(tops, lane, jnp.where(row == 0, spread[6 * k + 2], 0.0), SPEED_LANE + k)
    for q in range(27):
        put(near, far, WEIGHTS + q, mass_weight[q, :HALO], mass_weight[q, HALO:], even_y)
    for k in range(6):
        both = jnp.where(row == 0, spread[6 * k], pltpu.roll(spread[6 * k + 1], 1, 0))[:HALO].astype(BF16)
        near[SPEEDS + k] = both
        far[SPEEDS + k] = both
    pressure = pressure_in[...]
    for comp in range(3):
        parts[comp].wait()
        values = []
        for n in range(9):
            value = force_of(geometry, 9 * comp + n, pressure)
            values.append(value - gravity[n] if comp == 2 else value)
        tops, sent = add_tops(values, comp, 1, tops, sent)
        fill_plane(assemble_z(values, comp == 2), comp, 1, middle, near, far, even_y)
    middle[54] = tops
    middle[55] = sent


def rim_kernel(field, far, near, middle, near_in, far_in, out, near_out, far_out):
    even = is_even()
    even_y = is_even("brick")
    lane = lane_of((8, 128))
    tops, sent = middle[54], middle[55]
    for comp in range(3):
        i = 3 * comp + 1
        for k in range(6):
            out[6 * i + k] = middle[6 * i + k]
        for k in [4 * i, 4 * i + 1, 4 * i + 2, 4 * i + 3, 36 + i]:
            near_out[k] = near_in[k]
            far_out[k] = far_in[k]
        values = [field[18 * comp + n] for n in range(18)]
        for n in range(9):
            left, right = get(near, far, 9 * comp + n, even)
            values[n] = values[n] + double(left)
            values[9 + n] = values[9 + n] + double(right)
        for a, plane in ((0, values[:9]), (2, values[9:])):
            tops, sent = add_tops(plane, comp, a, tops, sent)
            fill_plane(assemble_z(plane, comp == 2), comp, a, out, near_out, far_out, even_y)
    out[54] = pltpu.roll(tops, HALO, 0)
    tops = jnp.where((lane % 3 == 0) & (lane < 27), sent, tops)
    put(near_out, far_out, TOPS, tops[:HALO], tops[HALO:OWN], even_y)
    for k in range(WEIGHTS, MESSAGE):
        near_out[k] = near_in[k]
        far_out[k] = far_in[k]


def send_planes(planes, near, far, even):
    lane = lane_of((8, 128))
    sides = [jnp.zeros((8, 128), F32)] * 2
    for comp in range(3):
        for b in range(2):
            left, right = [planes[comp][a + 3 * b : a + 3 * b + 3] for a in (0, 12)]
            for c in range(2):
                put(near, far, 4 * comp + 2 * b + c, left[c], right[c], even)
            sides = [to_lane(side, lane, plane[2], 2 * comp + b) for side, plane in zip(sides, (left, right))]
    put(near, far, 12, sides[0], sides[1], even)


def apply_mass(values, weight, wall):
    points = to_points(values)
    points = [points[q] * weight[q] for q in range(27)]
    return fold(from_points(points), wall)


def first_kernel(
    own, far_in, near_in, mass_weight, field, weight, image, near, far, rows
):
    even = is_even()
    even_y = is_even("brick")
    row = lax.broadcasted_iota(jnp.int32, (8, 128), 0)
    lane = lane_of((8, 128))
    mine = (row >= HALO) & (row < HALO + OWN)
    for k in range(SPEEDS):
        low, high = get(near_in, far_in, k, even_y)
        rows[k, :HALO] = low
        rows[k, HALO + OWN :] = high
        if k >= WEIGHTS:
            rows[k, HALO : HALO + OWN] = mass_weight[k - WEIGHTS]
    for q in range(27):
        weight[q] = rows[WEIGHTS + q] * (POINT_WEIGHT[q] * POINT_SCALE[q] ** 2)
    edge = (row == 1) | (row == 7)
    tops = jnp.where((lane % 3 == 2) & ~edge, 0.0, rows[TOPS])
    tops = jnp.where(mine, own[54], tops)
    tops = tops + jnp.where(lane % 3 == 0, pltpu.roll(pltpu.roll(tops, 126, 1), 1, 0), 0.0)
    planes = []
    for comp in range(3):
        values = []
        for a in range(3):
            i = 3 * comp + a
            columns = []
            for c in range(2):
                k = 2 * i + c
                halos = [rows[4 * i + c], rows[4 * i + 2 + c], rows[36 + k // 2]]
                halos[2] = jnp.where(edge, halos[2] if k % 2 == 1 else pltpu.roll(halos[2], 1, 0), 0.0)
                column = [jnp.where(mine, own[6 * i + 2 * b + c], halos[b]) for b in range(3)]
                columns.append([column[0] + pltpu.roll(column[2], 1, 0), column[1]])
            for b in range(2):
                values += [columns[0][b], columns[1][b], pltpu.roll(tops, 127 - 3 * i - b, 1)]
        for n in range(18):
            field[18 * comp + n] = values[n]
        values = apply_mass(unfold(values), weight, comp == 2)
        for n in range(18):
            image[18 * comp + n] = values[n]
        planes.append(values)
    send_planes(planes, near, far, even)


def speed_kernel(far_in, near_in, spread, speeds, plane_out):
    even_y = is_even("brick")
    row = lax.broadcasted_iota(jnp.int32, (8, 128), 0)
    lane = lane_of((8, 128))
    edge_tops = get(near_in, far_in, TOPS, even_y)[1]
    edge_tops = jnp.concatenate([edge_tops] * 4, axis=0)
    plane = []
    tops = jnp.zeros((8, 128), F32)
    for comp in range(3):
        for a in range(2):
            k = 2 * comp + a
            speed = [spread[6 * k + n] for n in range(6)]
            beyond = get(near_in, far_in, SPEEDS + k, even_y)[1]
            beyond = [beyond[c : c + 1] for c in range(2)]
            for c in range(2):
                speed.append(jnp.where(row == OWN - 1, beyond[c], pltpu.roll(speed[c], 7, 0)))
            third = third_along_z(jnp.broadcast_to(beyond[0], (8, 128)), edge_tops, lane, SPEED_LANE + k)[0:1]
            speed.append(jnp.where(row == OWN - 1, third, pltpu.roll(speed[2], 7, 0)))
            for n in range(9):
                speeds[18 * comp + 9 * a + n] = speed[n]
            if a == 0:
                for b in range(3):
                    plane += speed[3 * b : 3 * b + 2]
                    tops = to_lane(tops, lane, speed[3 * b + 2], SPEED_LANE + 3 * comp + b)
    for k in range(9):
        plane_out[k] = jnp.where(row < OWN, plane[2 * k], pltpu.roll(plane[2 * k + 1], OWN, 0))
    plane_out[9] = tops


def send_own(planes, speeds, near, far, even):
    row = lax.broadcasted_iota(jnp.int32, (8, 128), 0)
    lane = lane_of((8, 128))
    sides = [speeds[9], jnp.zeros((8, 128), F32)]
    after = [jnp.zeros((8, 128), F32)] * 2
    for comp in range(3):
        for b in range(2):
            both = []
            for side, a in enumerate((0, 12)):
                plane = planes[comp][a + 3 * b : a + 3 * b + 3]
                both.append(jnp.where(row < OWN, pltpu.roll(plane[0], 6, 0), pltpu.roll(plane[1], 2, 0)))
                sides[side] = to_lane(sides[side], lane, plane[2], 2 * comp + b)
                if b == 0:
                    for c in range(2):
                        k = 2 * comp + c
                        after[side] = jnp.where(row == k, pltpu.roll(plane[c], (k + 2) % 8, 0), after[side])
            put(near, far, 2 * comp + b, both[0], both[1], even)
    put(near, far, 6, after[0], after[1], even)
    put(near, far, 7, sides[0], sides[1], even)
    for k in range(9):
        near[8 + k] = speeds[k].astype(BF16)
        far[8 + k] = speeds[k].astype(BF16)


def take_planes(image, near, far, comp, even):
    def read(b):
        tiles = [get(near, far, 4 * comp + 2 * b + c, even) for c in range(2)]
        return [[tile[side] for tile in tiles] for side in range(2)]

    return add_planes(image, read, get(near, far, 12, even), comp)


def take_own(image, near, far, comp, even):
    row = lax.broadcasted_iota(jnp.int32, (8, 128), 0)
    after = get(near, far, 6, even)

    def read(b):
        sides = []
        for side, both in enumerate(get(near, far, 2 * comp + b, even)):
            plane = [pltpu.roll(both, 2, 0), pltpu.roll(both, 6, 0)]
            if b == 0:
                for c in range(2):
                    k = 2 * comp + c
                    plane[c] = jnp.where(row == 6, pltpu.roll(after[side], 6 - k, 0), plane[c])
            sides.append(plane)
        return sides

    return add_planes(image, read, get(near, far, 7, even), comp)


def add_planes(image, read, tops, comp):
    values = [image[18 * comp + n] for n in range(18)]
    for b in range(2):
        for a, plane, top in zip((0, 12), read(b), tops):
            n = a + 3 * b
            for c in range(2):
                values[n + c] = values[n + c] + plane[c]
            values[n + 2] = values[n + 2] + pltpu.roll(top, 127 - 2 * comp - b, 1)
    return values


def second_kernel(image, far_in, near_in, weight, speeds, field, image_out, near, far):
    even = is_even()
    planes = []
    for comp in range(3):
        values = take_planes(image, near_in, far_in, comp, even)
        for n in range(18):
            field[18 * comp + n] = values[n]
        values = apply_mass(unfold(values), weight, comp == 2)
        for n in range(18):
            image_out[18 * comp + n] = values[n]
        planes.append(values)
    send_own(planes, speeds, near, far, even)


def work_kernel(geometry, pressure_in, energy, energy_mass, speeds, far, near, out):
    even = is_even()
    pressure = pressure_in[...]
    work = jnp.zeros_like(pressure)
    row = lax.broadcasted_iota(jnp.int32, (8, 128), 0)
    lane = lane_of((8, 128))
    tops = get(near, far, 7, even)[1]
    for comp in range(3):
        speed = [speeds[18 * comp + n] for n in range(18)]
        for b in range(3):
            both = get(near, far, 8 + 3 * comp + b, even)[1]
            speed += [both, pltpu.roll(both, OWN, 0)]
            speed.append(third_along_z(both, tops, lane, SPEED_LANE + 3 * comp + b))
        for n in range(27):
            value = jnp.where(row < OWN, speed[n], pltpu.roll(speed[n], OWN, 0))
            work = work + geometry[pl.ds(4 * (27 * comp + n), 4)].astype(F32) * value[None]
    out[...] = energy[...] + HALF_STEP * pressure * work / energy_mass[...]


def dot_owned(first, second, comp, total):
    last = lane_of((8, 128)) == 127
    for a in range(2):
        for b in range(2):
            n = 18 * comp + 6 * a + 3 * b
            total = total + first[n] * second[n] + first[n + 1] * second[n + 1]
            total = total + jnp.where(last, first[n + 2] * second[n + 2], 0.0)
    return total


def product_kernel(zeroth, first, products):
    for k, (one, other) in enumerate([(zeroth, zeroth), (zeroth, first), (first, first)]):
        total = jnp.zeros((8, 128), F32)
        for comp in range(3):
            total = dot_owned(one, other, comp, total)
        products[k] = total


def moment_kernel(image, far, near, weight, first, products, second, moments):
    zero = jnp.zeros((8, 128), F32)
    cross, norm = zero, zero
    quadratic = [zero] * 3
    even = is_even()
    for comp in range(3):
        values = take_own(image, near, far, comp, even)
        for n in range(18):
            second[18 * comp + n] = values[n]
        values_at = {18 * comp + n: values[n] for n in range(18)}
        cross = dot_owned(first, values_at, comp, cross)
        norm = dot_owned(values_at, values_at, comp, norm)
        points = to_points(unfold(values))
        for q in range(27):
            quadratic[q % 3] = quadratic[q % 3] + points[q] * points[q] * weight[q]
    quadratic = quadratic[0] + quadratic[1] + quadratic[2]
    row = lax.broadcasted_iota(jnp.int32, (8, 128), 0)
    mine = (row >= HALO) & (row < HALO + OWN)
    sums = jnp.zeros((8, 128), F32)
    for k, total in enumerate([products[0], products[1], products[2], cross, norm, quadratic]):
        total = jnp.sum(jnp.where(mine, total, 0.0), axis=0, keepdims=True)
        sums = jnp.where(row == k, total, sums)
    sums = jnp.sum(sums, axis=1, keepdims=True)
    line = jnp.sum(jnp.where(lane_of((8, 128)) == row, sums, 0.0), axis=0, keepdims=True)
    moments[...] = jnp.broadcast_to(line, moments.shape)


def solve(moments):
    def ratio(top, pivot, scale):
        good = pivot > 1e-7 * scale
        return jnp.where(good, top / jnp.where(good, pivot, 1.0), 0.0)

    m = moments
    l10 = ratio(m[2], m[1], 0.0)
    l20 = ratio(m[3], m[1], 0.0)
    d1 = m[3] - l10 * m[2]
    e1 = m[4] - l20 * m[2]
    l21 = ratio(e1, d1, m[3])
    d2 = m[5] - l20 * m[3] - l21 * e1
    y1 = m[1] - l10 * m[0]
    y2 = m[2] - l20 * m[0] - l21 * y1
    c2 = ratio(y2, d2, m[5])
    c1 = ratio(y1, d1, m[3]) - l21 * c2
    c0 = ratio(m[0], m[1], 0.0) - l10 * c1 - l20 * c2
    return c0, c1, c2


def halves(x):
    high = x.astype(BF16)
    return high, (x - high.astype(F32)).astype(BF16)


def nodal_kernel(zeroth, first, second, out):
    row = lax.broadcasted_iota(jnp.int32, (48, 96), 0)
    source = lax.broadcasted_iota(jnp.int32, (48, 96), 1)
    wanted = (row // 8) * 16 + (row % 2) * 8 + HALO + (row % 8) // 2
    move = (source == wanted).astype(F32).astype(BF16)
    source = lax.broadcasted_iota(jnp.int32, (384, 384), 0)
    node = lax.broadcasted_iota(jnp.int32, (384, 384), 1)
    wanted = jnp.where(node < 256, (node % 2) * 128 + node // 2, 383)
    place = ((source == wanted) & (node <= 256)).astype(F32).astype(BF16)
    for k, field in enumerate((zeroth, first, second)):
        blocks = []
        for c in range(3):
            column = []
            for comp in range(3):
                for a in range(2):
                    for b in range(2):
                        column.append(field[18 * comp + 6 * a + 3 * b + c])
            blocks.append(jnp.concatenate(column, axis=0))
        high, low = halves(jnp.concatenate(blocks, axis=1))
        moved = jnp.dot(move, high, preferred_element_type=F32) + jnp.dot(move, low, preferred_element_type=F32)
        high, low = halves(moved)
        out[k] = jnp.dot(high, place, preferred_element_type=F32) + jnp.dot(low, place, preferred_element_type=F32)


def last_kernel(moments, nodal, velocity, out):
    line = jnp.sum(moments[...], axis=0, keepdims=True)
    lane = lane_of((1, 128))
    mu = [jnp.sum(jnp.where(lane == k, line, 0.0), axis=1, keepdims=True) for k in range(6)]
    c0, c1, c2 = [HALF_STEP * c for c in solve(mu)]
    for comp in range(3):
        for x in range(2):
            start = 16 * comp + 8 * x
            part = [nodal[k, pl.ds(start, 8), : velocity.shape[3]] for k in range(3)]
            out[comp, x] = velocity[comp, x] + (c0 * part[0] + c1 * part[1] + c2 * part[2])


VMEM = pl.BlockSpec(memory_space=pltpu.VMEM)


HBM = pl.BlockSpec(memory_space=pltpu.HBM)


def call(kernel, outs, *args, scratch=(), flops=100000, in_hbm=0, dtypes=None):
    shapes = [jax.ShapeDtypeStruct(shape, dtype) for shape, dtype in zip(outs, dtypes or [F32] * len(outs))]
    moved = sum(a.size * a.dtype.itemsize for a in args) + sum(4 * int(np.prod(s)) for s in outs)
    return pl.pallas_call(
        kernel,
        out_shape=shapes,
        in_specs=[HBM] * in_hbm + [VMEM] * (len(args) - in_hbm),
        out_specs=[VMEM] * len(outs),
        scratch_shapes=list(scratch),
        compiler_params=pltpu.CompilerParams(vmem_limit_bytes=32 * 1024 * 1024),
        cost_estimate=pl.CostEstimate(flops=flops, bytes_accessed=moved, transcendentals=0),
        name=kernel.__name__,
    )(*args)


def swap(near, far, axis="slab"):
    count = lax.axis_size(axis)
    far = lax.ppermute(far, axis, [(i, (i + (1 if i % 2 else -1)) % count) for i in range(count)])
    near = lax.ppermute(near, axis, [(i, i + (-1 if i % 2 else 1)) for i in range(count)])
    return near, far


def local(velocity, energy, density, material, geometry, mass_weight, energy_mass):
    tile = (4, 128)
    full = (8, 128)
    geometry = geometry.reshape((324,) + full)
    density = density.reshape((4,) + full)
    energy = energy.reshape((4,) + full)
    energy_mass = energy_mass.reshape((4,) + full)
    mass_weight = mass_weight.reshape((27,) + tile)
    material = material.reshape(tile)
    pair = (2, 128)
    devices = lax.axis_size("slab") * lax.axis_size("brick")

    stays = [
        pltpu.with_memory_space_constraint(x, pltpu.HBM) for x in (geometry, density, energy, material, mass_weight)
    ]
    force, near, far, pressure, gravity = call(
        force_kernel,
        [(54,) + full, (27,) + tile, (27,) + tile, (4,) + full, (9,) + full],
        *stays,
        scratch=[
            pltpu.VMEM((216,) + full, BF16),
            pltpu.VMEM((4,) + full, F32),
            pltpu.VMEM((4,) + full, F32),
            pltpu.VMEM(tile, jnp.int32),
            pltpu.VMEM((27,) + tile, F32),
            pltpu.SemaphoreType.DMA((10,)),
        ],
        in_hbm=5,
        dtypes=[F32, BF16, BF16, F32, F32],
    )
    spread, middle, near_part, far_part = call(
        spread_kernel,
        [(36,) + full, (56,) + full, (MESSAGE,) + pair, (MESSAGE,) + pair],
        stays[0], velocity, pressure, gravity, mass_weight,
        scratch=[pltpu.VMEM((108,) + full, BF16), pltpu.SemaphoreType.DMA((3,))],
        in_hbm=1,
        dtypes=[F32, F32, BF16, BF16],
    )
    near, far = swap(near, far)
    own, near, far = call(
        rim_kernel,
        [(55,) + full, (MESSAGE,) + pair, (MESSAGE,) + pair],
        force, far, near, middle, near_part, far_part,
        dtypes=[F32, BF16, BF16],
    )
    near_rim, far_rim = swap(near, far, "brick")
    zeroth, weight, image, near, far = call(
        first_kernel,
        [(54,) + full, (27,) + full, (54,) + full, (13,) + full, (13,) + full],
        own, far_rim, near_rim, mass_weight,
        scratch=[pltpu.VMEM((SPEEDS,) + full, F32)],
        dtypes=[F32, F32, F32, BF16, BF16],
    )
    near, far = swap(near, far)
    speeds, plane = call(speed_kernel, [(54,) + full, (10,) + full], far_rim, near_rim, spread)
    first, image, near, far = call(
        second_kernel,
        [(54,) + full, (54,) + full, (17,) + full, (17,) + full],
        image, far, near, weight, plane,
        dtypes=[F32, F32, BF16, BF16],
    )
    near, far = swap(near, far)
    (energy_half,) = call(
        work_kernel, [(4,) + full], geometry, pressure, energy, energy_mass, speeds, far, near
    )
    (products,) = call(product_kernel, [(3,) + full], zeroth, first)
    second, moments = call(
        moment_kernel, [(54,) + full, (devices, 128)], image, far, near, weight, first, products
    )
    moments = lax.all_to_all(moments, ("slab", "brick"), 0, 0, tiled=True)
    (nodal,) = call(nodal_kernel, [(3, 48, 384)], zeroth, first, second)
    (velocity_half,) = call(last_kernel, [velocity.shape], moments, nodal, velocity)
    return (velocity_half, energy_half.reshape(8, 1, 4, 128))


def solution(mesh):
    nodes = P(None, "slab", "brick", None)
    return jax.shard_map(
        local,
        mesh=mesh,
        in_specs=(
            nodes,
            nodes,
            nodes,
            P("slab", "brick", None),
            P(None, None, "slab", "brick", None),
            nodes,
            nodes,
        ),
        out_specs=(nodes, nodes),
        check_vma=False,
    )
```

```python
import jax
import jax.numpy as jnp
import numpy as np
from jax import lax
from jax.experimental import pallas as pl
from jax.experimental.pallas import tpu as pltpu
from jax.sharding import PartitionSpec as P

HALF_STEP = 0.25
GRAVITY = 1.0
F32 = jnp.float32
BF16 = jnp.bfloat16

OFFSET = float(np.sqrt(0.6) / 2.0)
SIDE = 0.3
MIDDLE = 0.4
ODD, EVEN = OFFSET / SIDE, MIDDLE / SIDE
LINE_WEIGHTS = (5.0 / 18.0, 8.0 / 18.0, 5.0 / 18.0)
POINT_WEIGHT = [a * b * c for a in LINE_WEIGHTS for b in LINE_WEIGHTS for c in LINE_WEIGHTS]
POINT_SCALE = [a * b * c for a in (SIDE, 1.0, SIDE) for b in (SIDE, 1.0, SIDE) for c in (SIDE, 1.0, SIDE)]
OWN = 4
HALO = 2


def lines(direction):
    stride = (9, 3, 1)[direction]
    return [(n, n + stride, n + 2 * stride) for n in range(27) if (n // stride) % 3 == 0]


def to_points(values):
    values = list(values)
    for direction in range(3):
        for i, j, k in lines(direction):
            even = (values[i] + values[k]) + EVEN * values[j]
            odd = ODD * (values[i] - values[k])
            values[i], values[k] = even + odd, even - odd
    return values


def from_points(values):
    values = list(values)
    for direction in range(3):
        for i, j, k in lines(direction):
            total = values[i] + values[k]
            odd = ODD * (values[i] - values[k])
            values[i], values[k] = total + odd, total - odd
            values[j] = values[j] + EVEN * total
    return values


def lane_of(shape):
    return lax.broadcasted_iota(jnp.int32, shape, len(shape) - 1)


def assemble_z(values, wall):
    values = list(values)
    lane = lane_of(values[0].shape)
    first, last = lane == 0, lane == 127
    for i, k in [(n, n + 2) for n in range(0, len(values), 3)]:
        total = values[i] + jnp.where(first, 0.0, pltpu.roll(values[k], 1, 1))
        top = values[k]
        if wall:
            total = jnp.where(first, 0.0, total)
            top = jnp.zeros_like(top)
        values[i] = total
        values[k] = jnp.where(last, top, pltpu.roll(total, 127, 1))
    return values


def fold(values, wall):
    lane = lane_of(values[0].shape)
    folded = []
    for a in (0, 9, 18):
        columns = [[values[a + c] + pltpu.roll(values[a + 6 + c], 1, 0), values[a + 3 + c]] for c in range(3)]
        for b in range(2):
            first = columns[0][b] + jnp.where(lane == 0, 0.0, pltpu.roll(columns[2][b], 1, 1))
            if wall:
                first = jnp.where(lane == 0, 0.0, first)
            folded += [first, columns[1][b], jnp.zeros_like(first) if wall else columns[2][b]]
    return folded


def unfold(folded):
    lane = lane_of(folded[0].shape)
    values = []
    for a in (0, 6, 12):
        planes = []
        for b in (0, 3):
            first, second, top = folded[a + b : a + b + 3]
            planes.append([first, second, jnp.where(lane == 127, top, pltpu.roll(first, 127, 1))])
        planes.append([pltpu.roll(value, 7, 0) for value in planes[0]])
        values += planes[0] + planes[1] + planes[2]
    return values


def is_even(axis="slab"):
    return lax.axis_index(axis) % 2 == 0


def put(near, far, slot, left, right, even):
    near[slot] = jnp.where(even, right, left).astype(BF16)
    far[slot] = jnp.where(even, left, right).astype(BF16)


def get(near, far, slot, even):
    one, other = near[slot].astype(F32), far[slot].astype(F32)
    return jnp.where(even, other, one), jnp.where(even, one, other)


def pressure_of(density, energy, material):
    gamma = jnp.where(material[...] == 0, 2.0 / 3.0, 0.4).astype(F32)
    gamma = jnp.concatenate([gamma, gamma], axis=0)
    return (gamma[None] * density[...] * energy[...]).astype(BF16).astype(F32)


def to_lane(tile, lane, values, slot):
    return jnp.where(lane == slot, pltpu.roll(values, slot + 1, 1), tile)


def third_along_z(values, tops, lane, slot):
    return jnp.where(lane == 127, pltpu.roll(tops, 127 - slot, 1), pltpu.roll(values, 127, 1))


def double(values):
    return jnp.concatenate([values, values], axis=0)


def force_of(geometry, r, pressure):
    value = jnp.sum(geometry[pl.ds(4 * r, 4)].astype(F32) * pressure, axis=0)
    return -(value + pltpu.roll(value, OWN, 0))


def force_kernel(
    geometry_in, density_in, energy_in, material_in, mass_weight_in,
    field, near, far, pressure_out, gravity_out,
    geometry, density, energy, material, mass_weight, sems,
):
    small = [
        pltpu.make_async_copy(source, target, sems.at[6 + i])
        for i, (source, target) in enumerate(
            [(density_in, density), (energy_in, energy), (material_in, material), (mass_weight_in, mass_weight)]
        )
    ]
    parts = [
        pltpu.make_async_copy(
            geometry_in.at[pl.ds(108 * comp + 36 * a, 36)], geometry.at[pl.ds(72 * comp + 18 * a, 36)], sems.at[2 * comp + a // 2]
        )
        for comp in range(3)
        for a in (0, 2)
    ]
    for copy in small + parts:
        copy.start()
    for copy in small:
        copy.wait()
    pressure = pressure_of(density, energy, material)
    gravity = from_points([double(mass_weight[q]) * (POINT_WEIGHT[q] * POINT_SCALE[q]) for q in range(27)])
    pressure_out[...] = pressure
    for n in range(9):
        gravity_out[n] = GRAVITY * gravity[9 + n]
    even = is_even()
    for comp in range(3):
        parts[2 * comp].wait()
        parts[2 * comp + 1].wait()
        values = []
        for n in range(18):
            value = force_of(geometry, 18 * comp + n, pressure)
            if comp == 2:
                value = value - GRAVITY * gravity[n if n < 9 else n + 9]
            field[18 * comp + n] = value
            values.append(value)
        for n in range(9):
            put(near, far, 9 * comp + n, values[n][:OWN], values[9 + n][:OWN], even)


def spread_velocity(velocity, out):
    rows = velocity[...].astype(BF16).reshape(48, velocity.shape[3])
    low = rows[:, :256]
    high = rows[:, 256:257].astype(F32)
    node = lax.broadcasted_iota(jnp.int32, (256, 384), 0)
    lane = lax.broadcasted_iota(jnp.int32, (256, 384), 1)
    pick = (node == 2 * (lane % 128) + lane // 128).astype(F32).astype(BF16)
    spread = jnp.dot(low, pick, preferred_element_type=F32)
    top = jnp.where(lane_of((48, 128)) == 127, high, 0.0)
    spread = jnp.concatenate([spread[:, :256], spread[:, 256:] + top], axis=1)
    row = lax.broadcasted_iota(jnp.int32, (96, 48), 0)
    source = lax.broadcasted_iota(jnp.int32, (96, 48), 1)
    wanted = (row // 16) * 8 + 2 * (row % 8) + (row // 8) % 2
    move = ((source == wanted) & (row % 8 < OWN)).astype(F32).astype(BF16)
    moved = jnp.dot(move, spread.astype(BF16), preferred_element_type=F32)
    for group in range(12):
        for c in range(3):
            out[3 * group + c] = moved[8 * group : 8 * group + 8, 128 * c : 128 * c + 128]


TOPS, WEIGHTS, SPEEDS, MESSAGE = 45, 46, 73, 79
SPEED_LANE = 32


def add_tops(values, comp, a, tops, sent):
    if comp == 2:
        return tops, sent
    row = lax.broadcasted_iota(jnp.int32, (8, 128), 0)
    lane = lane_of((8, 128))
    i = 3 * comp + a
    first, second, third = [values[3 * b + 2] for b in range(3)]
    for b, value in enumerate((first, second, third)):
        tops = to_lane(tops, lane, value, 3 * i + b)
    first = first + jnp.where(row % 2 == 1, pltpu.roll(third, 1, 0), 0.0)
    return tops, to_lane(sent, lane, first, 3 * i)


def fill_plane(values, comp, a, out, near, far, even_y):
    row = lax.broadcasted_iota(jnp.int32, (8, 128), 0)
    i = 3 * comp + a
    outer = []
    for c in range(2):
        first, second, third = [values[3 * b + c] for b in range(3)]
        for b, value in enumerate((first, second, third)):
            out[6 * i + 2 * b + c] = pltpu.roll(value, HALO, 0)
        first = first + jnp.where(row % 2 == 1, pltpu.roll(third, 1, 0), 0.0)
        for k, value in enumerate((first, second)):
            put(near, far, 4 * i + 2 * k + c, value[:HALO], value[HALO:OWN], even_y)
        outer.append(third)
    both = jnp.where(row % 2 == 1, outer[1], pltpu.roll(outer[0], 7, 0))
    put(near, far, 36 + i, both[:HALO], both[HALO:OWN], even_y)


def spread_kernel(
    geometry_in, velocity, pressure_in, gravity, mass_weight, spread, middle, near, far, geometry, sems
):
    parts = [
        pltpu.make_async_copy(
            geometry_in.at[pl.ds(108 * comp + 36, 36)], geometry.at[pl.ds(36 * comp, 36)], sems.at[comp]
        )
        for comp in range(3)
    ]
    for copy in parts:
        copy.start()
    even_y = is_even("brick")
    row = lax.broadcasted_iota(jnp.int32, (8, 128), 0)
    lane = lane_of((8, 128))
    spread_velocity(velocity, spread)
    tops = jnp.zeros((8, 128), F32)
    sent = tops
    for k in range(6):
        tops = to_lane(tops, lane, jnp.where(row == 0, spread[6 * k + 2], 0.0), SPEED_LANE + k)
    for q in range(27):
        put(near, far, WEIGHTS + q, mass_weight[q, :HALO], mass_weight[q, HALO:], even_y)
    for k in range(6):
        both = jnp.where(row == 0, spread[6 * k], pltpu.roll(spread[6 * k + 1], 1, 0))[:HALO].astype(BF16)
        near[SPEEDS + k] = both
        far[SPEEDS + k] = both
    pressure = pressure_in[...]
    for comp in range(3):
        parts[comp].wait()
        values = []
        for n in range(9):
            value = force_of(geometry, 9 * comp + n, pressure)
            values.append(value - gravity[n] if comp == 2 else value)
        tops, sent = add_tops(values, comp, 1, tops, sent)
        fill_plane(assemble_z(values, comp == 2), comp, 1, middle, near, far, even_y)
    middle[54] = tops
    middle[55] = sent


def rim_kernel(field, far, near, middle, near_in, far_in, out, near_out, far_out):
    even = is_even()
    even_y = is_even("brick")
    lane = lane_of((8, 128))
    tops, sent = middle[54], middle[55]
    for comp in range(3):
        i = 3 * comp + 1
        for k in range(6):
            out[6 * i + k] = middle[6 * i + k]
        for k in [4 * i, 4 * i + 1, 4 * i + 2, 4 * i + 3, 36 + i]:
            near_out[k] = near_in[k]
            far_out[k] = far_in[k]
        values = [field[18 * comp + n] for n in range(18)]
        for n in range(9):
            left, right = get(near, far, 9 * comp + n, even)
            values[n] = values[n] + double(left)
            values[9 + n] = values[9 + n] + double(right)
        for a, plane in ((0, values[:9]), (2, values[9:])):
            tops, sent = add_tops(plane, comp, a, tops, sent)
            fill_plane(assemble_z(plane, comp == 2), comp, a, out, near_out, far_out, even_y)
    out[54] = pltpu.roll(tops, HALO, 0)
    tops = jnp.where((lane % 3 == 0) & (lane < 27), sent, tops)
    put(near_out, far_out, TOPS, tops[:HALO], tops[HALO:OWN], even_y)
    for k in range(WEIGHTS, MESSAGE):
        near_out[k] = near_in[k]
        far_out[k] = far_in[k]


def send_planes(planes, near, far, even):
    lane = lane_of((8, 128))
    sides = [jnp.zeros((8, 128), F32)] * 2
    for comp in range(3):
        for b in range(2):
            left, right = [planes[comp][a + 3 * b : a + 3 * b + 3] for a in (0, 12)]
            for c in range(2):
                put(near, far, 4 * comp + 2 * b + c, left[c], right[c], even)
            sides = [to_lane(side, lane, plane[2], 2 * comp + b) for side, plane in zip(sides, (left, right))]
    put(near, far, 12, sides[0], sides[1], even)


def apply_mass(values, weight, wall):
    points = to_points(values)
    points = [points[q] * weight[q] for q in range(27)]
    return fold(from_points(points), wall)


def first_kernel(
    own, far_in, near_in, mass_weight, field, weight, image, near, far, rows
):
    even = is_even()
    even_y = is_even("brick")
    row = lax.broadcasted_iota(jnp.int32, (8, 128), 0)
    lane = lane_of((8, 128))
    mine = (row >= HALO) & (row < HALO + OWN)
    for k in range(SPEEDS):
        low, high = get(near_in, far_in, k, even_y)
        rows[k, :HALO] = low
        rows[k, HALO + OWN :] = high
        if k >= WEIGHTS:
            rows[k, HALO : HALO + OWN] = mass_weight[k - WEIGHTS]
    for q in range(27):
        weight[q] = rows[WEIGHTS + q] * (POINT_WEIGHT[q] * POINT_SCALE[q] ** 2)
    edge = (row == 1) | (row == 7)
    tops = jnp.where((lane % 3 == 2) & ~edge, 0.0, rows[TOPS])
    tops = jnp.where(mine, own[54], tops)
    tops = tops + jnp.where(lane % 3 == 0, pltpu.roll(pltpu.roll(tops, 126, 1), 1, 0), 0.0)
    planes = []
    for comp in range(3):
        values = []
        for a in range(3):
            i = 3 * comp + a
            columns = []
            for c in range(2):
                k = 2 * i + c
                halos = [rows[4 * i + c], rows[4 * i + 2 + c], rows[36 + k // 2]]
                halos[2] = jnp.where(edge, halos[2] if k % 2 == 1 else pltpu.roll(halos[2], 1, 0), 0.0)
                column = [jnp.where(mine, own[6 * i + 2 * b + c], halos[b]) for b in range(3)]
                columns.append([column[0] + pltpu.roll(column[2], 1, 0), column[1]])
            for b in range(2):
                values += [columns[0][b], columns[1][b], pltpu.roll(tops, 127 - 3 * i - b, 1)]
        for n in range(18):
            field[18 * comp + n] = values[n]
        values = apply_mass(unfold(values), weight, comp == 2)
        for n in range(18):
            image[18 * comp + n] = values[n]
        planes.append(values)
    send_planes(planes, near, far, even)


def speed_kernel(far_in, near_in, spread, speeds, near, far):
    even_y = is_even("brick")
    row = lax.broadcasted_iota(jnp.int32, (8, 128), 0)
    lane = lane_of((8, 128))
    edge_tops = get(near_in, far_in, TOPS, even_y)[1]
    edge_tops = jnp.concatenate([edge_tops] * 4, axis=0)
    plane = []
    tops = jnp.zeros((8, 128), F32)
    for comp in range(3):
        for a in range(2):
            k = 2 * comp + a
            speed = [spread[6 * k + n] for n in range(6)]
            beyond = get(near_in, far_in, SPEEDS + k, even_y)[1]
            beyond = [beyond[c : c + 1] for c in range(2)]
            for c in range(2):
                speed.append(jnp.where(row == OWN - 1, beyond[c], pltpu.roll(speed[c], 7, 0)))
            third = third_along_z(jnp.broadcast_to(beyond[0], (8, 128)), edge_tops, lane, SPEED_LANE + k)[0:1]
            speed.append(jnp.where(row == OWN - 1, third, pltpu.roll(speed[2], 7, 0)))
            for n in range(9):
                speeds[18 * comp + 9 * a + n] = speed[n]
            if a == 0:
                for b in range(3):
                    plane += speed[3 * b : 3 * b + 2]
                    tops = to_lane(tops, lane, speed[3 * b + 2], SPEED_LANE + 3 * comp + b)
    tiles = [jnp.where(row < OWN, plane[2 * k], pltpu.roll(plane[2 * k + 1], OWN, 0)) for k in range(9)]
    for k, value in enumerate(tiles + [tops]):
        near[k] = value.astype(BF16)
        far[k] = value.astype(BF16)


def send_own(planes, near, far, even):
    row = lax.broadcasted_iota(jnp.int32, (8, 128), 0)
    lane = lane_of((8, 128))
    sides = [jnp.zeros((8, 128), F32)] * 2
    after = [jnp.zeros((8, 128), F32)] * 2
    for comp in range(3):
        for b in range(2):
            both = []
            for side, a in enumerate((0, 12)):
                plane = planes[comp][a + 3 * b : a + 3 * b + 3]
                both.append(jnp.where(row < OWN, pltpu.roll(plane[0], 6, 0), pltpu.roll(plane[1], 2, 0)))
                sides[side] = to_lane(sides[side], lane, plane[2], 2 * comp + b)
                if b == 0:
                    for c in range(2):
                        k = 2 * comp + c
                        after[side] = jnp.where(row == k, pltpu.roll(plane[c], (k + 2) % 8, 0), after[side])
            put(near, far, 2 * comp + b, both[0], both[1], even)
    put(near, far, 6, after[0], after[1], even)
    put(near, far, 7, sides[0], sides[1], even)


def take_planes(image, near, far, comp, even):
    def read(b):
        tiles = [get(near, far, 4 * comp + 2 * b + c, even) for c in range(2)]
        return [[tile[side] for tile in tiles] for side in range(2)]

    return add_planes(image, read, get(near, far, 12, even), comp)


def take_own(image, near, far, comp, even):
    row = lax.broadcasted_iota(jnp.int32, (8, 128), 0)
    after = get(near, far, 6, even)

    def read(b):
        sides = []
        for side, both in enumerate(get(near, far, 2 * comp + b, even)):
            plane = [pltpu.roll(both, 2, 0), pltpu.roll(both, 6, 0)]
            if b == 0:
                for c in range(2):
                    k = 2 * comp + c
                    plane[c] = jnp.where(row == 6, pltpu.roll(after[side], 6 - k, 0), plane[c])
            sides.append(plane)
        return sides

    return add_planes(image, read, get(near, far, 7, even), comp)


def add_planes(image, read, tops, comp):
    values = [image[18 * comp + n] for n in range(18)]
    for b in range(2):
        for a, plane, top in zip((0, 12), read(b), tops):
            n = a + 3 * b
            for c in range(2):
                values[n + c] = values[n + c] + plane[c]
            values[n + 2] = values[n + 2] + pltpu.roll(top, 127 - 2 * comp - b, 1)
    return values


def second_kernel(image, far_in, near_in, weight, speeds, field, image_out, near, far):
    even = is_even()
    planes = []
    for comp in range(3):
        values = take_planes(image, near_in, far_in, comp, even)
        for n in range(18):
            field[18 * comp + n] = values[n]
        values = apply_mass(unfold(values), weight, comp == 2)
        for n in range(18):
            image_out[18 * comp + n] = values[n]
        planes.append(values)
    send_own(planes, near, far, even)


def work_kernel(geometry, pressure_in, energy, energy_mass, speeds, far, near, out):
    even = is_even()
    pressure = pressure_in[...]
    work = jnp.zeros_like(pressure)
    row = lax.broadcasted_iota(jnp.int32, (8, 128), 0)
    lane = lane_of((8, 128))
    tops = get(near, far, 9, even)[1]
    for comp in range(3):
        speed = [speeds[18 * comp + n] for n in range(18)]
        for b in range(3):
            both = get(near, far, 3 * comp + b, even)[1]
            speed += [both, pltpu.roll(both, OWN, 0)]
            speed.append(third_along_z(both, tops, lane, SPEED_LANE + 3 * comp + b))
        for n in range(27):
            value = jnp.where(row < OWN, speed[n], pltpu.roll(speed[n], OWN, 0))
            work = work + geometry[pl.ds(4 * (27 * comp + n), 4)].astype(F32) * value[None]
    out[...] = energy[...] + HALF_STEP * pressure * work / energy_mass[...]


def dot_owned(first, second, comp, total):
    last = lane_of((8, 128)) == 127
    for a in range(2):
        for b in range(2):
            n = 18 * comp + 6 * a + 3 * b
            total = total + first[n] * second[n] + first[n + 1] * second[n + 1]
            total = total + jnp.where(last, first[n + 2] * second[n + 2], 0.0)
    return total


def product_kernel(zeroth, first, far_speed, near_speed, products):
    for k, (one, other) in enumerate([(zeroth, zeroth), (zeroth, first), (first, first)]):
        total = jnp.zeros((8, 128), F32)
        for comp in range(3):
            total = dot_owned(one, other, comp, total)
        products[k] = total


def moment_kernel(image, far, near, weight, first, products, second, moments):
    zero = jnp.zeros((8, 128), F32)
    cross, norm = zero, zero
    quadratic = [zero] * 3
    even = is_even()
    for comp in range(3):
        values = take_own(image, near, far, comp, even)
        for n in range(18):
            second[18 * comp + n] = values[n]
        values_at = {18 * comp + n: values[n] for n in range(18)}
        cross = dot_owned(first, values_at, comp, cross)
        norm = dot_owned(values_at, values_at, comp, norm)
        points = to_points(unfold(values))
        for q in range(27):
            quadratic[q % 3] = quadratic[q % 3] + points[q] * points[q] * weight[q]
    quadratic = quadratic[0] + quadratic[1] + quadratic[2]
    row = lax.broadcasted_iota(jnp.int32, (8, 128), 0)
    mine = (row >= HALO) & (row < HALO + OWN)
    sums = jnp.zeros((8, 128), F32)
    for k, total in enumerate([products[0], products[1], products[2], cross, norm, quadratic]):
        total = jnp.sum(jnp.where(mine, total, 0.0), axis=0, keepdims=True)
        sums = jnp.where(row == k, total, sums)
    sums = jnp.sum(sums, axis=1, keepdims=True)
    line = jnp.sum(jnp.where(lane_of((8, 128)) == row, sums, 0.0), axis=0, keepdims=True)
    moments[...] = jnp.broadcast_to(line, moments.shape)


def solve(moments):
    def ratio(top, pivot, scale):
        good = pivot > 1e-7 * scale
        return jnp.where(good, top / jnp.where(good, pivot, 1.0), 0.0)

    m = moments
    l10 = ratio(m[2], m[1], 0.0)
    l20 = ratio(m[3], m[1], 0.0)
    d1 = m[3] - l10 * m[2]
    e1 = m[4] - l20 * m[2]
    l21 = ratio(e1, d1, m[3])
    d2 = m[5] - l20 * m[3] - l21 * e1
    y1 = m[1] - l10 * m[0]
    y2 = m[2] - l20 * m[0] - l21 * y1
    c2 = ratio(y2, d2, m[5])
    c1 = ratio(y1, d1, m[3]) - l21 * c2
    c0 = ratio(m[0], m[1], 0.0) - l10 * c1 - l20 * c2
    return c0, c1, c2


def halves(x):
    high = x.astype(BF16)
    return high, (x - high.astype(F32)).astype(BF16)


def nodal_kernel(zeroth, first, second, out):
    row = lax.broadcasted_iota(jnp.int32, (48, 96), 0)
    source = lax.broadcasted_iota(jnp.int32, (48, 96), 1)
    wanted = (row // 8) * 16 + (row % 2) * 8 + HALO + (row % 8) // 2
    move = (source == wanted).astype(F32).astype(BF16)
    source = lax.broadcasted_iota(jnp.int32, (384, 384), 0)
    node = lax.broadcasted_iota(jnp.int32, (384, 384), 1)
    wanted = jnp.where(node < 256, (node % 2) * 128 + node // 2, 383)
    place = ((source == wanted) & (node <= 256)).astype(F32).astype(BF16)
    for k, field in enumerate((zeroth, first, second)):
        blocks = []
        for c in range(3):
            column = []
            for comp in range(3):
                for a in range(2):
                    for b in range(2):
                        column.append(field[18 * comp + 6 * a + 3 * b + c])
            blocks.append(jnp.concatenate(column, axis=0))
        high, low = halves(jnp.concatenate(blocks, axis=1))
        moved = jnp.dot(move, high, preferred_element_type=F32) + jnp.dot(move, low, preferred_element_type=F32)
        high, low = halves(moved)
        out[k] = jnp.dot(high, place, preferred_element_type=F32) + jnp.dot(low, place, preferred_element_type=F32)


def last_kernel(moments, nodal, velocity, out):
    line = jnp.sum(moments[...], axis=0, keepdims=True)
    lane = lane_of((1, 128))
    mu = [jnp.sum(jnp.where(lane == k, line, 0.0), axis=1, keepdims=True) for k in range(6)]
    c0, c1, c2 = [HALF_STEP * c for c in solve(mu)]
    for comp in range(3):
        for x in range(2):
            start = 16 * comp + 8 * x
            part = [nodal[k, pl.ds(start, 8), : velocity.shape[3]] for k in range(3)]
            out[comp, x] = velocity[comp, x] + (c0 * part[0] + c1 * part[1] + c2 * part[2])


VMEM = pl.BlockSpec(memory_space=pltpu.VMEM)


HBM = pl.BlockSpec(memory_space=pltpu.HBM)


def call(kernel, outs, *args, scratch=(), flops=100000, in_hbm=0, dtypes=None):
    shapes = [jax.ShapeDtypeStruct(shape, dtype) for shape, dtype in zip(outs, dtypes or [F32] * len(outs))]
    moved = sum(a.size * a.dtype.itemsize for a in args) + sum(4 * int(np.prod(s)) for s in outs)
    return pl.pallas_call(
        kernel,
        out_shape=shapes,
        in_specs=[HBM] * in_hbm + [VMEM] * (len(args) - in_hbm),
        out_specs=[VMEM] * len(outs),
        scratch_shapes=list(scratch),
        compiler_params=pltpu.CompilerParams(vmem_limit_bytes=32 * 1024 * 1024),
        cost_estimate=pl.CostEstimate(flops=flops, bytes_accessed=moved, transcendentals=0),
        name=kernel.__name__,
    )(*args)


def swap(near, far, axis="slab"):
    count = lax.axis_size(axis)
    far = lax.ppermute(far, axis, [(i, (i + (1 if i % 2 else -1)) % count) for i in range(count)])
    near = lax.ppermute(near, axis, [(i, i + (-1 if i % 2 else 1)) for i in range(count)])
    return near, far


def local(velocity, energy, density, material, geometry, mass_weight, energy_mass):
    tile = (4, 128)
    full = (8, 128)
    geometry = geometry.reshape((324,) + full)
    density = density.reshape((4,) + full)
    energy = energy.reshape((4,) + full)
    energy_mass = energy_mass.reshape((4,) + full)
    mass_weight = mass_weight.reshape((27,) + tile)
    material = material.reshape(tile)
    pair = (2, 128)
    devices = lax.axis_size("slab") * lax.axis_size("brick")

    stays = [
        pltpu.with_memory_space_constraint(x, pltpu.HBM) for x in (geometry, density, energy, material, mass_weight)
    ]
    force, near, far, pressure, gravity = call(
        force_kernel,
        [(54,) + full, (27,) + tile, (27,) + tile, (4,) + full, (9,) + full],
        *stays,
        scratch=[
            pltpu.VMEM((216,) + full, BF16),
            pltpu.VMEM((4,) + full, F32),
            pltpu.VMEM((4,) + full, F32),
            pltpu.VMEM(tile, jnp.int32),
            pltpu.VMEM((27,) + tile, F32),
            pltpu.SemaphoreType.DMA((10,)),
        ],
        in_hbm=5,
        dtypes=[F32, BF16, BF16, F32, F32],
    )
    spread, middle, near_part, far_part = call(
        spread_kernel,
        [(36,) + full, (56,) + full, (MESSAGE,) + pair, (MESSAGE,) + pair],
        stays[0], velocity, pressure, gravity, mass_weight,
        scratch=[pltpu.VMEM((108,) + full, BF16), pltpu.SemaphoreType.DMA((3,))],
        in_hbm=1,
        dtypes=[F32, F32, BF16, BF16],
    )
    near, far = swap(near, far)
    own, near, far = call(
        rim_kernel,
        [(55,) + full, (MESSAGE,) + pair, (MESSAGE,) + pair],
        force, far, near, middle, near_part, far_part,
        dtypes=[F32, BF16, BF16],
    )
    near_rim, far_rim = swap(near, far, "brick")
    zeroth, weight, image, near, far = call(
        first_kernel,
        [(54,) + full, (27,) + full, (54,) + full, (13,) + full, (13,) + full],
        own, far_rim, near_rim, mass_weight,
        scratch=[pltpu.VMEM((SPEEDS,) + full, F32)],
        dtypes=[F32, F32, F32, BF16, BF16],
    )
    near, far = swap(near, far)
    speeds, near_speed, far_speed = call(
        speed_kernel,
        [(54,) + full, (10,) + full, (10,) + full],
        far_rim, near_rim, spread,
        dtypes=[F32, BF16, BF16],
    )
    near_speed, far_speed = swap(near_speed, far_speed)
    first, image, near, far = call(
        second_kernel,
        [(54,) + full, (54,) + full, (8,) + full, (8,) + full],
        image, far, near, weight, speeds,
        dtypes=[F32, F32, BF16, BF16],
    )
    near, far = swap(near, far)
    (energy_half,) = call(
        work_kernel, [(4,) + full], geometry, pressure, energy, energy_mass, speeds, far_speed, near_speed
    )
    (products,) = call(product_kernel, [(3,) + full], zeroth, first, far_speed, near_speed)
    second, moments = call(
        moment_kernel, [(54,) + full, (devices, 128)], image, far, near, weight, first, products
    )
    moments = lax.all_to_all(moments, ("slab", "brick"), 0, 0, tiled=True)
    (nodal,) = call(nodal_kernel, [(3, 48, 384)], zeroth, first, second)
    (velocity_half,) = call(last_kernel, [velocity.shape], moments, nodal, velocity)
    return (velocity_half, energy_half.reshape(8, 1, 4, 128))


def solution(mesh):
    nodes = P(None, "slab", "brick", None)
    return jax.shard_map(
        local,
        mesh=mesh,
        in_specs=(
            nodes,
            nodes,
            nodes,
            P("slab", "brick", None),
            P(None, None, "slab", "brick", None),
            nodes,
            nodes,
        ),
        out_specs=(nodes, nodes),
        check_vma=False,
    )
```

```python
import jax
import jax.numpy as jnp
import numpy as np
from jax import lax
from jax.experimental import pallas as pl
from jax.experimental.pallas import tpu as pltpu
from jax.sharding import PartitionSpec as P

HALF_STEP = 0.25
GRAVITY = 1.0
F32 = jnp.float32
BF16 = jnp.bfloat16

OFFSET = float(np.sqrt(0.6) / 2.0)
SIDE = 0.3
MIDDLE = 0.4
ODD, EVEN = OFFSET / SIDE, MIDDLE / SIDE
LINE_WEIGHTS = (5.0 / 18.0, 8.0 / 18.0, 5.0 / 18.0)
POINT_WEIGHT = [a * b * c for a in LINE_WEIGHTS for b in LINE_WEIGHTS for c in LINE_WEIGHTS]
POINT_SCALE = [a * b * c for a in (SIDE, 1.0, SIDE) for b in (SIDE, 1.0, SIDE) for c in (SIDE, 1.0, SIDE)]
OWN = 4
HALO = 2


def lines(direction):
    stride = (9, 3, 1)[direction]
    return [(n, n + stride, n + 2 * stride) for n in range(27) if (n // stride) % 3 == 0]


def to_points(values):
    values = list(values)
    for direction in range(3):
        for i, j, k in lines(direction):
            even = (values[i] + values[k]) + EVEN * values[j]
            odd = ODD * (values[i] - values[k])
            values[i], values[k] = even + odd, even - odd
    return values


def from_points(values):
    values = list(values)
    for direction in range(3):
        for i, j, k in lines(direction):
            total = values[i] + values[k]
            odd = ODD * (values[i] - values[k])
            values[i], values[k] = total + odd, total - odd
            values[j] = values[j] + EVEN * total
    return values


def lane_of(shape):
    return lax.broadcasted_iota(jnp.int32, shape, len(shape) - 1)


def assemble_z(values, wall):
    values = list(values)
    lane = lane_of(values[0].shape)
    first, last = lane == 0, lane == 127
    for i, k in [(n, n + 2) for n in range(0, len(values), 3)]:
        total = values[i] + jnp.where(first, 0.0, pltpu.roll(values[k], 1, 1))
        top = values[k]
        if wall:
            total = jnp.where(first, 0.0, total)
            top = jnp.zeros_like(top)
        values[i] = total
        values[k] = jnp.where(last, top, pltpu.roll(total, 127, 1))
    return values


def fold(values, wall):
    lane = lane_of(values[0].shape)
    folded = []
    for a in (0, 9, 18):
        columns = [[values[a + c] + pltpu.roll(values[a + 6 + c], 1, 0), values[a + 3 + c]] for c in range(3)]
        for b in range(2):
            first = columns[0][b] + jnp.where(lane == 0, 0.0, pltpu.roll(columns[2][b], 1, 1))
            if wall:
                first = jnp.where(lane == 0, 0.0, first)
            folded += [first, columns[1][b], jnp.zeros_like(first) if wall else columns[2][b]]
    return folded


def unfold(folded):
    lane = lane_of(folded[0].shape)
    values = []
    for a in (0, 6, 12):
        planes = []
        for b in (0, 3):
            first, second, top = folded[a + b : a + b + 3]
            planes.append([first, second, jnp.where(lane == 127, top, pltpu.roll(first, 127, 1))])
        planes.append([pltpu.roll(value, 7, 0) for value in planes[0]])
        values += planes[0] + planes[1] + planes[2]
    return values


def is_even(axis="slab"):
    return lax.axis_index(axis) % 2 == 0


def put(near, far, slot, left, right, even):
    near[slot] = jnp.where(even, right, left).astype(BF16)
    far[slot] = jnp.where(even, left, right).astype(BF16)


def get(near, far, slot, even):
    one, other = near[slot].astype(F32), far[slot].astype(F32)
    return jnp.where(even, other, one), jnp.where(even, one, other)


def pressure_of(density, energy, material):
    gamma = jnp.where(material[...] == 0, 2.0 / 3.0, 0.4).astype(F32)
    gamma = jnp.concatenate([gamma, gamma], axis=0)
    return (gamma[None] * density[...] * energy[...]).astype(BF16).astype(F32)


def to_lane(tile, lane, values, slot):
    return jnp.where(lane == slot, pltpu.roll(values, slot + 1, 1), tile)


def third_along_z(values, tops, lane, slot):
    return jnp.where(lane == 127, pltpu.roll(tops, 127 - slot, 1), pltpu.roll(values, 127, 1))


def double(values):
    return jnp.concatenate([values, values], axis=0)


def force_of(geometry, r, pressure):
    value = jnp.sum(geometry[pl.ds(4 * r, 4)].astype(F32) * pressure, axis=0)
    return -(value + pltpu.roll(value, OWN, 0))


def force_kernel(
    geometry_in, density_in, energy_in, material_in, mass_weight_in,
    field, near, far, pressure_out, gravity_out,
    geometry, density, energy, material, mass_weight, sems,
):
    small = [
        pltpu.make_async_copy(source, target, sems.at[6 + i])
        for i, (source, target) in enumerate(
            [(density_in, density), (energy_in, energy), (material_in, material), (mass_weight_in, mass_weight)]
        )
    ]
    parts = [
        pltpu.make_async_copy(
            geometry_in.at[pl.ds(108 * comp + 36 * a, 36)], geometry.at[pl.ds(72 * comp + 18 * a, 36)], sems.at[2 * comp + a // 2]
        )
        for comp in range(3)
        for a in (0, 2)
    ]
    for copy in small + parts:
        copy.start()
    for copy in small:
        copy.wait()
    pressure = pressure_of(density, energy, material)
    gravity = from_points([double(mass_weight[q]) * (POINT_WEIGHT[q] * POINT_SCALE[q]) for q in range(27)])
    pressure_out[...] = pressure
    for n in range(9):
        gravity_out[n] = GRAVITY * gravity[9 + n]
    even = is_even()
    for comp in range(3):
        parts[2 * comp].wait()
        parts[2 * comp + 1].wait()
        values = []
        for n in range(18):
            value = force_of(geometry, 18 * comp + n, pressure)
            if comp == 2:
                value = value - GRAVITY * gravity[n if n < 9 else n + 9]
            field[18 * comp + n] = value
            values.append(value)
        for n in range(9):
            put(near, far, 9 * comp + n, values[n][:OWN], values[9 + n][:OWN], even)


def spread_velocity(velocity, out):
    rows = velocity[...].astype(BF16).reshape(48, velocity.shape[3])
    low = rows[:, :256]
    high = rows[:, 256:257].astype(F32)
    node = lax.broadcasted_iota(jnp.int32, (256, 384), 0)
    lane = lax.broadcasted_iota(jnp.int32, (256, 384), 1)
    pick = (node == 2 * (lane % 128) + lane // 128).astype(F32).astype(BF16)
    spread = jnp.dot(low, pick, preferred_element_type=F32)
    top = jnp.where(lane_of((48, 128)) == 127, high, 0.0)
    spread = jnp.concatenate([spread[:, :256], spread[:, 256:] + top], axis=1)
    row = lax.broadcasted_iota(jnp.int32, (96, 48), 0)
    source = lax.broadcasted_iota(jnp.int32, (96, 48), 1)
    wanted = (row // 16) * 8 + 2 * (row % 8) + (row // 8) % 2
    move = ((source == wanted) & (row % 8 < OWN)).astype(F32).astype(BF16)
    moved = jnp.dot(move, spread.astype(BF16), preferred_element_type=F32)
    for group in range(12):
        for c in range(3):
            out[3 * group + c] = moved[8 * group : 8 * group + 8, 128 * c : 128 * c + 128]


TOPS, WEIGHTS, SPEEDS, MESSAGE = 45, 46, 73, 79
SPEED_LANE = 32


def add_tops(values, comp, a, tops, sent):
    if comp == 2:
        return tops, sent
    row = lax.broadcasted_iota(jnp.int32, (8, 128), 0)
    lane = lane_of((8, 128))
    i = 3 * comp + a
    first, second, third = [values[3 * b + 2] for b in range(3)]
    for b, value in enumerate((first, second, third)):
        tops = to_lane(tops, lane, value, 3 * i + b)
    first = first + jnp.where(row % 2 == 1, pltpu.roll(third, 1, 0), 0.0)
    return tops, to_lane(sent, lane, first, 3 * i)


def fill_plane(values, comp, a, out, near, far, even_y):
    row = lax.broadcasted_iota(jnp.int32, (8, 128), 0)
    i = 3 * comp + a
    outer = []
    for c in range(2):
        first, second, third = [values[3 * b + c] for b in range(3)]
        for b, value in enumerate((first, second, third)):
            out[6 * i + 2 * b + c] = pltpu.roll(value, HALO, 0)
        first = first + jnp.where(row % 2 == 1, pltpu.roll(third, 1, 0), 0.0)
        for k, value in enumerate((first, second)):
            put(near, far, 4 * i + 2 * k + c, value[:HALO], value[HALO:OWN], even_y)
        outer.append(third)
    both = jnp.where(row % 2 == 1, outer[1], pltpu.roll(outer[0], 7, 0))
    put(near, far, 36 + i, both[:HALO], both[HALO:OWN], even_y)


def spread_kernel(
    geometry_in, velocity, pressure_in, gravity, mass_weight, spread, middle, near, far, geometry, sems
):
    parts = [
        pltpu.make_async_copy(
            geometry_in.at[pl.ds(108 * comp + 36, 36)], geometry.at[pl.ds(36 * comp, 36)], sems.at[comp]
        )
        for comp in range(3)
    ]
    for copy in parts:
        copy.start()
    even_y = is_even("brick")
    row = lax.broadcasted_iota(jnp.int32, (8, 128), 0)
    lane = lane_of((8, 128))
    spread_velocity(velocity, spread)
    tops = jnp.zeros((8, 128), F32)
    sent = tops
    for k in range(6):
        tops = to_lane(tops, lane, jnp.where(row == 0, spread[6 * k + 2], 0.0), SPEED_LANE + k)
    for q in range(27):
        put(near, far, WEIGHTS + q, mass_weight[q, :HALO], mass_weight[q, HALO:], even_y)
    for k in range(6):
        both = jnp.where(row == 0, spread[6 * k], pltpu.roll(spread[6 * k + 1], 1, 0))[:HALO].astype(BF16)
        near[SPEEDS + k] = both
        far[SPEEDS + k] = both
    pressure = pressure_in[...]
    for comp in range(3):
        parts[comp].wait()
        values = []
        for n in range(9):
            value = force_of(geometry, 9 * comp + n, pressure)
            values.append(value - gravity[n] if comp == 2 else value)
        tops, sent = add_tops(values, comp, 1, tops, sent)
        fill_plane(assemble_z(values, comp == 2), comp, 1, middle, near, far, even_y)
    middle[54] = tops
    middle[55] = sent


def rim_kernel(field, far, near, middle, near_in, far_in, out, near_out, far_out):
    even = is_even()
    even_y = is_even("brick")
    lane = lane_of((8, 128))
    tops, sent = middle[54], middle[55]
    for comp in range(3):
        i = 3 * comp + 1
        for k in range(6):
            out[6 * i + k] = middle[6 * i + k]
        for k in [4 * i, 4 * i + 1, 4 * i + 2, 4 * i + 3, 36 + i]:
            near_out[k] = near_in[k]
            far_out[k] = far_in[k]
        values = [field[18 * comp + n] for n in range(18)]
        for n in range(9):
            left, right = get(near, far, 9 * comp + n, even)
            values[n] = values[n] + double(left)
            values[9 + n] = values[9 + n] + double(right)
        for a, plane in ((0, values[:9]), (2, values[9:])):
            tops, sent = add_tops(plane, comp, a, tops, sent)
            fill_plane(assemble_z(plane, comp == 2), comp, a, out, near_out, far_out, even_y)
    out[54] = pltpu.roll(tops, HALO, 0)
    tops = jnp.where((lane % 3 == 0) & (lane < 27), sent, tops)
    put(near_out, far_out, TOPS, tops[:HALO], tops[HALO:OWN], even_y)
    for k in range(WEIGHTS, MESSAGE):
        near_out[k] = near_in[k]
        far_out[k] = far_in[k]


def send_planes(planes, near, far, even):
    lane = lane_of((8, 128))
    sides = [jnp.zeros((8, 128), F32)] * 2
    for comp in range(3):
        for b in range(2):
            left, right = [planes[comp][a + 3 * b : a + 3 * b + 3] for a in (0, 12)]
            for c in range(2):
                put(near, far, 4 * comp + 2 * b + c, left[c], right[c], even)
            sides = [to_lane(side, lane, plane[2], 2 * comp + b) for side, plane in zip(sides, (left, right))]
    put(near, far, 12, sides[0], sides[1], even)


def apply_mass(values, weight, wall):
    points = to_points(values)
    points = [points[q] * weight[q] for q in range(27)]
    return fold(from_points(points), wall)


def first_kernel(
    own, far_in, near_in, mass_weight, field, weight, image, near, far, rows
):
    even = is_even()
    even_y = is_even("brick")
    row = lax.broadcasted_iota(jnp.int32, (8, 128), 0)
    lane = lane_of((8, 128))
    mine = (row >= HALO) & (row < HALO + OWN)
    for k in range(SPEEDS):
        low, high = get(near_in, far_in, k, even_y)
        rows[k, :HALO] = low
        rows[k, HALO + OWN :] = high
        if k >= WEIGHTS:
            rows[k, HALO : HALO + OWN] = mass_weight[k - WEIGHTS]
    for q in range(27):
        weight[q] = rows[WEIGHTS + q] * (POINT_WEIGHT[q] * POINT_SCALE[q] ** 2)
    edge = (row == 1) | (row == 7)
    tops = jnp.where((lane % 3 == 2) & ~edge, 0.0, rows[TOPS])
    tops = jnp.where(mine, own[54], tops)
    tops = tops + jnp.where(lane % 3 == 0, pltpu.roll(pltpu.roll(tops, 126, 1), 1, 0), 0.0)
    planes = []
    for comp in range(3):
        values = []
        for a in range(3):
            i = 3 * comp + a
            columns = []
            for c in range(2):
                k = 2 * i + c
                halos = [rows[4 * i + c], rows[4 * i + 2 + c], rows[36 + k // 2]]
                halos[2] = jnp.where(edge, halos[2] if k % 2 == 1 else pltpu.roll(halos[2], 1, 0), 0.0)
                column = [jnp.where(mine, own[6 * i + 2 * b + c], halos[b]) for b in range(3)]
                columns.append([column[0] + pltpu.roll(column[2], 1, 0), column[1]])
            for b in range(2):
                values += [columns[0][b], columns[1][b], pltpu.roll(tops, 127 - 3 * i - b, 1)]
        for n in range(18):
            field[18 * comp + n] = values[n]
        values = apply_mass(unfold(values), weight, comp == 2)
        for n in range(18):
            image[18 * comp + n] = values[n]
        planes.append(values)
    send_planes(planes, near, far, even)


def speed_kernel(far_in, near_in, spread, speeds, plane_out):
    even_y = is_even("brick")
    row = lax.broadcasted_iota(jnp.int32, (8, 128), 0)
    lane = lane_of((8, 128))
    edge_tops = get(near_in, far_in, TOPS, even_y)[1]
    edge_tops = jnp.concatenate([edge_tops] * 4, axis=0)
    plane = []
    tops = jnp.zeros((8, 128), F32)
    for comp in range(3):
        for a in range(2):
            k = 2 * comp + a
            speed = [spread[6 * k + n] for n in range(6)]
            beyond = get(near_in, far_in, SPEEDS + k, even_y)[1]
            beyond = [beyond[c : c + 1] for c in range(2)]
            for c in range(2):
                speed.append(jnp.where(row == OWN - 1, beyond[c], pltpu.roll(speed[c], 7, 0)))
            third = third_along_z(jnp.broadcast_to(beyond[0], (8, 128)), edge_tops, lane, SPEED_LANE + k)[0:1]
            speed.append(jnp.where(row == OWN - 1, third, pltpu.roll(speed[2], 7, 0)))
            for n in range(9):
                speeds[18 * comp + 9 * a + n] = speed[n]
            if a == 0:
                for b in range(3):
                    plane += speed[3 * b : 3 * b + 2]
                    tops = to_lane(tops, lane, speed[3 * b + 2], SPEED_LANE + 3 * comp + b)
    tiles = [jnp.where(row < OWN, plane[2 * k], pltpu.roll(plane[2 * k + 1], OWN, 0)) for k in range(9)]
    for k, value in enumerate(tiles + [tops]):
        plane_out[k] = value.astype(BF16)


def send_own(planes, near, far, even):
    row = lax.broadcasted_iota(jnp.int32, (8, 128), 0)
    lane = lane_of((8, 128))
    sides = [jnp.zeros((8, 128), F32)] * 2
    after = [jnp.zeros((8, 128), F32)] * 2
    for comp in range(3):
        for b in range(2):
            both = []
            for side, a in enumerate((0, 12)):
                plane = planes[comp][a + 3 * b : a + 3 * b + 3]
                both.append(jnp.where(row < OWN, pltpu.roll(plane[0], 6, 0), pltpu.roll(plane[1], 2, 0)))
                sides[side] = to_lane(sides[side], lane, plane[2], 2 * comp + b)
                if b == 0:
                    for c in range(2):
                        k = 2 * comp + c
                        after[side] = jnp.where(row == k, pltpu.roll(plane[c], (k + 2) % 8, 0), after[side])
            put(near, far, 2 * comp + b, both[0], both[1], even)
    put(near, far, 6, after[0], after[1], even)
    put(near, far, 7, sides[0], sides[1], even)


def take_planes(image, near, far, comp, even):
    def read(b):
        tiles = [get(near, far, 4 * comp + 2 * b + c, even) for c in range(2)]
        return [[tile[side] for tile in tiles] for side in range(2)]

    return add_planes(image, read, get(near, far, 12, even), comp)


def take_own(image, near, far, comp, even):
    row = lax.broadcasted_iota(jnp.int32, (8, 128), 0)
    after = get(near, far, 6, even)

    def read(b):
        sides = []
        for side, both in enumerate(get(near, far, 2 * comp + b, even)):
            plane = [pltpu.roll(both, 2, 0), pltpu.roll(both, 6, 0)]
            if b == 0:
                for c in range(2):
                    k = 2 * comp + c
                    plane[c] = jnp.where(row == 6, pltpu.roll(after[side], 6 - k, 0), plane[c])
            sides.append(plane)
        return sides

    return add_planes(image, read, get(near, far, 7, even), comp)


def add_planes(image, read, tops, comp):
    values = [image[18 * comp + n] for n in range(18)]
    for b in range(2):
        for a, plane, top in zip((0, 12), read(b), tops):
            n = a + 3 * b
            for c in range(2):
                values[n + c] = values[n + c] + plane[c]
            values[n + 2] = values[n + 2] + pltpu.roll(top, 127 - 2 * comp - b, 1)
    return values


def second_kernel(image, far_in, near_in, weight, speeds, field, image_out, near, far):
    even = is_even()
    planes = []
    for comp in range(3):
        values = take_planes(image, near_in, far_in, comp, even)
        for n in range(18):
            field[18 * comp + n] = values[n]
        values = apply_mass(unfold(values), weight, comp == 2)
        for n in range(18):
            image_out[18 * comp + n] = values[n]
        planes.append(values)
    send_own(planes, near, far, even)


def work_kernel(geometry, pressure_in, energy, energy_mass, speeds, beyond, out):
    even = is_even()
    pressure = pressure_in[...]
    work = jnp.zeros_like(pressure)
    row = lax.broadcasted_iota(jnp.int32, (8, 128), 0)
    lane = lane_of((8, 128))
    tops = beyond[9].astype(F32)
    for comp in range(3):
        speed = [speeds[18 * comp + n] for n in range(18)]
        for b in range(3):
            both = beyond[3 * comp + b].astype(F32)
            speed += [both, pltpu.roll(both, OWN, 0)]
            speed.append(third_along_z(both, tops, lane, SPEED_LANE + 3 * comp + b))
        for n in range(27):
            value = jnp.where(row < OWN, speed[n], pltpu.roll(speed[n], OWN, 0))
            work = work + geometry[pl.ds(4 * (27 * comp + n), 4)].astype(F32) * value[None]
    out[...] = energy[...] + HALF_STEP * pressure * work / energy_mass[...]


def dot_owned(first, second, comp, total):
    last = lane_of((8, 128)) == 127
    for a in range(2):
        for b in range(2):
            n = 18 * comp + 6 * a + 3 * b
            total = total + first[n] * second[n] + first[n + 1] * second[n + 1]
            total = total + jnp.where(last, first[n + 2] * second[n + 2], 0.0)
    return total


def product_kernel(zeroth, first, beyond, products):
    for k, (one, other) in enumerate([(zeroth, zeroth), (zeroth, first), (first, first)]):
        total = jnp.zeros((8, 128), F32)
        for comp in range(3):
            total = dot_owned(one, other, comp, total)
        products[k] = total


def moment_kernel(image, far, near, weight, first, products, second, moments):
    zero = jnp.zeros((8, 128), F32)
    cross, norm = zero, zero
    quadratic = [zero] * 3
    even = is_even()
    for comp in range(3):
        values = take_own(image, near, far, comp, even)
        for n in range(18):
            second[18 * comp + n] = values[n]
        values_at = {18 * comp + n: values[n] for n in range(18)}
        cross = dot_owned(first, values_at, comp, cross)
        norm = dot_owned(values_at, values_at, comp, norm)
        points = to_points(unfold(values))
        for q in range(27):
            quadratic[q % 3] = quadratic[q % 3] + points[q] * points[q] * weight[q]
    quadratic = quadratic[0] + quadratic[1] + quadratic[2]
    row = lax.broadcasted_iota(jnp.int32, (8, 128), 0)
    mine = (row >= HALO) & (row < HALO + OWN)
    sums = jnp.zeros((8, 128), F32)
    for k, total in enumerate([products[0], products[1], products[2], cross, norm, quadratic]):
        total = jnp.sum(jnp.where(mine, total, 0.0), axis=0, keepdims=True)
        sums = jnp.where(row == k, total, sums)
    sums = jnp.sum(sums, axis=1, keepdims=True)
    line = jnp.sum(jnp.where(lane_of((8, 128)) == row, sums, 0.0), axis=0, keepdims=True)
    moments[...] = jnp.broadcast_to(line, moments.shape)


def solve(moments):
    def ratio(top, pivot, scale):
        good = pivot > 1e-7 * scale
        return jnp.where(good, top / jnp.where(good, pivot, 1.0), 0.0)

    m = moments
    l10 = ratio(m[2], m[1], 0.0)
    l20 = ratio(m[3], m[1], 0.0)
    d1 = m[3] - l10 * m[2]
    e1 = m[4] - l20 * m[2]
    l21 = ratio(e1, d1, m[3])
    d2 = m[5] - l20 * m[3] - l21 * e1
    y1 = m[1] - l10 * m[0]
    y2 = m[2] - l20 * m[0] - l21 * y1
    c2 = ratio(y2, d2, m[5])
    c1 = ratio(y1, d1, m[3]) - l21 * c2
    c0 = ratio(m[0], m[1], 0.0) - l10 * c1 - l20 * c2
    return c0, c1, c2


def halves(x):
    high = x.astype(BF16)
    return high, (x - high.astype(F32)).astype(BF16)


def nodal_kernel(zeroth, first, second, out):
    row = lax.broadcasted_iota(jnp.int32, (48, 96), 0)
    source = lax.broadcasted_iota(jnp.int32, (48, 96), 1)
    wanted = (row // 8) * 16 + (row % 2) * 8 + HALO + (row % 8) // 2
    move = (source == wanted).astype(F32).astype(BF16)
    source = lax.broadcasted_iota(jnp.int32, (384, 384), 0)
    node = lax.broadcasted_iota(jnp.int32, (384, 384), 1)
    wanted = jnp.where(node < 256, (node % 2) * 128 + node // 2, 383)
    place = ((source == wanted) & (node <= 256)).astype(F32).astype(BF16)
    for k, field in enumerate((zeroth, first, second)):
        blocks = []
        for c in range(3):
            column = []
            for comp in range(3):
                for a in range(2):
                    for b in range(2):
                        column.append(field[18 * comp + 6 * a + 3 * b + c])
            blocks.append(jnp.concatenate(column, axis=0))
        high, low = halves(jnp.concatenate(blocks, axis=1))
        moved = jnp.dot(move, high, preferred_element_type=F32) + jnp.dot(move, low, preferred_element_type=F32)
        high, low = halves(moved)
        out[k] = jnp.dot(high, place, preferred_element_type=F32) + jnp.dot(low, place, preferred_element_type=F32)


def last_kernel(moments, nodal, velocity, out):
    line = jnp.sum(moments[...], axis=0, keepdims=True)
    lane = lane_of((1, 128))
    mu = [jnp.sum(jnp.where(lane == k, line, 0.0), axis=1, keepdims=True) for k in range(6)]
    c0, c1, c2 = [HALF_STEP * c for c in solve(mu)]
    for comp in range(3):
        for x in range(2):
            start = 16 * comp + 8 * x
            part = [nodal[k, pl.ds(start, 8), : velocity.shape[3]] for k in range(3)]
            out[comp, x] = velocity[comp, x] + (c0 * part[0] + c1 * part[1] + c2 * part[2])


VMEM = pl.BlockSpec(memory_space=pltpu.VMEM)


HBM = pl.BlockSpec(memory_space=pltpu.HBM)


def call(kernel, outs, *args, scratch=(), flops=100000, in_hbm=0, dtypes=None):
    shapes = [jax.ShapeDtypeStruct(shape, dtype) for shape, dtype in zip(outs, dtypes or [F32] * len(outs))]
    moved = sum(a.size * a.dtype.itemsize for a in args) + sum(4 * int(np.prod(s)) for s in outs)
    return pl.pallas_call(
        kernel,
        out_shape=shapes,
        in_specs=[HBM] * in_hbm + [VMEM] * (len(args) - in_hbm),
        out_specs=[VMEM] * len(outs),
        scratch_shapes=list(scratch),
        compiler_params=pltpu.CompilerParams(vmem_limit_bytes=32 * 1024 * 1024),
        cost_estimate=pl.CostEstimate(flops=flops, bytes_accessed=moved, transcendentals=0),
        name=kernel.__name__,
    )(*args)


def swap(near, far, axis="slab"):
    count = lax.axis_size(axis)
    far = lax.ppermute(far, axis, [(i, (i + (1 if i % 2 else -1)) % count) for i in range(count)])
    near = lax.ppermute(near, axis, [(i, i + (-1 if i % 2 else 1)) for i in range(count)])
    return near, far


def local(velocity, energy, density, material, geometry, mass_weight, energy_mass):
    tile = (4, 128)
    full = (8, 128)
    geometry = geometry.reshape((324,) + full)
    density = density.reshape((4,) + full)
    energy = energy.reshape((4,) + full)
    energy_mass = energy_mass.reshape((4,) + full)
    mass_weight = mass_weight.reshape((27,) + tile)
    material = material.reshape(tile)
    pair = (2, 128)
    devices = lax.axis_size("slab") * lax.axis_size("brick")

    stays = [
        pltpu.with_memory_space_constraint(x, pltpu.HBM) for x in (geometry, density, energy, material, mass_weight)
    ]
    force, near, far, pressure, gravity = call(
        force_kernel,
        [(54,) + full, (27,) + tile, (27,) + tile, (4,) + full, (9,) + full],
        *stays,
        scratch=[
            pltpu.VMEM((216,) + full, BF16),
            pltpu.VMEM((4,) + full, F32),
            pltpu.VMEM((4,) + full, F32),
            pltpu.VMEM(tile, jnp.int32),
            pltpu.VMEM((27,) + tile, F32),
            pltpu.SemaphoreType.DMA((10,)),
        ],
        in_hbm=5,
        dtypes=[F32, BF16, BF16, F32, F32],
    )
    spread, middle, near_part, far_part = call(
        spread_kernel,
        [(36,) + full, (56,) + full, (MESSAGE,) + pair, (MESSAGE,) + pair],
        stays[0], velocity, pressure, gravity, mass_weight,
        scratch=[pltpu.VMEM((108,) + full, BF16), pltpu.SemaphoreType.DMA((3,))],
        in_hbm=1,
        dtypes=[F32, F32, BF16, BF16],
    )
    near, far = swap(near, far)
    own, near, far = call(
        rim_kernel,
        [(55,) + full, (MESSAGE,) + pair, (MESSAGE,) + pair],
        force, far, near, middle, near_part, far_part,
        dtypes=[F32, BF16, BF16],
    )
    near_rim, far_rim = swap(near, far, "brick")
    zeroth, weight, image, near, far = call(
        first_kernel,
        [(54,) + full, (27,) + full, (54,) + full, (13,) + full, (13,) + full],
        own, far_rim, near_rim, mass_weight,
        scratch=[pltpu.VMEM((SPEEDS,) + full, F32)],
        dtypes=[F32, F32, F32, BF16, BF16],
    )
    near, far = swap(near, far)
    speeds, plane = call(
        speed_kernel,
        [(54,) + full, (10,) + full],
        far_rim, near_rim, spread,
        dtypes=[F32, BF16],
    )
    count = lax.axis_size("slab")
    beyond = lax.ppermute(plane, "slab", [(i, (i - 1) % count) for i in range(count)])
    first, image, near, far = call(
        second_kernel,
        [(54,) + full, (54,) + full, (8,) + full, (8,) + full],
        image, far, near, weight, speeds,
        dtypes=[F32, F32, BF16, BF16],
    )
    near, far = swap(near, far)
    (energy_half,) = call(
        work_kernel, [(4,) + full], geometry, pressure, energy, energy_mass, speeds, beyond
    )
    (products,) = call(product_kernel, [(3,) + full], zeroth, first, beyond)
    second, moments = call(
        moment_kernel, [(54,) + full, (devices, 128)], image, far, near, weight, first, products
    )
    moments = lax.all_to_all(moments, ("slab", "brick"), 0, 0, tiled=True)
    (nodal,) = call(nodal_kernel, [(3, 48, 384)], zeroth, first, second)
    (velocity_half,) = call(last_kernel, [velocity.shape], moments, nodal, velocity)
    return (velocity_half, energy_half.reshape(8, 1, 4, 128))


def solution(mesh):
    nodes = P(None, "slab", "brick", None)
    return jax.shard_map(
        local,
        mesh=mesh,
        in_specs=(
            nodes,
            nodes,
            nodes,
            P("slab", "brick", None),
            P(None, None, "slab", "brick", None),
            nodes,
            nodes,
        ),
        out_specs=(nodes, nodes),
        check_vma=False,
    )
```
